512 devices in a mesh: section: 32 (over x, y_lo, core), dp: 16 (over z, y_hi).
Axes of the slice: x: 4, y: 8 (y_hi: 2, y_lo: 4; y = y_hi * 4 + y_lo), z: 8, core: 2. Of those that a mesh axis runs over, the one named last changes fastest.
Arguments:
- saved_inputs: bfloat16 [4, 32, 2048, 2560], P(None, 'section', 'dp'), may hold values from -24 to 24
- grad_in: bfloat16 [32, 2048, 2560], P('section', 'dp'), may hold values from -6 to 6
- adapter_down: bfloat16 [2, 32, 128, 2560], P(None, 'section', None, 'dp'), may hold values from -0.125 to 0.125
- adapter_up: bfloat16 [2, 32, 128, 2560], P(None, 'section', None, 'dp'), may hold values from -0.5 to 0.5
Outputs:
- grad_out: bfloat16 [32, 2048, 2560], P('section', 'dp')
- down_grad: float32 [2, 32, 128, 2560], P(None, 'section', None, 'dp')
- up_grad: float32 [2, 32, 128, 2560], P(None, 'section', None, 'dp')
The draws below stay inside these ranges and needn't reach their ends.
All inputs are finite; a program needn't handle non-finite values.
Results may differ from the reference program's by a relative error of at most 0.024.
Values may be sent and summed in bfloat16 or wider, within the bound.
No kernel may reach another device: no remote copies, remote signals or barrier semaphores. Data moves between devices by JAX's collectives and lax.ppermute only.
A program may use at most 64 MiB of HBM per device.

```python
import math
import jax
import jax.numpy as jnp
from jax import lax

D = 2560
RANK = 128
VIRT = 2
TICKS = 4
ROWS = 128
SECTIONS = 32
BATCH_ROWS = 2048
N_DP = 16


def draw_saved_inputs(key, part):
    key = jax.random.fold_in(key, 7)
    key_base, key_rows, key_cols = jax.random.split(key, 3)
    shape = (TICKS, SECTIONS, BATCH_ROWS, D)
    row_scale = jnp.exp(jax.random.uniform(key_rows, (TICKS, SECTIONS, BATCH_ROWS, 1), jnp.float32, math.log(0.3), math.log(3.0)))
    col_scale = jnp.exp(jax.random.uniform(key_cols, (1, 1, 1, D), jnp.float32, math.log(0.5), math.log(2.0)))
    base = jnp.clip(jax.random.normal(key_base, shape, jnp.float32), -4.0, 4.0)
    return (base * row_scale * col_scale).astype(jnp.bfloat16)


def block_scale(rng, extent, pieces, low, largest):
    level = 1.0
    for axis_at, blocks in pieces:
        heights = jax.random.uniform(jax.random.fold_in(jax.random.fold_in(rng, 6), axis_at), (blocks,), jnp.float32, low / len(pieces), largest / len(pieces))
        level = level * jnp.repeat(jnp.exp(heights), extent[axis_at] // blocks).reshape((-1,) + (1,) * (len(extent) - 1 - axis_at))
    return level


def bell_draw(rng, extent, scale, limit, pieces=(), dtype=jnp.bfloat16):
    drawn = jax.random.normal(rng, extent, jnp.float32) * scale
    if len(pieces) > 0:
        drawn = block_scale(rng, extent, pieces, -0.22, 0.18) * drawn
    return jnp.clip(drawn, min=-limit, max=limit).astype(dtype)


def setup_inputs(seed: int = 0) -> dict:
    streams_of = jax.random.split(jax.random.key(seed), 5)
    saved_inputs = draw_saved_inputs(jax.random.fold_in(streams_of[4], 71), 0)
    grad_in = bell_draw(streams_of[1], (SECTIONS, BATCH_ROWS, D), 1.0, 6.0, ((0, 32), (1, 16)))
    adapter_down = bell_draw(streams_of[2], (VIRT, SECTIONS, RANK, D), D ** -0.5, 0.125, ((1, 32), (3, 16)))
    adapter_up = bell_draw(streams_of[3], (VIRT, SECTIONS, RANK, D), RANK ** -0.5, 0.5, ((1, 32), (3, 16)))
    return {"saved_inputs": saved_inputs, "grad_in": grad_in, "adapter_down": adapter_down, "adapter_up": adapter_up}


EPS = 1e-06

def layer_back(inputs_now, incoming, down_matrix, up_matrix):
    inputs_f32 = inputs_now.astype(jnp.float32)
    inverse_rms = lax.rsqrt(lax.optimization_barrier(jnp.mean(inputs_f32 * inputs_f32, axis=-1, keepdims=True)) + EPS)
    normed = inputs_f32 * inverse_rms
    normed_half = normed.astype(jnp.bfloat16)
    latent = lax.dot_general(normed_half, down_matrix, (((1,), (1,)), ((), ())), preferred_element_type=jnp.float32)
    gate_sig = jax.nn.sigmoid(latent)
    activated = (latent * gate_sig).astype(jnp.bfloat16)
    grad_act = lax.dot_general(incoming, up_matrix, (((1,), (1,)), ((), ())), preferred_element_type=jnp.float32)
    grad_latent = (grad_act * gate_sig * (1.0 + latent * (1.0 - gate_sig))).astype(jnp.bfloat16)
    grad_normed = jnp.dot(grad_latent, down_matrix, preferred_element_type=jnp.float32)
    inner = lax.optimization_barrier(jnp.mean(grad_normed * normed, axis=-1, keepdims=True))
    outgoing = incoming.astype(jnp.float32) + inverse_rms * (grad_normed - normed * inner)
    return (outgoing.astype(jnp.bfloat16), grad_latent, activated, normed_half)

def reference(saved_inputs, grad_in, adapter_down, adapter_up):
    section_ids = jnp.arange(SECTIONS)
    current = grad_in
    history = []
    for tick in range(TICKS):
        history.append(current)
        levels = VIRT - 1 - (section_ids + tick) // SECTIONS
        downs = adapter_down[levels, section_ids]
        ups = adapter_up[levels, section_ids]

        def one_section(items):
            return layer_back(items[0], items[1], items[2], items[3])[0]
        sent = lax.map(one_section, (saved_inputs[tick], current, downs, ups))
        current = jnp.roll(sent, -1, axis=0)
    grads_seen = jnp.stack(history, axis=1)
    inputs_seen = jnp.swapaxes(saved_inputs, 0, 1)
    downs_all = jnp.swapaxes(adapter_down, 0, 1)
    ups_all = jnp.swapaxes(adapter_up, 0, 1)

    def section_terms(items):
        inputs_section, grads_section, down_section, up_section, section_id = items
        totals_down = jnp.zeros((VIRT, N_DP, RANK, D), jnp.float32)
        totals_up = jnp.zeros((VIRT, N_DP, RANK, D), jnp.float32)
        for tick in range(TICKS):
            level = (VIRT - 1 - (section_id + tick) // SECTIONS).astype(jnp.int32)
            down_matrix = lax.dynamic_index_in_dim(down_section, level, 0, keepdims=False)
            up_matrix = lax.dynamic_index_in_dim(up_section, level, 0, keepdims=False)
            incoming = grads_section[tick]
            unused, grad_latent, activated, normed_half = layer_back(inputs_section[tick], incoming, down_matrix, up_matrix)
            lat_blocks = grad_latent.astype(jnp.float32).reshape(N_DP, ROWS, RANK)
            act_blocks = activated.astype(jnp.float32).reshape(N_DP, ROWS, RANK)
            norm_blocks = normed_half.astype(jnp.float32).reshape(N_DP, ROWS, D)
            grad_blocks = incoming.astype(jnp.float32).reshape(N_DP, ROWS, D)
            term_down = jnp.einsum('bri,brd->bid', lat_blocks, norm_blocks)
            term_up = jnp.einsum('bri,brd->bid', act_blocks, grad_blocks)
            totals_down = totals_down.at[level].add(term_down)
            totals_up = totals_up.at[level].add(term_up)
        rounded_down = lax.optimization_barrier(totals_down.astype(jnp.bfloat16)).astype(jnp.float32)
        rounded_up = lax.optimization_barrier(totals_up.astype(jnp.bfloat16)).astype(jnp.float32)
        return (lax.optimization_barrier(jnp.sum(rounded_down, axis=1)), lax.optimization_barrier(jnp.sum(rounded_up, axis=1)))
    sum_down, sum_up = lax.map(section_terms, (inputs_seen, grads_seen, downs_all, ups_all, section_ids.astype(jnp.int32)))
    return (current, jnp.swapaxes(sum_down, 0, 1), jnp.swapaxes(sum_up, 0, 1))
```

```python
import jax
import jax.numpy as jnp
from jax import lax
from jax.sharding import PartitionSpec as P

EPS = 1e-06
F32 = jnp.float32
BF16 = jnp.bfloat16


def dp_pairs(n_z, step, flip):
    return [
        (2 * z + h, 2 * ((z + step) % n_z) + (h ^ flip)) for z in range(n_z) for h in range(2)
    ]


def shifted(value, n_z, step):
    return lax.ppermute(value, "dp", dp_pairs(n_z, step, 0))


def swapped(value, n_z):
    return lax.ppermute(value, "dp", dp_pairs(n_z, 0, 1))


def ring_gather(shard, n_z):
    index = lax.axis_index("dp")
    z, h = index // 2, index % 2
    other = swapped(shard, n_z)
    pair = jnp.stack([jnp.where(h == 0, shard, other), jnp.where(h == 0, other, shard)])
    full = jnp.zeros((n_z,) + pair.shape, pair.dtype)
    full = lax.dynamic_update_index_in_dim(full, pair, z, 0)
    right, left = pair, pair
    half = n_z // 2
    for step in range(1, half):
        right, left = shifted(right, n_z, 1), shifted(left, n_z, -1)
        full = lax.dynamic_update_index_in_dim(full, right, (z - step) % n_z, 0)
        full = lax.dynamic_update_index_in_dim(full, left, (z + step) % n_z, 0)
    right, left = shifted(right[:1], n_z, 1), shifted(left[1:], n_z, -1)
    last = jnp.concatenate([right, left], axis=0)
    return lax.dynamic_update_index_in_dim(full, last, (z + half) % n_z, 0)


def ring_reduce(parts, n_z):
    index = lax.axis_index("dp")
    z, h = index // 2, index % 2
    half = n_z // 2

    def at(offset):
        return lax.dynamic_index_in_dim(parts, (z + offset) % n_z, 0, keepdims=False)

    far = at(half)
    right, left = shifted(far[:1], n_z, 1), shifted(far[1:], n_z, -1)
    for step in range(half - 1, 0, -1):
        here, there = at(step), at(-step)
        if step == half - 1:
            here = jnp.concatenate([here[:1] + right, here[1:]], axis=0)
            there = jnp.concatenate([there[:1], there[1:] + left], axis=0)
        else:
            here, there = here + right, there + left
        right, left = shifted(here, n_z, 1), shifted(there, n_z, -1)
    total = at(0).astype(F32) + right.astype(F32) + left.astype(F32)
    mine = lax.dynamic_index_in_dim(total, h, 0, keepdims=False)
    other = lax.dynamic_index_in_dim(total, 1 - h, 0, keepdims=False)
    return mine + swapped(other.astype(BF16), n_z).astype(F32)


def on_device(saved_inputs, grad_in, adapter_down, adapter_up):
    n_sec = lax.axis_size("section")
    n_dp = lax.axis_size("dp")
    n_z = n_dp // 2
    position = lax.axis_index("section")
    ticks = saved_inputs.shape[0]
    rank, share = adapter_down.shape[2], adapter_down.shape[3]
    width = saved_inputs.shape[3]
    even = position % 2 == 0
    two_layers = position + ticks - 1 >= n_sec
    levels = [1 - (position + tick) // n_sec for tick in range(ticks)]

    x = saved_inputs[:, 0].astype(F32)
    inverse = lax.rsqrt(jnp.mean(x * x, axis=-1, keepdims=True) + EPS)
    normed = (x * inverse).astype(BF16)

    shard = jnp.concatenate(
        [jnp.swapaxes(adapter_down[:, 0], 1, 2), jnp.swapaxes(adapter_up[:, 0], 1, 2)], axis=2
    )

    def gather_two(shards):
        full = ring_gather(shards, n_z)
        full = jnp.moveaxis(full, 2, 0)
        return full.reshape(2, width, 2 * rank)

    def gather_one(shards):
        copies = jnp.broadcast_to(shards[1][None], (n_dp,) + shards.shape[1:])
        full = lax.all_to_all(copies, "dp", 0, 0, tiled=True).reshape(1, width, 2 * rank)
        return jnp.concatenate([full, full], axis=0)

    maps = lax.cond(two_layers, gather_two, gather_one, shard)

    latents, actives, slopes, downs, ups = [], [], [], [], []
    for tick in range(ticks):
        both = lax.dynamic_index_in_dim(maps, levels[tick], 0, keepdims=False)
        down, up = both[:, :rank], both[:, rank:]
        latent = jnp.dot(normed[tick], down, preferred_element_type=F32)
        gate = jax.nn.sigmoid(latent)
        downs.append(down)
        ups.append(up)
        latents.append(latent)
        actives.append((latent * gate).astype(BF16))
        slopes.append(gate * (1.0 + latent * (1.0 - gate)))

    def layer(tick, incoming):
        grad_act = jnp.dot(incoming, ups[tick], preferred_element_type=F32)
        grad_latent = (grad_act * slopes[tick]).astype(BF16)
        inner = jnp.sum(grad_latent.astype(F32) * latents[tick], axis=-1, keepdims=True) / width
        grad_normed = lax.dot_general(
            grad_latent, downs[tick], (((1,), (1,)), ((), ())), preferred_element_type=F32
        )
        inv = inverse[tick]
        sent = incoming.astype(F32) + inv * (grad_normed - x[tick] * (inv * inner))
        return sent.astype(BF16), grad_latent

    inside = [(s, s - 1) for s in range(1, n_sec, 2)]
    across = [(s, (s - 1) % n_sec) for s in range(0, n_sec, 2)]

    incoming = [grad_in[0]]
    sent, grad_latent = layer(0, grad_in[0])
    grad_latents = [grad_latent]
    over = lax.ppermute(sent, "section", across)
    core = lax.ppermute(sent, "section", inside)
    for tick in range(1, ticks):
        incoming.append(jnp.where(even, core, over))
        sent_even, latent_even = layer(tick, core)
        next_over = lax.ppermute(sent_even, "section", across)
        sent_odd, latent_odd = layer(tick, over)
        next_core = lax.ppermute(sent_odd, "section", inside)
        grad_latents.append(jnp.where(even, latent_even, latent_odd))
        over, core = next_over, next_core
    grad_out = jnp.where(even, core, over)

    normed_all = normed.reshape(-1, width)
    incoming_all = jnp.concatenate(incoming, axis=0)

    def partials(lats, acts):
        contract = (((0,), (0,)), ((), ()))
        down = lax.dot_general(normed_all, lats, contract, preferred_element_type=F32)
        up = lax.dot_general(incoming_all, acts, contract, preferred_element_type=F32)
        return jnp.concatenate([down.astype(BF16), up.astype(BF16)], axis=1)

    def reduce_one(stacks):
        parts = partials(*[s.reshape(-1, rank) for s in stacks])
        moved = lax.all_to_all(parts.reshape(n_dp, share, 2 * rank), "dp", 0, 0, tiled=True)
        total = jnp.sum(moved.astype(F32), axis=0)
        return jnp.stack([jnp.zeros_like(total), total])

    def reduce_two(stacks):
        level_stack = jnp.stack(levels)
        parts = []
        for level in range(2):
            keep = (level_stack == level)[:, None, None]
            parts.append(
                partials(*[jnp.where(keep, s, jnp.zeros((), BF16)).reshape(-1, rank) for s in stacks])
            )
        both = jnp.stack([p.reshape(n_z, 2, share, 2 * rank) for p in parts], axis=2)
        return ring_reduce(both, n_z)

    stacks = (jnp.stack(grad_latents), jnp.stack(actives))
    total = lax.cond(two_layers, reduce_two, reduce_one, stacks)
    total = jnp.swapaxes(total, 1, 2)
    return grad_out[None], total[:, None, :rank], total[:, None, rank:]


def solution(mesh):
    in_specs = (
        P(None, "section", "dp", None),
        P("section", "dp", None),
        P(None, "section", None, "dp"),
        P(None, "section", None, "dp"),
    )
    out_specs = (
        P("section", "dp", None),
        P(None, "section", None, "dp"),
        P(None, "section", None, "dp"),
    )
    return jax.shard_map(
        on_device, mesh=mesh, in_specs=in_specs, out_specs=out_specs, check_vma=False
    )
```

```python
import functools

import jax
import jax.numpy as jnp
from jax import lax
from jax.experimental import pallas as pl
from jax.experimental.pallas import tpu as pltpu
from jax.sharding import PartitionSpec as P

EPS = 1e-06
F32 = jnp.float32
BF16 = jnp.bfloat16
LIMIT = pltpu.CompilerParams(vmem_limit_bytes=24 * 1024 * 1024)
IN_VMEM = pl.BlockSpec(memory_space=pltpu.VMEM)
ANYWHERE = pl.BlockSpec(memory_space=pl.ANY)
SCALAR = pl.BlockSpec(memory_space=pltpu.SMEM)


def dp_pairs(n_z, step, flip):
    return [
        (2 * z + h, 2 * ((z + step) % n_z) + (h ^ flip)) for z in range(n_z) for h in range(2)
    ]


def shifted(value, n_z, step):
    return lax.ppermute(value, "dp", dp_pairs(n_z, step, 0))


def swapped(value, n_z):
    return lax.ppermute(value, "dp", dp_pairs(n_z, 0, 1))


def place_kernel(n_z, place_ref, *refs):
    half = n_z // 2
    pieces, outs = refs[: n_z + 1], refs[n_z + 1 :]
    z = place_ref[0]
    offsets = [0] + list(range(-1, -half, -1)) + list(range(1, half))
    for level, out in enumerate(outs):
        lanes = slice(level * out.shape[2], (level + 1) * out.shape[2])
        for piece, offset in zip(pieces, offsets):
            at = lax.rem(z + (offset + n_z), n_z) * 2
            out[pl.ds(at, 2)] = piece[:, :, lanes]
        far = lax.rem(z + half, n_z) * 2
        for h in range(2):
            out[pl.ds(far + h, 1)] = pieces[n_z - 1 + h][:, :, lanes]


def ring_gather(shard, n_z):
    index = lax.axis_index("dp")
    z, h = index // 2, index % 2
    other = swapped(shard, n_z)
    pair = jnp.stack([jnp.where(h == 0, shard, other), jnp.where(h == 0, other, shard)])
    half = n_z // 2
    rights, lefts = [], []
    right, left = pair, pair
    for _ in range(1, half):
        right, left = shifted(right, n_z, 1), shifted(left, n_z, -1)
        rights.append(right)
        lefts.append(left)
    pieces = [pair] + rights + lefts + [shifted(right[:1], n_z, 1), shifted(left[1:], n_z, -1)]
    share, lanes = shard.shape[0], shard.shape[1] // 2
    whole = jax.ShapeDtypeStruct((2 * n_z, share, lanes), shard.dtype)
    return pl.pallas_call(
        functools.partial(place_kernel, n_z),
        out_shape=[whole, whole],
        in_specs=[SCALAR] + [IN_VMEM] * len(pieces),
        out_specs=[IN_VMEM] * 2,
        compiler_params=LIMIT,
        name="place_maps",
    )(z.astype(jnp.int32)[None], *pieces)


def ring_reduce(parts, n_z):
    index = lax.axis_index("dp")
    z, h = index // 2, index % 2
    half = n_z // 2

    def at(offset):
        return lax.dynamic_index_in_dim(parts, (z + offset) % n_z, 0, keepdims=False)

    far = at(half)
    right, left = shifted(far[:1], n_z, 1), shifted(far[1:], n_z, -1)
    for step in range(half - 1, 0, -1):
        here, there = at(step), at(-step)
        if step == half - 1:
            here = jnp.concatenate([here[:1] + right, here[1:]], axis=0)
            there = jnp.concatenate([there[:1], there[1:] + left], axis=0)
        else:
            here, there = here + right, there + left
        here, there = lax.optimization_barrier((here, there))
        right, left = shifted(here, n_z, 1), shifted(there, n_z, -1)
    total = at(0).astype(F32) + right.astype(F32) + left.astype(F32)
    mine = lax.dynamic_index_in_dim(total, h, 0, keepdims=False)
    other = lax.dynamic_index_in_dim(total, 1 - h, 0, keepdims=False).astype(BF16)
    return mine, swapped(other, n_z)


def empty_kernel(out_ref):
    pass


def unset(shape, dtype):
    return pl.pallas_call(
        empty_kernel,
        out_shape=jax.ShapeDtypeStruct(shape, dtype),
        out_specs=ANYWHERE,
        name="unset",
    )()


def relay(incoming_ref, x_ref, map_ref, latent, slope, inverse, sent_ref, grad_latent_ref):
    width, rank = x_ref.shape[-1], latent.shape[1]
    grad_act = jnp.dot(incoming_ref[...], map_ref[:, rank:], preferred_element_type=F32)
    grad_latent = (grad_act * slope).astype(BF16)
    grad_latent_ref[...] = grad_latent
    inner = jnp.sum(grad_latent.astype(F32) * latent, axis=-1, keepdims=True) / width
    scale = inverse * inverse * inner
    run = width // 4
    for start in range(0, width, run):
        at = pl.ds(start, run)
        grad_normed = lax.dot_general(
            grad_latent, map_ref[at, :rank], (((1,), (1,)), ((), ())), preferred_element_type=F32
        )
        x = x_ref[0, 0, :, at].astype(F32)
        sent = incoming_ref[:, at].astype(F32) + (inverse * grad_normed - x * scale)
        sent_ref[:, at] = sent.astype(BF16)


def normalise(x_ref, normed_ref):
    x = x_ref[0, 0].astype(F32)
    inverse = lax.rsqrt(jnp.mean(x * x, axis=-1, keepdims=True) + EPS)
    normed_ref[...] = (x * inverse).astype(BF16)
    return inverse


def first_kernel(x_ref, incoming_ref, map_ref, sent_ref, grad_latent_ref, active_ref, normed_ref):
    rank = active_ref.shape[1]
    inverse = normalise(x_ref, normed_ref)
    latent = jnp.dot(normed_ref[...], map_ref[:, :rank], preferred_element_type=F32)
    gate = jax.nn.sigmoid(latent)
    active_ref[...] = (latent * gate).astype(BF16)
    slope = gate * (1.0 + latent * (1.0 - gate))
    relay(incoming_ref, x_ref, map_ref, latent, slope, inverse, sent_ref, grad_latent_ref)


def first_tick(saved_inputs, incoming, maps):
    ticks, _, rows, width = saved_inputs.shape
    rank = maps.shape[1] // 2
    wide = jax.ShapeDtypeStruct((rows, width), BF16)
    narrow = jax.ShapeDtypeStruct((rows, rank), BF16)
    return pl.pallas_call(
        first_kernel,
        grid=(1,),
        out_shape=[wide, narrow, narrow, wide],
        in_specs=[pl.BlockSpec((1, 1, rows, width), lambda i: (0, 0, 0, 0)), IN_VMEM, IN_VMEM],
        out_specs=[IN_VMEM] * 4,
        compiler_params=LIMIT,
        cost_estimate=pl.CostEstimate(flops=6 * rows * width * rank, bytes_accessed=4 * 2 * rows * width, transcendentals=0),
        name="first_tick",
    )(saved_inputs, incoming, maps)


def forward_kernel(level_ref, x_ref, first_ref, second_ref, dep_ref, normed_ref, active_ref, latent_ref, slope_ref, inverse_ref):
    rank = active_ref.shape[2]
    inverse = normalise(x_ref, normed_ref.at[0])
    inverse_ref[0] = jnp.broadcast_to(inverse, inverse_ref.shape[1:])
    level = level_ref[pl.program_id(0) + 1]
    for value, map_ref in ((1, first_ref), (0, second_ref)):

        @pl.when(level == value)
        def _():
            latent_ref[0] = jnp.dot(
                normed_ref[0], map_ref[:, :rank], preferred_element_type=F32
            )

    latent = latent_ref[0]
    gate = jax.nn.sigmoid(latent)
    active_ref[0] = (latent * gate).astype(BF16)
    slope_ref[0] = gate * (1.0 + latent * (1.0 - gate))


def forward_rest(levels, saved_inputs, first, second, dep):
    ticks, _, rows, width = saved_inputs.shape
    rank = first.shape[1] // 2
    rest = ticks - 1

    def made(lanes, dtype):
        return jax.ShapeDtypeStruct((rest, rows, lanes), dtype)

    def block(lanes):
        return pl.BlockSpec((1, rows, lanes), lambda i: (i, 0, 0))

    return pl.pallas_call(
        forward_kernel,
        grid=(rest,),
        out_shape=[made(width, BF16), made(rank, BF16), made(rank, F32), made(rank, F32), made(rank, F32)],
        in_specs=[
            SCALAR,
            pl.BlockSpec((1, 1, rows, width), lambda i: (i + 1, 0, 0, 0)),
            IN_VMEM,
            IN_VMEM,
            ANYWHERE,
        ],
        out_specs=[block(width)] + [block(rank)] * 4,
        compiler_params=LIMIT,
        cost_estimate=pl.CostEstimate(flops=rest * 2 * rows * width * rank, bytes_accessed=rest * 4 * rows * width, transcendentals=0),
        name="forward_rest",
    )(levels, saved_inputs, first, second, dep)


def tick_kernel(flags_ref, incoming_ref, x_ref, first_ref, second_ref, latent_ref, slope_ref, inverse_ref, dep_ref, sent_ref, grad_latent_ref):
    for value, map_ref in ((1, first_ref), (0, second_ref)):

        @pl.when((flags_ref[0] == 1) & (flags_ref[1] == value))
        def _():
            relay(
                incoming_ref,
                x_ref,
                map_ref,
                latent_ref[0],
                slope_ref[0],
                inverse_ref[0][:, :1],
                sent_ref,
                grad_latent_ref,
            )


def later_tick(tick, works, level, incoming, saved_inputs, first, second, latents, slopes, inverses, dep):
    _, _, rows, width = saved_inputs.shape
    rank = first.shape[1] // 2
    narrow = pl.BlockSpec((1, rows, rank), lambda i: (tick - 1, 0, 0))
    return pl.pallas_call(
        tick_kernel,
        grid=(1,),
        out_shape=[
            jax.ShapeDtypeStruct((rows, width), BF16),
            jax.ShapeDtypeStruct((rows, rank), BF16),
        ],
        in_specs=[
            SCALAR,
            IN_VMEM,
            pl.BlockSpec((1, 1, rows, width), lambda i: (tick, 0, 0, 0)),
            IN_VMEM,
            IN_VMEM,
            narrow,
            narrow,
            narrow,
            ANYWHERE,
        ],
        out_specs=[IN_VMEM] * 2,
        compiler_params=LIMIT,
        cost_estimate=pl.CostEstimate(flops=4 * rows * width * rank, bytes_accessed=3 * 2 * rows * width, transcendentals=0),
        name="later_tick",
    )(
        jnp.stack([works.astype(jnp.int32), level.astype(jnp.int32)]),
        incoming,
        saved_inputs,
        first,
        second,
        latents,
        slopes,
        inverses,
        dep,
    )


def turned(block):
    share, rank = block.shape
    room = -(-share // 128) * 128
    if room != share:
        block = jnp.concatenate([block, jnp.zeros((room - share, rank), block.dtype)], axis=0)
    return block.T[:, :share]


def finish_one_kernel(moved_ref, down_ref, up_ref):
    rank = down_ref.shape[1]
    total = jnp.sum(moved_ref[...].astype(F32), axis=0)
    down_ref[0] = jnp.zeros(down_ref.shape[1:], F32)
    up_ref[0] = jnp.zeros(up_ref.shape[1:], F32)
    down_ref[1] = turned(total[:, :rank])
    up_ref[1] = turned(total[:, rank:])


def finish_two_kernel(mine_ref, other_ref, down_ref, up_ref):
    rank = down_ref.shape[1]
    total = mine_ref[...] + other_ref[...].astype(F32)
    for i, out in enumerate((down_ref, up_ref)):
        for j, level in enumerate((1, 0)):
            at = (2 * i + j) * rank
            out[level] = turned(total[:, at : at + rank])


def finish(kernel, rank, share, *args):
    made = jax.ShapeDtypeStruct((2, rank, share), F32)
    return pl.pallas_call(
        kernel,
        out_shape=[made, made],
        in_specs=[IN_VMEM] * len(args),
        out_specs=[IN_VMEM] * 2,
        compiler_params=LIMIT,
        name="finish_sums",
    )(*args)


def on_device(saved_inputs, grad_in, adapter_down, adapter_up):
    n_sec = lax.axis_size("section")
    n_dp = lax.axis_size("dp")
    n_z = n_dp // 2
    position = lax.axis_index("section")
    ticks = saved_inputs.shape[0]
    rank, share = adapter_down.shape[2], adapter_down.shape[3]
    width = saved_inputs.shape[3]
    even = position % 2 == 0
    two_layers = position + ticks - 1 >= n_sec
    levels = [1 - (position + tick) // n_sec for tick in range(ticks)]

    def gather_two(down, up):
        shard = jnp.concatenate([down[1].T, up[1].T, down[0].T, up[0].T], axis=1)
        first, second = ring_gather(shard, n_z)
        return first.reshape(width, 2 * rank), second.reshape(width, 2 * rank)

    def gather_one(down, up):
        shard = jnp.concatenate([down[1].T, up[1].T], axis=1)
        copies = jnp.broadcast_to(shard[None], (n_dp,) + shard.shape)
        full = lax.all_to_all(copies, "dp", 0, 0, tiled=True)
        full = full.reshape(width, 2 * rank)
        return full, unset(full.shape, full.dtype)

    first, second = lax.cond(
        two_layers, gather_two, gather_one, adapter_down[:, 0], adapter_up[:, 0]
    )

    sent, grad_latent, active, normed = first_tick(saved_inputs, grad_in[0], first)
    level_stack = jnp.stack(levels).astype(jnp.int32)
    normeds, actives, latents, slopes, inverses = forward_rest(
        level_stack, saved_inputs, first, second, grad_latent
    )

    inside = [(s, s - 1) for s in range(1, n_sec, 2)]
    across = [(s, (s - 1) % n_sec) for s in range(0, n_sec, 2)]

    grads = [grad_in[0]]
    grad_latents = [grad_latent]
    over = lax.ppermute(sent, "section", across)
    core = lax.ppermute(sent, "section", inside)
    for tick in range(1, ticks):

        def layer(works, incoming, dep):
            return later_tick(
                tick,
                works,
                levels[tick],
                incoming,
                saved_inputs,
                first,
                second,
                latents,
                slopes,
                inverses,
                dep,
            )

        sent_even, latent_even = layer(even, core, normeds)
        next_over = lax.ppermute(sent_even, "section", across)
        sent_odd, latent_odd = layer(~even, over, latent_even)
        next_core = lax.ppermute(sent_odd, "section", inside)
        grads.append(jnp.where(even, core, over))
        grad_latents.append(jnp.where(even, latent_even, latent_odd))
        over, core = next_over, next_core

    normed_all = jnp.concatenate([normed[None], normeds], axis=0).reshape(-1, width)
    grads_all = jnp.concatenate(grads, axis=0)
    actives_all = jnp.concatenate([active[None], actives], axis=0)

    def products(lats, acts):
        contract = (((0,), (0,)), ((), ()))
        down = lax.dot_general(normed_all, lats, contract, preferred_element_type=F32)
        up = lax.dot_general(grads_all, acts, contract, preferred_element_type=F32)
        return jnp.concatenate([down.astype(BF16), up.astype(BF16)], axis=1)

    def reduce_one(lats, acts):
        parts = products(lats.reshape(-1, rank), acts.reshape(-1, rank))
        moved = lax.all_to_all(parts.reshape(n_dp, share, 2 * rank), "dp", 0, 0, tiled=True)
        return finish(finish_one_kernel, rank, share, moved)

    def reduce_two(lats, acts):
        level = level_stack[:, None, None]
        zero = jnp.zeros((), BF16)

        def split(value):
            both = [jnp.where(level == 1, value, zero), jnp.where(level == 0, value, zero)]
            return jnp.concatenate(both, axis=2).reshape(-1, 2 * rank)

        parts = products(split(lats), split(acts))
        mine, other = ring_reduce(parts.reshape(n_z, 2, share, 4 * rank), n_z)
        return finish(finish_two_kernel, rank, share, mine, other)

    down_grad, up_grad = lax.cond(
        two_layers, reduce_two, reduce_one, jnp.stack(grad_latents), actives_all
    )
    grad_out = jnp.where(even, core, over)
    return grad_out[None], down_grad[:, None], up_grad[:, None]


def solution(mesh):
    in_specs = (
        P(None, "section", "dp", None),
        P("section", "dp", None),
        P(None, "section", None, "dp"),
        P(None, "section", None, "dp"),
    )
    out_specs = (
        P("section", "dp", None),
        P(None, "section", None, "dp"),
        P(None, "section", None, "dp"),
    )
    return jax.shard_map(
        on_device, mesh=mesh, in_specs=in_specs, out_specs=out_specs, check_vma=False
    )
```

```python
import functools

import jax
import jax.numpy as jnp
from jax import lax
from jax.experimental import pallas as pl
from jax.experimental.pallas import tpu as pltpu
from jax.sharding import PartitionSpec as P

EPS = 1e-06
F32 = jnp.float32
BF16 = jnp.bfloat16
LIMIT = pltpu.CompilerParams(vmem_limit_bytes=24 * 1024 * 1024)
IN_VMEM = pl.BlockSpec(memory_space=pltpu.VMEM)
ANYWHERE = pl.BlockSpec(memory_space=pl.ANY)
SCALAR = pl.BlockSpec(memory_space=pltpu.SMEM)


def dp_pairs(sections, n_dp, step, flip):
    n_z = n_dp // 2
    return [
        (s * n_dp + 2 * z + h, s * n_dp + 2 * ((z + step) % n_z) + (h ^ flip))
        for s in sections
        for z in range(n_z)
        for h in range(2)
    ]


def shifted(value, ring, step):
    return lax.ppermute(value, ("section", "dp"), dp_pairs(*ring, step, 0))


def swapped(value, ring):
    return lax.ppermute(value, ("section", "dp"), dp_pairs(*ring, 0, 1))


def ring_gather(shard, ring):
    h = lax.axis_index("dp") % 2
    other = swapped(shard, ring)
    pair = jnp.stack([jnp.where(h == 0, shard, other), jnp.where(h == 0, other, shard)])
    rights, lefts = [], []
    right, left = pair, pair
    for _ in range(1, ring[1] // 4):
        right, left = shifted(right, ring, 1), shifted(left, ring, -1)
        rights.append(right)
        lefts.append(left)
    return [pair] + rights + lefts + [shifted(right[:1], ring, 1), shifted(left[1:], ring, -1)]


def ring_reduce(parts, ring):
    n_z = ring[1] // 2
    index = lax.axis_index("dp")
    z, h = index // 2, index % 2
    half = n_z // 2

    def at(offset):
        return lax.dynamic_index_in_dim(parts, (z + offset) % n_z, 0, keepdims=False)

    far = at(half)
    right, left = shifted(far[:1], ring, 1), shifted(far[1:], ring, -1)
    for step in range(half - 1, 0, -1):
        here, there = at(step), at(-step)
        if step == half - 1:
            here = jnp.concatenate([here[:1] + right, here[1:]], axis=0)
            there = jnp.concatenate([there[:1], there[1:] + left], axis=0)
        else:
            here, there = here + right, there + left
        here, there = lax.optimization_barrier((here, there))
        right, left = shifted(here, ring, 1), shifted(there, ring, -1)
    total = at(0).astype(F32) + right.astype(F32) + left.astype(F32)
    mine = lax.dynamic_index_in_dim(total, h, 0, keepdims=False)
    other = lax.dynamic_index_in_dim(total, 1 - h, 0, keepdims=False).astype(BF16)
    return mine, swapped(other, ring)


def norm_kernel(x_ref, normed_ref, inverse_ref):
    x = x_ref[0, 0].astype(F32)
    inverse = lax.rsqrt(jnp.mean(x * x, axis=-1, keepdims=True) + EPS)
    normed_ref[0] = (x * inverse).astype(BF16)
    inverse_ref[0] = jnp.broadcast_to(inverse, inverse_ref.shape[1:])


def norms(saved_inputs):
    ticks, _, rows, width = saved_inputs.shape
    return pl.pallas_call(
        norm_kernel,
        grid=(ticks,),
        out_shape=[
            jax.ShapeDtypeStruct((ticks, rows, width), BF16),
            jax.ShapeDtypeStruct((ticks, rows, 128), F32),
        ],
        in_specs=[pl.BlockSpec((1, 1, rows, width), lambda i: (i, 0, 0, 0))],
        out_specs=[
            pl.BlockSpec((1, rows, width), lambda i: (i, 0, 0)),
            pl.BlockSpec((1, rows, 128), lambda i: (i, 0, 0)),
        ],
        compiler_params=LIMIT,
        cost_estimate=pl.CostEstimate(
            flops=8 * ticks * rows * width, bytes_accessed=4 * ticks * rows * width, transcendentals=0
        ),
        name="norms",
    )(saved_inputs)


def tick_kernel(tick, n_pieces, flags_ref, *refs):
    incoming_ref, normed_ref, inverse_ref, first_ref = refs[:4]
    pieces = refs[4 : 4 + n_pieces]
    sent_ref, grad_latent_ref, active_ref = refs[5 + n_pieces : 8 + n_pieces]
    incoming, normed, inverse, down, up, sent, sems = refs[8 + n_pieces :]
    n_dp, share, rank = down.shape
    width = n_dp * share

    @pl.when(flags_ref[0] == 1)
    def _():
        gets = [
            pltpu.make_async_copy(normed_ref.at[tick], normed, sems.at[0]),
            pltpu.make_async_copy(first_ref.at[:, 0], down, sems.at[1]),
            pltpu.make_async_copy(first_ref.at[:, 1], up, sems.at[2]),
            pltpu.make_async_copy(incoming_ref, incoming, sems.at[3]),
            pltpu.make_async_copy(inverse_ref.at[tick], inverse, sems.at[4]),
        ]
        gets[0].start()
        gets[3].start()
        gets[4].start()

        def from_first():
            gets[1].start()
            gets[2].start()

        if n_pieces:
            n_z = n_dp // 2
            half = n_z // 2
            offsets = [0] + list(range(-1, -half, -1)) + list(range(1, half))
            z = flags_ref[2]
            pl.when(flags_ref[1] == 1)(from_first)

            @pl.when(flags_ref[1] == 0)
            def _():
                for which, target in enumerate((down, up)):
                    sem = sems.at[1 + which]
                    for piece, offset in zip(pieces, offsets):
                        at = lax.rem(z + (offset + n_z), n_z) * 2
                        pltpu.make_async_copy(
                            piece.at[:, which], target.at[pl.ds(at, 2)], sem
                        ).start()
                    far = lax.rem(z + half, n_z) * 2
                    for h in range(2):
                        pltpu.make_async_copy(
                            pieces[n_z - 1 + h].at[:, which], target.at[pl.ds(far + h, 1)], sem
                        ).start()
        else:
            from_first()

        gets[0].wait()
        gets[1].wait()
        down_map = down[...].reshape(width, rank)
        latent = jnp.dot(normed[...], down_map, preferred_element_type=F32)
        gate = jax.nn.sigmoid(latent)
        active_ref[...] = (latent * gate).astype(BF16)
        slope = gate * (1.0 + latent * (1.0 - gate))
        gets[2].wait()
        gets[3].wait()
        gets[4].wait()
        up_map = up[...].reshape(width, rank)
        grad_act = jnp.dot(incoming[...], up_map, preferred_element_type=F32)
        grad_latent = (grad_act * slope).astype(BF16)
        grad_latent_ref[...] = grad_latent
        inner = jnp.sum(grad_latent.astype(F32) * latent, axis=-1, keepdims=True) / width
        inv = inverse[:, :1]
        scale = inv * inner
        blocks = 4
        run = width // blocks
        for block in range(blocks):
            at = pl.ds(block * run, run)
            piece = down[pl.ds(block * n_dp // blocks, n_dp // blocks)].reshape(run, rank)
            grad_normed = lax.dot_general(
                grad_latent, piece, (((1,), (1,)), ((), ())), preferred_element_type=F32
            )
            new = incoming[:, at].astype(F32) + (
                inv * grad_normed - normed[:, at].astype(F32) * scale
            )
            sent[:, at] = new.astype(BF16)
        put = pltpu.make_async_copy(sent, sent_ref, sems.at[5])
        put.start()
        put.wait()


def tick_layer(tick, works, level, z, incoming, normed, inverse, first, pieces, dep):
    _, rows, width = normed.shape
    n_dp, _, share, rank = first.shape
    wide = jax.ShapeDtypeStruct((rows, width), BF16)
    narrow = jax.ShapeDtypeStruct((rows, rank), BF16)
    flags = jnp.stack([works.astype(jnp.int32), level.astype(jnp.int32), z.astype(jnp.int32)])
    return pl.pallas_call(
        functools.partial(tick_kernel, tick, len(pieces)),
        out_shape=[wide, narrow, narrow],
        in_specs=[SCALAR] + [ANYWHERE] * (5 + len(pieces)),
        out_specs=[ANYWHERE, IN_VMEM, IN_VMEM],
        scratch_shapes=[
            pltpu.VMEM((rows, width), BF16),
            pltpu.VMEM((rows, width), BF16),
            pltpu.VMEM((rows, 128), F32),
            pltpu.VMEM((n_dp, share, rank), BF16),
            pltpu.VMEM((n_dp, share, rank), BF16),
            pltpu.VMEM((rows, width), BF16),
            pltpu.SemaphoreType.DMA((6,)),
        ],
        compiler_params=LIMIT,
        cost_estimate=pl.CostEstimate(
            flops=40 * rows * width * rank, bytes_accessed=40 * rows * width, transcendentals=0
        ),
        name="tick_layer",
    )(flags, incoming, normed, inverse, first, *pieces, dep)


def turned(block):
    share, rank = block.shape
    room = -(-share // 128) * 128
    if room != share:
        block = jnp.concatenate([block, jnp.zeros((room - share, rank), block.dtype)], axis=0)
    return block.T[:, :share]


def finish_kernel(level_ref, moved_ref, mine_ref, other_ref, down_ref, up_ref):
    rank = down_ref.shape[1]
    level = level_ref[0]
    main = jnp.sum(moved_ref[...].astype(F32), axis=0)
    rest = mine_ref[...] + other_ref[...].astype(F32)
    for i, out in enumerate((down_ref, up_ref)):
        out[level] = turned(main[i])
        out[1 - level] = turned(rest[i])


def finish(level, moved, mine, other):
    _, share, rank = mine.shape
    made = jax.ShapeDtypeStruct((2, rank, share), F32)
    return pl.pallas_call(
        finish_kernel,
        out_shape=[made, made],
        in_specs=[SCALAR] + [IN_VMEM] * 3,
        out_specs=[IN_VMEM] * 2,
        compiler_params=LIMIT,
        name="finish_sums",
    )(level.astype(jnp.int32)[None], moved, mine, other)


def on_device(saved_inputs, grad_in, adapter_down, adapter_up):
    n_sec = lax.axis_size("section")
    n_dp = lax.axis_size("dp")
    n_z = n_dp // 2
    position = lax.axis_index("section")
    z = lax.axis_index("dp") // 2
    ticks = saved_inputs.shape[0]
    rank, share = adapter_down.shape[2], adapter_down.shape[3]
    width = saved_inputs.shape[3]
    even = position % 2 == 0
    levels = [1 - (position + tick) // n_sec for tick in range(ticks)]
    ring = (list(range(n_sec - ticks + 1, n_sec)), n_dp)

    def shard_of(level):
        return jnp.stack([adapter_down[level, 0].T, adapter_up[level, 0].T])

    shard = shard_of(1)
    copies = jnp.broadcast_to(shard[None], (n_dp,) + shard.shape)
    first = lax.all_to_all(copies, "dp", 0, 0, tiled=True)
    pieces = ring_gather(shard_of(0), ring)
    normed, inverse = norms(saved_inputs)

    def layer(tick, works, incoming, dep):
        met = any(s % 2 == (0 if works is even else 1) for s in range(n_sec - tick, n_sec))
        return tick_layer(
            tick,
            jnp.ones((), jnp.int32) if works is None else works,
            levels[tick],
            z,
            incoming,
            normed,
            inverse,
            first,
            pieces if met else [],
            dep,
        )

    inside = [(s, s - 1) for s in range(1, n_sec, 2)]
    across = [(s, (s - 1) % n_sec) for s in range(0, n_sec, 2)]
    odd = ~even

    sent, latent, active = layer(0, None, grad_in[0], inverse)
    grads, latents, actives = [grad_in[0]], [latent], [active]
    over = lax.ppermute(sent, "section", across)
    core = lax.ppermute(sent, "section", inside)
    for tick in range(1, ticks):
        sent_even, latent_even, active_even = layer(tick, even, core, latent)
        next_over = lax.ppermute(sent_even, "section", across)
        sent_odd, latent_odd, active_odd = layer(tick, odd, over, latent_even)
        next_core = lax.ppermute(sent_odd, "section", inside)
        grads.append(jnp.where(even, core, over))
        latents.append(jnp.where(even, latent_even, latent_odd))
        actives.append(jnp.where(even, active_even, active_odd))
        latent = latent_odd
        over, core = next_over, next_core
    grad_out = jnp.where(even, core, over)

    def product(wide, narrow):
        return lax.dot_general(wide, narrow, (((0,), (0,)), ((), ())), preferred_element_type=F32)

    last = ticks - 1
    zero = jnp.zeros((), BF16)

    def split(values):
        same = [jnp.where(levels[t] == levels[last], values[t], zero) for t in range(last)]
        differ = [jnp.where(levels[t] == levels[last], zero, values[t]) for t in range(last)]
        return jnp.concatenate([jnp.concatenate(same), jnp.concatenate(differ)], axis=1)

    early_down = product(normed[:last].reshape(-1, width), split(latents))
    early_up = product(jnp.concatenate(grads[:last]), split(actives))
    rest = jnp.stack([v[:, rank:].reshape(n_dp, share, rank) for v in (early_down, early_up)], axis=1)
    mine, other = ring_reduce(rest.astype(BF16).reshape(n_z, 2, 2, share, rank), ring)
    down = early_down[:, :rank] + product(normed[last], latents[last])
    up = early_up[:, :rank] + product(grads[last], actives[last])
    main = jnp.stack([v.astype(BF16).reshape(n_dp, share, rank) for v in (down, up)], axis=1)
    moved = lax.all_to_all(main, "dp", 0, 0, tiled=True)
    down_grad, up_grad = finish(levels[last], moved, mine, other)
    return grad_out[None], down_grad[:, None], up_grad[:, None]


def solution(mesh):
    in_specs = (
        P(None, "section", "dp", None),
        P("section", "dp", None),
        P(None, "section", None, "dp"),
        P(None, "section", None, "dp"),
    )
    out_specs = (
        P("section", "dp", None),
        P(None, "section", None, "dp"),
        P(None, "section", None, "dp"),
    )
    return jax.shard_map(
        on_device, mesh=mesh, in_specs=in_specs, out_specs=out_specs, check_vma=False
    )
```

```python
import functools

import jax
import jax.numpy as jnp
from jax import lax
from jax.experimental import pallas as pl
from jax.experimental.pallas import tpu as pltpu
from jax.sharding import PartitionSpec as P

EPS = 1e-06
F32 = jnp.float32
BF16 = jnp.bfloat16
LIMIT = pltpu.CompilerParams(vmem_limit_bytes=24 * 1024 * 1024)
IN_VMEM = pl.BlockSpec(memory_space=pltpu.VMEM)
ANYWHERE = pl.BlockSpec(memory_space=pl.ANY)
SCALAR = pl.BlockSpec(memory_space=pltpu.SMEM)


def dp_pairs(sections, n_dp):
    return [(s * n_dp + d, s * n_dp + (d ^ 1)) for s in sections for d in range(n_dp)]


def swapped(value, ring):
    return lax.ppermute(value, ("section", "dp"), dp_pairs(*ring))


def z_groups(n_dp):
    return [[2 * z + h for z in range(n_dp // 2)] for h in range(2)]


def paired(shard, ring):
    h = lax.axis_index("dp") % 2
    other = swapped(shard, ring)
    return jnp.stack([jnp.where(h == 0, shard, other), jnp.where(h == 0, other, shard)])


def reduced(parts, ring):
    h = lax.axis_index("dp") % 2
    total = lax.psum_scatter(
        parts, "dp", scatter_dimension=0, tiled=False, axis_index_groups=z_groups(ring[1])
    )
    mine = lax.dynamic_index_in_dim(total, h, 0, keepdims=False)
    other = lax.dynamic_index_in_dim(total, 1 - h, 0, keepdims=False)
    return mine, swapped(other, ring)


def norm_kernel(x_ref, normed_ref, inverse_ref):
    x = x_ref[0, 0].astype(F32)
    inverse = lax.rsqrt(jnp.mean(x * x, axis=-1, keepdims=True) + EPS)
    normed_ref[0] = (x * inverse).astype(BF16)
    inverse_ref[0] = jnp.broadcast_to(inverse, inverse_ref.shape[1:])


def norms(saved_inputs):
    ticks, _, rows, width = saved_inputs.shape
    return pl.pallas_call(
        norm_kernel,
        grid=(ticks,),
        out_shape=[
            jax.ShapeDtypeStruct((ticks, rows, width), BF16),
            jax.ShapeDtypeStruct((ticks, rows, 128), F32),
        ],
        in_specs=[pl.BlockSpec((1, 1, rows, width), lambda i: (i, 0, 0, 0))],
        out_specs=[
            pl.BlockSpec((1, rows, width), lambda i: (i, 0, 0)),
            pl.BlockSpec((1, rows, 128), lambda i: (i, 0, 0)),
        ],
        compiler_params=LIMIT,
        cost_estimate=pl.CostEstimate(
            flops=8 * ticks * rows * width, bytes_accessed=4 * ticks * rows * width, transcendentals=0
        ),
        name="norms",
    )(saved_inputs)


def tick_kernel(tick, flags_ref, *refs):
    incoming_ref, normed_ref, inverse_ref = refs[:3]
    level_refs = refs[3:-11]
    sent_ref, grad_latent_ref, active_ref = refs[-10:-7]
    incoming, normed, inverse, down, up, sent, sems = refs[-7:]
    n_dp, share, rank = down.shape
    width = n_dp * share

    @pl.when(flags_ref[0] == 1)
    def _():
        get_incoming = pltpu.make_async_copy(incoming_ref, incoming, sems.at[3])
        get_normed = pltpu.make_async_copy(normed_ref.at[tick], normed, sems.at[0])
        get_inverse = pltpu.make_async_copy(inverse_ref.at[tick], inverse, sems.at[4])
        get_incoming.start()
        for value, maps_ref in zip((1, 0), level_refs):

            @pl.when(flags_ref[1] == value)
            def _():
                pltpu.make_async_copy(maps_ref.at[:, 1], up, sems.at[2]).start()
                pltpu.make_async_copy(maps_ref.at[:, 0], down, sems.at[1]).start()

        get_normed.start()
        get_inverse.start()
        get_incoming.wait()
        pltpu.make_async_copy(level_refs[0].at[:, 1], up, sems.at[2]).wait()
        grad_act = jnp.dot(
            incoming[...], up[...].reshape(width, rank), preferred_element_type=F32
        )
        pltpu.make_async_copy(level_refs[0].at[:, 0], down, sems.at[1]).wait()
        get_normed.wait()
        get_inverse.wait()
        latent = jnp.dot(
            normed[...], down[...].reshape(width, rank), preferred_element_type=F32
        )
        gate = jax.nn.sigmoid(latent)
        active_ref[...] = (latent * gate).astype(BF16)
        slope = gate * (1.0 + latent * (1.0 - gate))
        grad_latent = (grad_act * slope).astype(BF16)
        grad_latent_ref[...] = grad_latent
        inner = jnp.sum(grad_latent.astype(F32) * latent, axis=-1, keepdims=True) / width
        inv = inverse[:, :1]
        scale = inv * inner
        blocks = 4
        run = width // blocks
        puts = []
        for block in range(blocks):
            at = pl.ds(block * run, run)
            piece = down[pl.ds(block * n_dp // blocks, n_dp // blocks)].reshape(run, rank)
            grad_normed = lax.dot_general(
                grad_latent, piece, (((1,), (1,)), ((), ())), preferred_element_type=F32
            )
            new = incoming[:, at].astype(F32) + (
                inv * grad_normed - normed[:, at].astype(F32) * scale
            )
            sent[:, at] = new.astype(BF16)
            puts.append(
                pltpu.make_async_copy(sent.at[:, at], sent_ref.at[:, at], sems.at[5 + block])
            )
            puts[-1].start()
        for put in puts:
            put.wait()


def tick_layer(tick, works, level, incoming, normed, inverse, maps, dep):
    _, rows, width = normed.shape
    n_dp, _, share, rank = maps[0].shape
    wide = jax.ShapeDtypeStruct((rows, width), BF16)
    narrow = jax.ShapeDtypeStruct((rows, rank), BF16)
    flags = jnp.stack([works.astype(jnp.int32), level.astype(jnp.int32)])
    return pl.pallas_call(
        functools.partial(tick_kernel, tick),
        out_shape=[wide, narrow, narrow],
        in_specs=[SCALAR] + [ANYWHERE] * (4 + len(maps)),
        out_specs=[ANYWHERE, IN_VMEM, IN_VMEM],
        scratch_shapes=[
            pltpu.VMEM((rows, width), BF16),
            pltpu.VMEM((rows, width), BF16),
            pltpu.VMEM((rows, 128), F32),
            pltpu.VMEM((n_dp, share, rank), BF16),
            pltpu.VMEM((n_dp, share, rank), BF16),
            pltpu.VMEM((rows, width), BF16),
            pltpu.SemaphoreType.DMA((9,)),
        ],
        compiler_params=LIMIT,
        cost_estimate=pl.CostEstimate(
            flops=40 * rows * width * rank, bytes_accessed=40 * rows * width, transcendentals=0
        ),
        name="tick_layer",
    )(flags, incoming, normed, inverse, *maps, dep)


def turned(block):
    share, rank = block.shape
    room = -(-share // 128) * 128
    if room != share:
        block = jnp.concatenate([block, jnp.zeros((room - share, rank), block.dtype)], axis=0)
    return block.T[:, :share]


def finish_kernel(level_ref, moved_ref, mine_ref, other_ref, down_ref, up_ref):
    rank = down_ref.shape[1]
    level = level_ref[0]
    main = jnp.sum(moved_ref[...].astype(F32), axis=0)
    rest = mine_ref[...].astype(F32) + other_ref[...].astype(F32)
    for i, out in enumerate((down_ref, up_ref)):
        lanes = slice(i * rank, (i + 1) * rank)
        out[level] = turned(main[:, lanes])
        out[1 - level] = turned(rest[:, lanes])


def finish(level, moved, mine, other):
    share, lanes = mine.shape
    rank = lanes // 2
    made = jax.ShapeDtypeStruct((2, rank, share), F32)
    return pl.pallas_call(
        finish_kernel,
        out_shape=[made, made],
        in_specs=[SCALAR] + [IN_VMEM] * 3,
        out_specs=[IN_VMEM] * 2,
        compiler_params=LIMIT,
        name="finish_sums",
    )(level.astype(jnp.int32)[None], moved, mine, other)


def on_device(saved_inputs, grad_in, adapter_down, adapter_up):
    n_sec = lax.axis_size("section")
    n_dp = lax.axis_size("dp")
    position = lax.axis_index("section")
    ticks = saved_inputs.shape[0]
    rank, share = adapter_down.shape[2], adapter_down.shape[3]
    width = saved_inputs.shape[3]
    even = position % 2 == 0
    levels = [1 - (position + tick) // n_sec for tick in range(ticks)]
    ring = (list(range(n_sec - ticks + 1, n_sec)), n_dp)

    def shard_of(level):
        return jnp.stack([adapter_down[level, 0].T, adapter_up[level, 0].T])

    pair = paired(shard_of(0), ring)
    shard = lax.optimization_barrier((shard_of(1), pair))[0]
    copies = jnp.broadcast_to(shard[None], (n_dp,) + shard.shape)
    first = lax.all_to_all(copies, "dp", 0, 0, tiled=True)
    second = lax.all_gather(pair, "dp", axis=0, axis_index_groups=z_groups(n_dp))
    second = second.reshape(first.shape)
    normed, inverse = norms(saved_inputs)

    def layer(tick, works, incoming, dep):
        met = any(s % 2 == (0 if works is even else 1) for s in range(n_sec - tick, n_sec))
        return tick_layer(
            tick,
            jnp.ones((), jnp.int32) if works is None else works,
            levels[tick],
            incoming,
            normed,
            inverse,
            [first, second] if met else [first],
            dep,
        )

    inside = [(s, s - 1) for s in range(1, n_sec, 2)]
    across = [(s, (s - 1) % n_sec) for s in range(0, n_sec, 2)]
    odd = ~even

    sent, latent, active = layer(0, None, grad_in[0], inverse)
    grads, latents, actives = [grad_in[0]], [latent], [active]
    over = lax.ppermute(sent, "section", across)
    core = lax.ppermute(sent, "section", inside)
    for tick in range(1, ticks):
        sent_even, latent_even, active_even = layer(tick, even, core, latent)
        next_over = lax.ppermute(sent_even, "section", across)
        sent_odd, latent_odd, active_odd = layer(tick, odd, over, latent_even)
        next_core = lax.ppermute(sent_odd, "section", inside)
        grads.append(jnp.where(even, core, over))
        latents.append(jnp.where(even, latent_even, latent_odd))
        actives.append(jnp.where(even, active_even, active_odd))
        latent = latent_odd
        over, core = next_over, next_core
    grad_out = jnp.where(even, core, over)

    def product(wide, narrow):
        return lax.dot_general(wide, narrow, (((0,), (0,)), ((), ())), preferred_element_type=F32)

    last = ticks - 1
    zero = jnp.zeros((), BF16)

    def kept(values, count, same):
        pick = [levels[t] == levels[last] for t in range(count)]
        return jnp.concatenate(
            [jnp.where(p if same else ~p, v, zero) for p, v in zip(pick, values)]
        )

    early = jnp.concatenate(grads[:last])
    early_normed = normed[:last].reshape(-1, width)
    rest = jnp.concatenate(
        [
            product(early_normed, kept(latents, last, False)).astype(BF16),
            product(early, kept(actives, last, False)).astype(BF16),
        ],
        axis=1,
    )
    mine, other = reduced(rest.reshape(n_dp // 2, 2, share, 2 * rank), ring)
    early_up = product(early, kept(actives, last, True))
    down = product(normed.reshape(-1, width), kept(latents, ticks, True))
    up = early_up + product(grads[last], actives[last])
    main = jnp.concatenate([down.astype(BF16), up.astype(BF16)], axis=1)
    moved = lax.all_to_all(main.reshape(n_dp, share, 2 * rank), "dp", 0, 0, tiled=True)
    down_grad, up_grad = finish(levels[last], moved, mine, other)
    return grad_out[None], down_grad[:, None], up_grad[:, None]


def solution(mesh):
    in_specs = (
        P(None, "section", "dp", None),
        P("section", "dp", None),
        P(None, "section", None, "dp"),
        P(None, "section", None, "dp"),
    )
    out_specs = (
        P("section", "dp", None),
        P(None, "section", None, "dp"),
        P(None, "section", None, "dp"),
    )
    return jax.shard_map(
        on_device, mesh=mesh, in_specs=in_specs, out_specs=out_specs, check_vma=False
    )
```

```python
import functools

import jax
import jax.numpy as jnp
from jax import lax
from jax.experimental import pallas as pl
from jax.experimental.pallas import tpu as pltpu
from jax.sharding import PartitionSpec as P

EPS = 1e-06
F32 = jnp.float32
BF16 = jnp.bfloat16
LIMIT = pltpu.CompilerParams(vmem_limit_bytes=24 * 1024 * 1024)
IN_VMEM = pl.BlockSpec(memory_space=pltpu.VMEM)
ANYWHERE = pl.BlockSpec(memory_space=pl.ANY)
SCALAR = pl.BlockSpec(memory_space=pltpu.SMEM)


def dp_pairs(sections, n_dp, step, flip):
    n_z = n_dp // 2
    return [
        (s * n_dp + 2 * z + h, s * n_dp + 2 * ((z + step) % n_z) + (h ^ flip))
        for s in sections
        for z in range(n_z)
        for h in range(2)
    ]


def shifted(value, ring, step):
    return lax.ppermute(value, ("section", "dp"), dp_pairs(*ring, step, 0))


def swapped(value, ring):
    return lax.ppermute(value, ("section", "dp"), dp_pairs(*ring, 0, 1))


def together(*lists):
    flat = iter(lax.optimization_barrier(tuple(v for values in lists for v in values)))
    return [[next(flat) for _ in values] for values in lists]


def gathered(shards, rings):
    h = lax.axis_index("dp") % 2
    pairs = []
    for shard, ring in zip(shards, rings):
        other = swapped(shard, ring)
        pairs.append(
            jnp.stack([jnp.where(h == 0, shard, other), jnp.where(h == 0, other, shard)])
        )
    steps = rings[0][1] // 4
    rights, lefts = [pairs], [pairs]
    for step in range(1, steps):
        right = [shifted(v, ring, 1) for v, ring in zip(rights[-1], rings)]
        left = [shifted(v, ring, -1) for v, ring in zip(lefts[-1], rings)]
        if step < steps - 1:
            right, left = together(right, left)
        rights.append(right)
        lefts.append(left)
    return [
        [pairs[i]]
        + [right[i] for right in rights[1:]]
        + [left[i] for left in lefts[1:]]
        + [shifted(rights[-1][i][:1], ring, 1), shifted(lefts[-1][i][1:], ring, -1)]
        for i, ring in enumerate(rings)
    ]


def reduced(parts, rings):
    n_z = rings[0][1] // 2
    index = lax.axis_index("dp")
    z, h = index // 2, index % 2
    half = n_z // 2

    def at(part, offset):
        return lax.dynamic_index_in_dim(part, (z + offset) % n_z, 0, keepdims=False)

    right = [shifted(at(part, half)[:1], ring, 1) for part, ring in zip(parts, rings)]
    left = [shifted(at(part, half)[1:], ring, -1) for part, ring in zip(parts, rings)]
    for step in range(half - 1, 0, -1):
        right, left = together(right, left)
        here = [at(part, step) for part in parts]
        there = [at(part, -step) for part in parts]
        if step == half - 1:
            here = [jnp.concatenate([v[:1] + r, v[1:]], axis=0) for v, r in zip(here, right)]
            there = [jnp.concatenate([v[:1], v[1:] + r], axis=0) for v, r in zip(there, left)]
        else:
            here = [v + r for v, r in zip(here, right)]
            there = [v + r for v, r in zip(there, left)]
        right = [shifted(v, ring, 1) for v, ring in zip(here, rings)]
        left = [shifted(v, ring, -1) for v, ring in zip(there, rings)]
    terms = []
    for part, ring, r, v in zip(parts, rings, right, left):
        total = at(part, 0).astype(F32) + r.astype(F32) + v.astype(F32)
        mine = lax.dynamic_index_in_dim(total, h, 0, keepdims=False)
        other = lax.dynamic_index_in_dim(total, 1 - h, 0, keepdims=False).astype(BF16)
        terms += [mine, swapped(other, ring)]
    return terms


def norm_kernel(x_ref, normed_ref, inverse_ref):
    x = x_ref[0, 0].astype(F32)
    inverse = lax.rsqrt(jnp.mean(x * x, axis=-1, keepdims=True) + EPS)
    normed_ref[0] = (x * inverse).astype(BF16)
    inverse_ref[0] = jnp.broadcast_to(inverse, inverse_ref.shape[1:])


def norms(saved_inputs):
    ticks, _, rows, width = saved_inputs.shape
    return pl.pallas_call(
        norm_kernel,
        grid=(ticks,),
        out_shape=[
            jax.ShapeDtypeStruct((ticks, rows, width), BF16),
            jax.ShapeDtypeStruct((ticks, rows, 128), F32),
        ],
        in_specs=[pl.BlockSpec((1, 1, rows, width), lambda i: (i, 0, 0, 0))],
        out_specs=[
            pl.BlockSpec((1, rows, width), lambda i: (i, 0, 0)),
            pl.BlockSpec((1, rows, 128), lambda i: (i, 0, 0)),
        ],
        compiler_params=LIMIT,
        cost_estimate=pl.CostEstimate(
            flops=8 * ticks * rows * width, bytes_accessed=4 * ticks * rows * width, transcendentals=0
        ),
        name="norms",
    )(saved_inputs)


def tick_kernel(tick, flags_ref, *refs):
    incoming_ref, normed_ref, inverse_ref = refs[:3]
    pieces = refs[3:-11]
    sent_ref, grad_latent_ref, active_ref = refs[-10:-7]
    incoming, normed, inverse, down, up, sent, sems = refs[-7:]
    n_dp, share, rank = down.shape
    width = n_dp * share
    n_z = n_dp // 2
    half = n_z // 2
    offsets = [0] + list(range(-1, -half, -1)) + list(range(1, half))

    def place(level_pieces, which, target, sem):
        z = flags_ref[2]
        for piece, offset in zip(level_pieces, offsets):
            at = lax.rem(z + (offset + n_z), n_z) * 2
            pltpu.make_async_copy(piece.at[:, which], target.at[pl.ds(at, 2)], sem).start()
        far = lax.rem(z + half, n_z) * 2
        for h in range(2):
            piece = level_pieces[n_z - 1 + h]
            pltpu.make_async_copy(piece.at[:, which], target.at[pl.ds(far + h, 1)], sem).start()

    def placed(target, sem):
        pltpu.make_async_copy(target, target, sem).wait()

    @pl.when(flags_ref[0] == 1)
    def _():
        get_incoming = pltpu.make_async_copy(incoming_ref, incoming, sems.at[3])
        get_normed = pltpu.make_async_copy(normed_ref.at[tick], normed, sems.at[0])
        get_inverse = pltpu.make_async_copy(inverse_ref.at[tick], inverse, sems.at[4])
        get_incoming.start()
        for value, start in ((1, 0), (0, n_z + 1)):
            if start < len(pieces):

                @pl.when(flags_ref[1] == value)
                def _():
                    place(pieces[start : start + n_z + 1], 1, up, sems.at[2])
                    place(pieces[start : start + n_z + 1], 0, down, sems.at[1])

        get_normed.start()
        get_inverse.start()
        get_incoming.wait()
        placed(up, sems.at[2])
        grad_act = jnp.dot(
            incoming[...], up[...].reshape(width, rank), preferred_element_type=F32
        )
        placed(down, sems.at[1])
        get_normed.wait()
        get_inverse.wait()
        latent = jnp.dot(
            normed[...], down[...].reshape(width, rank), preferred_element_type=F32
        )
        gate = jax.nn.sigmoid(latent)
        active_ref[...] = (latent * gate).astype(BF16)
        slope = gate * (1.0 + latent * (1.0 - gate))
        grad_latent = (grad_act * slope).astype(BF16)
        grad_latent_ref[...] = grad_latent
        inner = jnp.sum(grad_latent.astype(F32) * latent, axis=-1, keepdims=True) / width
        inv = inverse[:, :1]
        scale = inv * inner
        blocks = 4
        run = width // blocks
        puts = []
        for block in range(blocks):
            at = pl.ds(block * run, run)
            piece = down[pl.ds(block * n_dp // blocks, n_dp // blocks)].reshape(run, rank)
            grad_normed = lax.dot_general(
                grad_latent, piece, (((1,), (1,)), ((), ())), preferred_element_type=F32
            )
            new = incoming[:, at].astype(F32) + (
                inv * grad_normed - normed[:, at].astype(F32) * scale
            )
            sent[:, at] = new.astype(BF16)
            puts.append(
                pltpu.make_async_copy(sent.at[:, at], sent_ref.at[:, at], sems.at[5 + block])
            )
            puts[-1].start()
        for put in puts:
            put.wait()


def tick_layer(tick, works, level, z, incoming, normed, inverse, pieces, dep):
    _, rows, width = normed.shape
    _, _, share, rank = pieces[0].shape
    n_dp = width // share
    wide = jax.ShapeDtypeStruct((rows, width), BF16)
    narrow = jax.ShapeDtypeStruct((rows, rank), BF16)
    flags = jnp.stack([works.astype(jnp.int32), level.astype(jnp.int32), z.astype(jnp.int32)])
    return pl.pallas_call(
        functools.partial(tick_kernel, tick),
        out_shape=[wide, narrow, narrow],
        in_specs=[SCALAR] + [ANYWHERE] * (4 + len(pieces)),
        out_specs=[ANYWHERE, IN_VMEM, IN_VMEM],
        scratch_shapes=[
            pltpu.VMEM((rows, width), BF16),
            pltpu.VMEM((rows, width), BF16),
            pltpu.VMEM((rows, 128), F32),
            pltpu.VMEM((n_dp, share, rank), BF16),
            pltpu.VMEM((n_dp, share, rank), BF16),
            pltpu.VMEM((rows, width), BF16),
            pltpu.SemaphoreType.DMA((9,)),
        ],
        compiler_params=LIMIT,
        cost_estimate=pl.CostEstimate(
            flops=40 * rows * width * rank, bytes_accessed=40 * rows * width, transcendentals=0
        ),
        name="tick_layer",
    )(flags, incoming, normed, inverse, *pieces, dep)


def turned(block):
    share, rank = block.shape
    room = -(-share // 128) * 128
    if room != share:
        block = jnp.concatenate([block, jnp.zeros((room - share, rank), block.dtype)], axis=0)
    return block.T[:, :share]


def finish_kernel(level_ref, mine_ref, other_ref, rest_mine_ref, rest_other_ref, down_ref, up_ref):
    rank = down_ref.shape[1]
    level = level_ref[0]
    main = mine_ref[...] + other_ref[...].astype(F32)
    rest = rest_mine_ref[...] + rest_other_ref[...].astype(F32)
    for i, out in enumerate((down_ref, up_ref)):
        lanes = slice(i * rank, (i + 1) * rank)
        out[level] = turned(main[:, lanes])
        out[1 - level] = turned(rest[:, lanes])


def finish(level, terms):
    share, lanes = terms[0].shape
    rank = lanes // 2
    made = jax.ShapeDtypeStruct((2, rank, share), F32)
    return pl.pallas_call(
        finish_kernel,
        out_shape=[made, made],
        in_specs=[SCALAR] + [IN_VMEM] * 4,
        out_specs=[IN_VMEM] * 2,
        compiler_params=LIMIT,
        name="finish_sums",
    )(level.astype(jnp.int32)[None], *terms)


def on_device(saved_inputs, grad_in, adapter_down, adapter_up):
    n_sec = lax.axis_size("section")
    n_dp = lax.axis_size("dp")
    position = lax.axis_index("section")
    z = lax.axis_index("dp") // 2
    ticks = saved_inputs.shape[0]
    rank, share = adapter_down.shape[2], adapter_down.shape[3]
    width = saved_inputs.shape[3]
    even = position % 2 == 0
    levels = [1 - (position + tick) // n_sec for tick in range(ticks)]
    ring = (list(range(n_sec - ticks + 1, n_sec)), n_dp)

    def shard_of(level):
        return jnp.stack([adapter_down[level, 0].T, adapter_up[level, 0].T])

    rings = [(list(range(n_sec)), n_dp), ring]
    first, second = gathered([shard_of(1), shard_of(0)], rings)
    normed, inverse = norms(saved_inputs)

    def layer(tick, works, incoming, dep):
        met = any(s % 2 == (0 if works is even else 1) for s in range(n_sec - tick, n_sec))
        return tick_layer(
            tick,
            jnp.ones((), jnp.int32) if works is None else works,
            levels[tick],
            z,
            incoming,
            normed,
            inverse,
            first + second if met else first,
            dep,
        )

    inside = [(s, s - 1) for s in range(1, n_sec, 2)]
    across = [(s, (s - 1) % n_sec) for s in range(0, n_sec, 2)]
    odd = ~even

    sent, latent, active = layer(0, None, grad_in[0], inverse)
    grads, latents, actives = [grad_in[0]], [latent], [active]
    over = lax.ppermute(sent, "section", across)
    core = lax.ppermute(sent, "section", inside)
    for tick in range(1, ticks):
        sent_even, latent_even, active_even = layer(tick, even, core, latent)
        next_over = lax.ppermute(sent_even, "section", across)
        sent_odd, latent_odd, active_odd = layer(tick, odd, over, latent_even)
        next_core = lax.ppermute(sent_odd, "section", inside)
        grads.append(jnp.where(even, core, over))
        latents.append(jnp.where(even, latent_even, latent_odd))
        actives.append(jnp.where(even, active_even, active_odd))
        latent = latent_odd
        over, core = next_over, next_core
    grad_out = jnp.where(even, core, over)

    def product(wide, narrow):
        return lax.dot_general(wide, narrow, (((0,), (0,)), ((), ())), preferred_element_type=F32)

    last = ticks - 1
    zero = jnp.zeros((), BF16)

    def kept(values, count, same):
        pick = [levels[t] == levels[last] for t in range(count)]
        return jnp.concatenate(
            [jnp.where(p if same else ~p, v, zero) for p, v in zip(pick, values)]
        )

    early = lax.optimization_barrier((jnp.concatenate(grads[:last]), latent_even))[0]
    early_normed = lax.optimization_barrier((normed[:last].reshape(-1, width), latent_even))[0]
    rest = jnp.concatenate(
        [
            product(early_normed, kept(latents, last, False)).astype(BF16),
            product(early, kept(actives, last, False)).astype(BF16),
        ],
        axis=1,
    )
    early_up = product(early, kept(actives, last, True))
    down = product(normed.reshape(-1, width), kept(latents, ticks, True))
    up = early_up + product(grads[last], actives[last])
    main = jnp.concatenate([down.astype(BF16), up.astype(BF16)], axis=1)
    parts = [v.reshape(n_dp // 2, 2, share, 2 * rank) for v in (main, rest)]
    down_grad, up_grad = finish(levels[last], reduced(parts, rings))
    return grad_out[None], down_grad[:, None], up_grad[:, None]


def solution(mesh):
    in_specs = (
        P(None, "section", "dp", None),
        P("section", "dp", None),
        P(None, "section", None, "dp"),
        P(None, "section", None, "dp"),
    )
    out_specs = (
        P("section", "dp", None),
        P(None, "section", None, "dp"),
        P(None, "section", None, "dp"),
    )
    return jax.shard_map(
        on_device, mesh=mesh, in_specs=in_specs, out_specs=out_specs, check_vma=False
    )
```

```python
import functools

import jax
import jax.numpy as jnp
from jax import lax
from jax.experimental import pallas as pl
from jax.experimental.pallas import tpu as pltpu
from jax.sharding import PartitionSpec as P

EPS = 1e-06
F32 = jnp.float32
BF16 = jnp.bfloat16
LIMIT = pltpu.CompilerParams(vmem_limit_bytes=24 * 1024 * 1024)
IN_VMEM = pl.BlockSpec(memory_space=pltpu.VMEM)
ANYWHERE = pl.BlockSpec(memory_space=pl.ANY)
SCALAR = pl.BlockSpec(memory_space=pltpu.SMEM)


def dp_pairs(n_z, step, flip):
    return [
        (2 * z + h, 2 * ((z + step) % n_z) + (h ^ flip)) for z in range(n_z) for h in range(2)
    ]


def shifted(value, n_z, step):
    return lax.ppermute(value, "dp", dp_pairs(n_z, step, 0))


def swapped(value, n_z):
    return lax.ppermute(value, "dp", dp_pairs(n_z, 0, 1))


def place_kernel(n_z, place_ref, *refs):
    half = n_z // 2
    pieces, outs, sem = refs[: n_z + 1], refs[n_z + 1 : n_z + 3], refs[n_z + 3]
    z = place_ref[0]
    offsets = [0] + list(range(-1, -half, -1)) + list(range(1, half))
    copies = []
    for level, out in enumerate(outs):
        for piece, offset in zip(pieces, offsets):
            at = lax.rem(z + (offset + n_z), n_z) * 2
            copies.append((piece.at[:, level], out.at[pl.ds(at, 2)]))
        far = lax.rem(z + half, n_z) * 2
        for h in range(2):
            copies.append((pieces[n_z - 1 + h].at[:, level], out.at[pl.ds(far + h, 1)]))
    started = [
        pltpu.make_async_copy(source, target, sem.at[i])
        for i, (source, target) in enumerate(copies)
    ]
    for copy in started:
        copy.start()
    for copy in started:
        copy.wait()


def ring_gather(shard, n_z):
    index = lax.axis_index("dp")
    z, h = index // 2, index % 2
    other = swapped(shard, n_z)
    pair = jnp.stack([jnp.where(h == 0, shard, other), jnp.where(h == 0, other, shard)])
    half = n_z // 2
    rights, lefts = [], []
    right, left = pair, pair
    for _ in range(1, half):
        right, left = shifted(right, n_z, 1), shifted(left, n_z, -1)
        rights.append(right)
        lefts.append(left)
    pieces = [pair] + rights + lefts + [shifted(right[:1], n_z, 1), shifted(left[1:], n_z, -1)]
    _, share, lanes = shard.shape
    whole = jax.ShapeDtypeStruct((2 * n_z, share, lanes), shard.dtype)
    return pl.pallas_call(
        functools.partial(place_kernel, n_z),
        out_shape=[whole, whole],
        in_specs=[SCALAR] + [ANYWHERE] * len(pieces),
        out_specs=[ANYWHERE] * 2,
        scratch_shapes=[pltpu.SemaphoreType.DMA((2 * (n_z + 1),))],
        name="place_maps",
    )(z.astype(jnp.int32)[None], *pieces)


def empty_kernel(out_ref):
    pass


def unset(shape, dtype):
    return pl.pallas_call(
        empty_kernel,
        out_shape=jax.ShapeDtypeStruct(shape, dtype),
        out_specs=ANYWHERE,
        name="unset",
    )()


def relay(incoming_ref, x_ref, map_ref, latent, slope, inverse, sent_ref, grad_latent_ref):
    width, rank = x_ref.shape[-1], latent.shape[1]
    grad_act = jnp.dot(incoming_ref[...], map_ref[:, rank:], preferred_element_type=F32)
    grad_latent = (grad_act * slope).astype(BF16)
    grad_latent_ref[...] = grad_latent
    inner = jnp.sum(grad_latent.astype(F32) * latent, axis=-1, keepdims=True) / width
    scale = inverse * inverse * inner
    run = width // 4
    for start in range(0, width, run):
        at = pl.ds(start, run)
        grad_normed = lax.dot_general(
            grad_latent, map_ref[at, :rank], (((1,), (1,)), ((), ())), preferred_element_type=F32
        )
        x = x_ref[0, 0, :, at].astype(F32)
        sent = incoming_ref[:, at].astype(F32) + (inverse * grad_normed - x * scale)
        sent_ref[:, at] = sent.astype(BF16)


def normalise(x_ref, normed_ref):
    x = x_ref[0, 0].astype(F32)
    inverse = lax.rsqrt(jnp.mean(x * x, axis=-1, keepdims=True) + EPS)
    normed_ref[...] = (x * inverse).astype(BF16)
    return inverse


def first_kernel(x_ref, incoming_ref, map_ref, sent_ref, grad_latent_ref, active_ref, normed_ref):
    rank = active_ref.shape[1]
    inverse = normalise(x_ref, normed_ref)
    latent = jnp.dot(normed_ref[...], map_ref[:, :rank], preferred_element_type=F32)
    gate = jax.nn.sigmoid(latent)
    active_ref[...] = (latent * gate).astype(BF16)
    slope = gate * (1.0 + latent * (1.0 - gate))
    relay(incoming_ref, x_ref, map_ref, latent, slope, inverse, sent_ref, grad_latent_ref)


def first_tick(saved_inputs, incoming, maps):
    ticks, _, rows, width = saved_inputs.shape
    rank = maps.shape[1] // 2
    wide = jax.ShapeDtypeStruct((rows, width), BF16)
    narrow = jax.ShapeDtypeStruct((rows, rank), BF16)
    return pl.pallas_call(
        first_kernel,
        grid=(1,),
        out_shape=[wide, narrow, narrow],
        in_specs=[pl.BlockSpec((1, 1, rows, width), lambda i: (0, 0, 0, 0)), IN_VMEM, IN_VMEM],
        out_specs=[IN_VMEM] * 3,
        scratch_shapes=[pltpu.VMEM((rows, width), BF16)],
        compiler_params=LIMIT,
        cost_estimate=pl.CostEstimate(flops=6 * rows * width * rank, bytes_accessed=4 * 2 * rows * width, transcendentals=0),
        name="first_tick",
    )(saved_inputs, incoming, maps)


def forward_kernel(level_ref, x_ref, first_ref, second_ref, dep_ref, normed_ref, active_ref, latent_ref, slope_ref, inverse_ref):
    rank = active_ref.shape[2]
    inverse = normalise(x_ref, normed_ref.at[0])
    inverse_ref[0] = jnp.broadcast_to(inverse, inverse_ref.shape[1:])
    level = level_ref[pl.program_id(0)]
    for value, map_ref in ((1, first_ref), (0, second_ref)):

        @pl.when(level == value)
        def _():
            latent_ref[0] = jnp.dot(
                normed_ref[0], map_ref[:, :rank], preferred_element_type=F32
            )

    latent = latent_ref[0]
    gate = jax.nn.sigmoid(latent)
    active_ref[0] = (latent * gate).astype(BF16)
    slope_ref[0] = gate * (1.0 + latent * (1.0 - gate))


def forward_all(levels, saved_inputs, first, second, dep):
    ticks, _, rows, width = saved_inputs.shape
    rank = first.shape[1] // 2
    rest = ticks

    def made(lanes, dtype):
        return jax.ShapeDtypeStruct((rest, rows, lanes), dtype)

    def block(lanes):
        return pl.BlockSpec((1, rows, lanes), lambda i: (i, 0, 0))

    return pl.pallas_call(
        forward_kernel,
        grid=(rest,),
        out_shape=[made(width, BF16), made(rank, BF16), made(rank, F32), made(rank, F32), made(rank, F32)],
        in_specs=[
            SCALAR,
            pl.BlockSpec((1, 1, rows, width), lambda i: (i, 0, 0, 0)),
            IN_VMEM,
            IN_VMEM,
            ANYWHERE,
        ],
        out_specs=[block(width)] + [block(rank)] * 4,
        compiler_params=LIMIT,
        cost_estimate=pl.CostEstimate(flops=rest * 2 * rows * width * rank, bytes_accessed=rest * 4 * rows * width, transcendentals=0),
        name="forward_all",
    )(levels, saved_inputs, first, second, dep)


def tick_kernel(tick, flags_ref, incoming_ref, x_ref, first_ref, second_ref, latent_ref, slope_ref, inverse_ref, dep_ref, sent_ref, grad_latent_ref, x, second, sems):
    level = flags_ref[1]
    get_x = pltpu.make_async_copy(x_ref.at[pl.ds(tick, 1)], x, sems.at[0])
    get_second = pltpu.make_async_copy(second_ref, second, sems.at[1])

    @pl.when(flags_ref[0] == 1)
    def _():
        get_x.start()

        @pl.when(level == 0)
        def _():
            get_second.start()
            get_second.wait()

        get_x.wait()
        for value, map_ref in ((1, first_ref), (0, second)):

            @pl.when(level == value)
            def _():
                relay(
                    incoming_ref,
                    x,
                    map_ref,
                    latent_ref[0],
                    slope_ref[0],
                    inverse_ref[0][:, :1],
                    sent_ref,
                    grad_latent_ref,
                )


def later_tick(tick, works, level, incoming, saved_inputs, first, second, latents, slopes, inverses, dep):
    _, _, rows, width = saved_inputs.shape
    rank = first.shape[1] // 2
    narrow = pl.BlockSpec((1, rows, rank), lambda i: (tick, 0, 0))
    return pl.pallas_call(
        functools.partial(tick_kernel, tick),
        grid=(1,),
        out_shape=[
            jax.ShapeDtypeStruct((rows, width), BF16),
            jax.ShapeDtypeStruct((rows, rank), BF16),
        ],
        in_specs=[
            SCALAR,
            IN_VMEM,
            ANYWHERE,
            IN_VMEM,
            ANYWHERE,
            narrow,
            narrow,
            narrow,
            ANYWHERE,
        ],
        out_specs=[IN_VMEM] * 2,
        scratch_shapes=[
            pltpu.VMEM((1, 1, rows, width), BF16),
            pltpu.VMEM(second.shape, BF16),
            pltpu.SemaphoreType.DMA((2,)),
        ],
        compiler_params=LIMIT,
        cost_estimate=pl.CostEstimate(
            flops=40 * rows * width * rank, bytes_accessed=40 * rows * width, transcendentals=0
        ),
        name="later_tick",
    )(
        jnp.stack([works.astype(jnp.int32), level.astype(jnp.int32)]),
        incoming,
        saved_inputs,
        first,
        second,
        latents,
        slopes,
        inverses,
        dep,
    )


def turned(block):
    share, rank = block.shape
    room = -(-share // 128) * 128
    if room != share:
        block = jnp.concatenate([block, jnp.zeros((room - share, rank), block.dtype)], axis=0)
    return block.T[:, :share]


def beside_kernel(left_ref, right_ref, out_ref):
    lanes = left_ref.shape[1]
    out_ref[:, :lanes] = left_ref[...]
    out_ref[:, lanes:] = right_ref[...]


def beside(left, right):
    rows, lanes = left.shape
    run = rows // 4
    block = pl.BlockSpec((run, lanes), lambda i: (i, 0))
    return pl.pallas_call(
        beside_kernel,
        grid=(rows // run,),
        out_shape=jax.ShapeDtypeStruct((rows, 2 * lanes), left.dtype),
        in_specs=[block, block],
        out_specs=pl.BlockSpec((run, 2 * lanes), lambda i: (i, 0)),
        compiler_params=LIMIT,
        name="side_by_side",
    )(left, right)


def sum_kernel(moved_ref, out_ref):
    total = jnp.sum(moved_ref[...].astype(F32), axis=0)
    if total.shape == out_ref.shape:
        out_ref[...] = total
    else:
        rank = total.shape[1] // 2
        zeros = jnp.zeros((total.shape[0], rank), F32)
        out_ref[...] = jnp.concatenate([total[:, :rank], zeros, total[:, rank:], zeros], axis=1)


def summed(moved, lanes):
    return pl.pallas_call(
        sum_kernel,
        out_shape=jax.ShapeDtypeStruct((moved.shape[1], lanes), F32),
        in_specs=[IN_VMEM],
        out_specs=IN_VMEM,
        compiler_params=LIMIT,
        name="sum_partials",
    )(moved)


def finish_kernel(even_ref, total_ref, core_ref, over_ref, grad_ref, down_ref, up_ref, sem):
    for value, source in ((1, core_ref), (0, over_ref)):

        @pl.when(even_ref[0] == value)
        def _():
            pltpu.make_async_copy(source, grad_ref.at[0], sem).start()

    rank = down_ref.shape[2]
    for i, out in enumerate((down_ref, up_ref)):
        for j, level in enumerate((1, 0)):
            at = (2 * i + j) * rank
            out[level, 0] = turned(total_ref[:, at : at + rank])
    pltpu.make_async_copy(core_ref, grad_ref.at[0], sem).wait()


def finish(flag, total, core, over, share, rank):
    made = jax.ShapeDtypeStruct((2, 1, rank, share), F32)
    return pl.pallas_call(
        finish_kernel,
        out_shape=[jax.ShapeDtypeStruct((1,) + core.shape, core.dtype), made, made],
        in_specs=[SCALAR, IN_VMEM, ANYWHERE, ANYWHERE],
        out_specs=[ANYWHERE, IN_VMEM, IN_VMEM],
        scratch_shapes=[pltpu.SemaphoreType.DMA],
        compiler_params=LIMIT,
        name="finish",
    )(flag, total, core, over)


def on_device(saved_inputs, grad_in, adapter_down, adapter_up):
    n_sec = lax.axis_size("section")
    n_dp = lax.axis_size("dp")
    n_z = n_dp // 2
    position = lax.axis_index("section")
    ticks = saved_inputs.shape[0]
    rank, share = adapter_down.shape[2], adapter_down.shape[3]
    width = saved_inputs.shape[3]
    even = position % 2 == 0
    two_layers = position + ticks - 1 >= n_sec
    levels = [1 - (position + tick) // n_sec for tick in range(ticks)]

    def gather_two(down, up):
        shard = jnp.stack(
            [jnp.concatenate([down[v].T, up[v].T], axis=1) for v in (1, 0)]
        )
        first, second = ring_gather(shard, n_z)
        return first.reshape(width, 2 * rank), second.reshape(width, 2 * rank)

    def gather_one(down, up):
        shard = jnp.concatenate([down[1].T, up[1].T], axis=1)
        copies = jnp.broadcast_to(shard[None], (n_dp,) + shard.shape)
        full = lax.all_to_all(copies, "dp", 0, 0, tiled=True)
        full = full.reshape(width, 2 * rank)
        return full, unset(full.shape, full.dtype)

    first, second = lax.cond(
        two_layers, gather_two, gather_one, adapter_down[:, 0], adapter_up[:, 0]
    )

    sent, grad_latent, _ = first_tick(saved_inputs, grad_in[0], first)
    level_stack = jnp.stack(levels).astype(jnp.int32)
    normeds, actives, latents, slopes, inverses = forward_all(
        level_stack, saved_inputs, first, second, grad_latent
    )

    inside = [(s, s - 1) for s in range(1, n_sec, 2)]
    across = [(s, (s - 1) % n_sec) for s in range(0, n_sec, 2)]

    grads = [grad_in[0]]
    grad_latents = [grad_latent]
    over = lax.ppermute(sent, "section", across)
    core = lax.ppermute(sent, "section", inside)
    for tick in range(1, ticks):

        def layer(works, incoming, dep):
            return later_tick(
                tick,
                works,
                levels[tick],
                incoming,
                saved_inputs,
                first,
                second,
                latents,
                slopes,
                inverses,
                dep,
            )

        sent_even, latent_even = layer(even, core, grad_latent)
        next_over = lax.ppermute(sent_even, "section", across)
        sent_odd, latent_odd = layer(~even, over, latent_even)
        next_core = lax.ppermute(sent_odd, "section", inside)
        grads.append(jnp.where(even, core, over))
        grad_latents.append(jnp.where(even, latent_even, latent_odd))
        over, core = next_over, next_core

    normed_all = normeds.reshape(-1, width)
    grads_all = jnp.concatenate(grads, axis=0)

    def products(lats, acts):
        contract = (((0,), (0,)), ((), ()))
        down = lax.dot_general(normed_all, lats, contract, preferred_element_type=F32)
        up = lax.dot_general(grads_all, acts, contract, preferred_element_type=F32)
        both = beside(down.astype(BF16), up.astype(BF16))
        moved = lax.all_to_all(both.reshape(n_dp, share, -1), "dp", 0, 0, tiled=True)
        return summed(moved, 4 * rank)

    def reduce_one(lats, acts):
        return products(lats.reshape(-1, rank), acts.reshape(-1, rank))

    def reduce_two(lats, acts):
        level = level_stack[:, None, None]
        zero = jnp.zeros((), BF16)

        def split(value):
            both = [jnp.where(level == 1, value, zero), jnp.where(level == 0, value, zero)]
            return jnp.concatenate(both, axis=2).reshape(-1, 2 * rank)

        return products(split(lats), split(acts))

    total = lax.cond(two_layers, reduce_two, reduce_one, jnp.stack(grad_latents), actives)
    flag = even.astype(jnp.int32)[None]
    return tuple(finish(flag, total, core, over, share, rank))


def solution(mesh):
    in_specs = (
        P(None, "section", "dp", None),
        P("section", "dp", None),
        P(None, "section", None, "dp"),
        P(None, "section", None, "dp"),
    )
    out_specs = (
        P("section", "dp", None),
        P(None, "section", None, "dp"),
        P(None, "section", None, "dp"),
    )
    return jax.shard_map(
        on_device, mesh=mesh, in_specs=in_specs, out_specs=out_specs, check_vma=False
    )
```

```python
import functools

import jax
import jax.numpy as jnp
from jax import lax
from jax.experimental import pallas as pl
from jax.experimental.pallas import tpu as pltpu
from jax.sharding import PartitionSpec as P

EPS = 1e-06
F32 = jnp.float32
BF16 = jnp.bfloat16
LIMIT = pltpu.CompilerParams(vmem_limit_bytes=24 * 1024 * 1024)
IN_VMEM = pl.BlockSpec(memory_space=pltpu.VMEM)
ANYWHERE = pl.BlockSpec(memory_space=pl.ANY)
COST = pl.CostEstimate(flops=2**32, bytes_accessed=2**23, transcendentals=0)
SCALAR = pl.BlockSpec(memory_space=pltpu.SMEM)


def dp_pairs(n_z, step, flip):
    return [
        (2 * z + h, 2 * ((z + step) % n_z) + (h ^ flip)) for z in range(n_z) for h in range(2)
    ]


def shifted(value, n_z, step):
    return lax.ppermute(value, "dp", dp_pairs(n_z, step, 0))


def swapped(value, n_z):
    return lax.ppermute(value, "dp", dp_pairs(n_z, 0, 1))


def place_kernel(n_z, place_ref, *refs):
    half = n_z // 2
    pieces, outs, sem = refs[: n_z + 1], refs[n_z + 1 : n_z + 3], refs[n_z + 3]
    z = place_ref[0]
    offsets = [0] + list(range(-1, -half, -1)) + list(range(1, half))
    copies = []
    for level, out in enumerate(outs):
        for piece, offset in zip(pieces, offsets):
            at = lax.rem(z + (offset + n_z), n_z) * 2
            copies.append((piece.at[:, level], out.at[pl.ds(at, 2)]))
        far = lax.rem(z + half, n_z) * 2
        for h in range(2):
            copies.append((pieces[n_z - 1 + h].at[:, level], out.at[pl.ds(far + h, 1)]))
    started = [
        pltpu.make_async_copy(source, target, sem.at[i])
        for i, (source, target) in enumerate(copies)
    ]
    for copy in started:
        copy.start()
    for copy in started:
        copy.wait()


def ring_gather(shard, n_z):
    index = lax.axis_index("dp")
    z, h = index // 2, index % 2
    other = swapped(shard, n_z)
    pair = jnp.stack([jnp.where(h == 0, shard, other), jnp.where(h == 0, other, shard)])
    half = n_z // 2
    rights, lefts = [], []
    right, left = pair, pair
    for _ in range(1, half):
        right, left = shifted(right, n_z, 1), shifted(left, n_z, -1)
        rights.append(right)
        lefts.append(left)
    pieces = [pair] + rights + lefts + [shifted(right[:1], n_z, 1), shifted(left[1:], n_z, -1)]
    _, share, lanes = shard.shape
    whole = jax.ShapeDtypeStruct((2 * n_z, share, lanes), shard.dtype)
    return pl.pallas_call(
        functools.partial(place_kernel, n_z),
        out_shape=[whole, whole],
        in_specs=[SCALAR] + [ANYWHERE] * len(pieces),
        out_specs=[IN_VMEM] * 2,
        scratch_shapes=[pltpu.SemaphoreType.DMA((2 * (n_z + 1),))],
        compiler_params=LIMIT,
        name="place_maps",
    )(z.astype(jnp.int32)[None], *pieces)


def empty_kernel(out_ref):
    pass


def unset(shape, dtype):
    return pl.pallas_call(
        empty_kernel,
        out_shape=jax.ShapeDtypeStruct(shape, dtype),
        out_specs=ANYWHERE,
        name="unset",
    )()


def relay(incoming_ref, x_ref, map_ref, latent, slope, inverse, sent_ref, grad_latent_ref):
    width, rank = x_ref.shape[-1], latent.shape[1]
    grad_act = jnp.dot(incoming_ref[...], map_ref[:, rank:], preferred_element_type=F32)
    grad_latent = (grad_act * slope).astype(BF16)
    grad_latent_ref[...] = grad_latent
    inner = jnp.sum(grad_latent.astype(F32) * latent, axis=-1, keepdims=True) / width
    scale = inverse * inverse * inner
    run = width // 4
    for start in range(0, width, run):
        at = pl.ds(start, run)
        grad_normed = lax.dot_general(
            grad_latent, map_ref[at, :rank], (((1,), (1,)), ((), ())), preferred_element_type=F32
        )
        x = x_ref[0, 0, :, at].astype(F32)
        sent = incoming_ref[:, at].astype(F32) + (inverse * grad_normed - x * scale)
        sent_ref[:, at] = sent.astype(BF16)


def normalise(x_ref, normed_ref):
    x = x_ref[0, 0].astype(F32)
    inverse = lax.rsqrt(jnp.mean(x * x, axis=-1, keepdims=True) + EPS)
    normed_ref[...] = (x * inverse).astype(BF16)
    return inverse


def first_kernel(x_ref, incoming_ref, map_ref, dep_ref, sent_ref, grad_latent_ref, normed_ref):
    rank = grad_latent_ref.shape[1]
    inverse = normalise(x_ref, normed_ref)
    latent = jnp.dot(normed_ref[...], map_ref[:, :rank], preferred_element_type=F32)
    gate = jax.nn.sigmoid(latent)
    slope = gate * (1.0 + latent * (1.0 - gate))
    relay(incoming_ref, x_ref, map_ref, latent, slope, inverse, sent_ref, grad_latent_ref)


def first_tick(part, saved_inputs, incoming, maps, dep):
    _, _, rows, width = saved_inputs.shape
    rows //= 2
    rank = maps.shape[1] // 2
    return pl.pallas_call(
        first_kernel,
        grid=(1,),
        out_shape=[
            jax.ShapeDtypeStruct((rows, width), BF16),
            jax.ShapeDtypeStruct((rows, rank), BF16),
        ],
        in_specs=[
            pl.BlockSpec((1, 1, rows, width), lambda i: (0, 0, part, 0)),
            pl.BlockSpec((rows, width), lambda i: (part, 0)),
            IN_VMEM,
            ANYWHERE,
        ],
        out_specs=[IN_VMEM] * 2,
        scratch_shapes=[pltpu.VMEM((rows, width), BF16)],
        compiler_params=LIMIT,
        cost_estimate=COST,
        name="first_tick",
    )(saved_inputs, incoming, maps, dep)


def forward_kernel(level_ref, x_ref, first_ref, second_ref, dep_ref, normed_ref, active_ref, latent_ref, slope_ref, inverse_ref):
    rank = active_ref.shape[2]
    inverse = normalise(x_ref, normed_ref.at[0])
    inverse_ref[0] = jnp.broadcast_to(inverse, inverse_ref.shape[1:])
    level = level_ref[pl.program_id(0)]
    for value, map_ref in ((1, first_ref), (0, second_ref)):

        @pl.when(level == value)
        def _():
            latent_ref[0] = jnp.dot(
                normed_ref[0], map_ref[:, :rank], preferred_element_type=F32
            )

    latent = latent_ref[0]
    gate = jax.nn.sigmoid(latent)
    active_ref[0] = (latent * gate).astype(BF16)
    slope_ref[0] = gate * (1.0 + latent * (1.0 - gate))


def forward_all(levels, saved_inputs, first, second, dep):
    ticks, _, rows, width = saved_inputs.shape
    rank = first.shape[1] // 2
    rest = ticks

    def made(lanes, dtype):
        return jax.ShapeDtypeStruct((rest, rows, lanes), dtype)

    def block(lanes):
        return pl.BlockSpec((1, rows, lanes), lambda i: (i, 0, 0))

    return pl.pallas_call(
        forward_kernel,
        grid=(rest,),
        out_shape=[made(width, BF16), made(rank, BF16), made(rank, F32), made(rank, F32), made(rank, F32)],
        in_specs=[
            SCALAR,
            pl.BlockSpec((1, 1, rows, width), lambda i: (i, 0, 0, 0)),
            IN_VMEM,
            IN_VMEM,
            ANYWHERE,
        ],
        out_specs=[block(width)] + [block(rank)] * 4,
        compiler_params=LIMIT,
        cost_estimate=pl.CostEstimate(flops=rest * 2 * rows * width * rank, bytes_accessed=rest * 4 * rows * width, transcendentals=0),
        name="forward_all",
    )(levels, saved_inputs, first, second, dep)


def tick_kernel(tick, part, level_ref, incoming_ref, x_ref, first_ref, second_ref, latent_ref, slope_ref, inverse_ref, dep_ref, sent_ref, grad_latent_ref, x, second, sems):
    level = level_ref[tick]
    rows = x.shape[2]
    get_x = pltpu.make_async_copy(
        x_ref.at[pl.ds(tick, 1), :, pl.ds(part * rows, rows)], x, sems.at[0]
    )
    get_x.start()

    @pl.when(level == 0)
    def _():
        get_second = pltpu.make_async_copy(second_ref, second, sems.at[1])
        get_second.start()
        get_second.wait()

    get_x.wait()
    for value, map_ref in ((1, first_ref), (0, second)):

        @pl.when(level == value)
        def _():
            relay(
                incoming_ref,
                x,
                map_ref,
                latent_ref[0],
                slope_ref[0],
                inverse_ref[0][:, :1],
                sent_ref,
                grad_latent_ref,
            )


def later_tick(tick, part, levels, incoming, saved_inputs, first, second, latents, slopes, inverses, dep):
    rows, width = incoming.shape
    rank = first.shape[1] // 2
    narrow = pl.BlockSpec((1, rows, rank), lambda i: (tick, part, 0))
    return pl.pallas_call(
        functools.partial(tick_kernel, tick, part),
        grid=(1,),
        out_shape=[
            jax.ShapeDtypeStruct((rows, width), BF16),
            jax.ShapeDtypeStruct((rows, rank), BF16),
        ],
        in_specs=[SCALAR, IN_VMEM, ANYWHERE, IN_VMEM, ANYWHERE, narrow, narrow, narrow, ANYWHERE],
        out_specs=[IN_VMEM] * 2,
        scratch_shapes=[
            pltpu.VMEM((1, 1, rows, width), BF16),
            pltpu.VMEM(second.shape, BF16),
            pltpu.SemaphoreType.DMA((2,)),
        ],
        compiler_params=LIMIT,
        cost_estimate=COST,
        name="later_tick",
    )(levels, incoming, saved_inputs, first, second, latents, slopes, inverses, dep)


def beside_kernel(left_ref, right_ref, out_ref):
    lanes = left_ref.shape[1]
    out_ref[:, :lanes] = left_ref[...]
    out_ref[:, lanes:] = right_ref[...]


def beside(left, right):
    rows, lanes = left.shape
    run = rows // 4
    block = pl.BlockSpec((run, lanes), lambda i: (i, 0))
    return pl.pallas_call(
        beside_kernel,
        grid=(rows // run,),
        out_shape=jax.ShapeDtypeStruct((rows, 2 * lanes), left.dtype),
        in_specs=[block, block],
        out_specs=pl.BlockSpec((run, 2 * lanes), lambda i: (i, 0)),
        compiler_params=LIMIT,
        name="side_by_side",
    )(left, right)


def sum_kernel(moved_ref, out_ref):
    total = jnp.sum(moved_ref[...].astype(F32), axis=0)
    if total.shape == out_ref.shape:
        out_ref[...] = total
    else:
        rank = total.shape[1] // 2
        zeros = jnp.zeros((total.shape[0], rank), F32)
        out_ref[...] = jnp.concatenate([total[:, :rank], zeros, total[:, rank:], zeros], axis=1)


def summed(moved, lanes):
    return pl.pallas_call(
        sum_kernel,
        out_shape=jax.ShapeDtypeStruct((moved.shape[1], lanes), F32),
        in_specs=[IN_VMEM],
        out_specs=IN_VMEM,
        compiler_params=LIMIT,
        name="sum_partials",
    )(moved)


def finish_kernel(total_ref, low_ref, high_ref, grad_ref, down_ref, up_ref):
    rows, rank = low_ref.shape[0], down_ref.shape[3]
    grad_ref[0, :rows] = low_ref[...]
    grad_ref[0, rows:] = high_ref[...]
    for i, out in enumerate((down_ref, up_ref)):
        for j, level in enumerate((1, 0)):
            at = (2 * i + j) * rank
            out[level, 0] = total_ref[:, at : at + rank]


def finish(total, low, high, share, rank):
    rows, width = low.shape
    made = jax.ShapeDtypeStruct((2, 1, share, rank), F32)
    return pl.pallas_call(
        finish_kernel,
        out_shape=[jax.ShapeDtypeStruct((1, 2 * rows, width), low.dtype), made, made],
        in_specs=[IN_VMEM] * 3,
        out_specs=[IN_VMEM] * 3,
        compiler_params=LIMIT,
        name="finish",
    )(total, low, high)


def on_device(saved_inputs, grad_in, adapter_down, adapter_up):
    n_sec = lax.axis_size("section")
    n_dp = lax.axis_size("dp")
    n_z = n_dp // 2
    position = lax.axis_index("section")
    ticks = saved_inputs.shape[0]
    rank, share = adapter_down.shape[2], adapter_down.shape[3]
    width = saved_inputs.shape[3]
    two_layers = position + ticks - 1 >= n_sec
    levels = [1 - (position + tick) // n_sec for tick in range(ticks)]

    def gather_two(down, up):
        shard = jnp.stack(
            [jnp.concatenate([down[v].T, up[v].T], axis=1) for v in (1, 0)]
        )
        first, second = ring_gather(shard, n_z)
        return first.reshape(width, 2 * rank), second.reshape(width, 2 * rank)

    def gather_one(down, up):
        shard = jnp.concatenate([down[1].T, up[1].T], axis=1)
        copies = jnp.broadcast_to(shard[None], (n_dp,) + shard.shape)
        full = lax.all_to_all(copies, "dp", 0, 0, tiled=True)
        full = full.reshape(width, 2 * rank)
        return full, unset(full.shape, full.dtype)

    first, second = lax.cond(
        two_layers, gather_two, gather_one, adapter_down[:, 0], adapter_up[:, 0]
    )

    down_one = [(s, (s - 1) % n_sec) for s in range(n_sec)]
    grads = [grad_in[0]]
    grad_latents = []
    moving = []
    dep = first
    for part in range(2):
        sent, dep = first_tick(part, saved_inputs, grad_in[0], first, dep)
        grad_latents.append(dep)
        moving.append(lax.ppermute(sent, "section", down_one))
    level_stack = jnp.stack(levels).astype(jnp.int32)
    normeds, actives, latents, slopes, inverses = forward_all(
        level_stack, saved_inputs, first, second, dep
    )
    for tick in range(1, ticks):
        grads += moving
        arrived, moving = moving, []
        for part in range(2):
            sent, dep = later_tick(
                tick,
                part,
                level_stack,
                arrived[part],
                saved_inputs,
                first,
                second,
                latents,
                slopes,
                inverses,
                dep,
            )
            grad_latents.append(dep)
            moving.append(lax.ppermute(sent, "section", down_one))

    normed_all = normeds.reshape(-1, width)
    grads_all = jnp.concatenate(grads, axis=0)

    def products(lats, acts):
        contract = (((0,), (0,)), ((), ()))
        down = lax.dot_general(normed_all, lats, contract, preferred_element_type=F32)
        up = lax.dot_general(grads_all, acts, contract, preferred_element_type=F32)
        both = beside(down.astype(BF16), up.astype(BF16))
        moved = lax.all_to_all(both.reshape(n_dp, share, -1), "dp", 0, 0, tiled=True)
        return summed(moved, 4 * rank)

    def reduce_one(lats, acts):
        return products(lats.reshape(-1, rank), acts.reshape(-1, rank))

    def reduce_two(lats, acts):
        level = level_stack[:, None, None]
        zero = jnp.zeros((), BF16)

        def split(value):
            both = [jnp.where(level == 1, value, zero), jnp.where(level == 0, value, zero)]
            return jnp.concatenate(both, axis=2).reshape(-1, 2 * rank)

        return products(split(lats), split(acts))

    total = lax.cond(two_layers, reduce_two, reduce_one, jnp.concatenate(grad_latents).reshape(actives.shape), actives)
    grad_out, down_grad, up_grad = finish(total, *moving, share, rank)
    return grad_out, jnp.swapaxes(down_grad, 2, 3), jnp.swapaxes(up_grad, 2, 3)


def solution(mesh):
    in_specs = (
        P(None, "section", "dp", None),
        P("section", "dp", None),
        P(None, "section", None, "dp"),
        P(None, "section", None, "dp"),
    )
    out_specs = (
        P("section", "dp", None),
        P(None, "section", None, "dp"),
        P(None, "section", None, "dp"),
    )
    return jax.shard_map(
        on_device, mesh=mesh, in_specs=in_specs, out_specs=out_specs, check_vma=False
    )
```

```python
import functools

import jax
import jax.numpy as jnp
from jax import lax
from jax.experimental import pallas as pl
from jax.experimental.pallas import tpu as pltpu
from jax.sharding import PartitionSpec as P

EPS = 1e-06
F32 = jnp.float32
BF16 = jnp.bfloat16
LIMIT = pltpu.CompilerParams(vmem_limit_bytes=24 * 1024 * 1024)
IN_VMEM = pl.BlockSpec(memory_space=pltpu.VMEM)
ANYWHERE = pl.BlockSpec(memory_space=pl.ANY)
COST = pl.CostEstimate(flops=2**32, bytes_accessed=2**23, transcendentals=0)
SCALAR = pl.BlockSpec(memory_space=pltpu.SMEM)


def dp_pairs(n_z, step, flip):
    return [
        (2 * z + h, 2 * ((z + step) % n_z) + (h ^ flip)) for z in range(n_z) for h in range(2)
    ]


def shifted(value, n_z, step):
    return lax.ppermute(value, "dp", dp_pairs(n_z, step, 0))


def swapped(value, n_z):
    return lax.ppermute(value, "dp", dp_pairs(n_z, 0, 1))


def ring_gather(shard, n_z):
    index = lax.axis_index("dp")
    z, h = index // 2, index % 2
    other = swapped(shard, n_z)
    pair = jnp.stack([jnp.where(h == 0, shard, other), jnp.where(h == 0, other, shard)], axis=1)
    half = n_z // 2
    full = unset((2, n_z) + pair.shape[1:], pair.dtype)

    def placed(full, piece, offset):
        return lax.dynamic_update_slice(full, piece[:, None], (0, (z + offset) % n_z, 0, 0, 0))

    full = placed(full, pair, 0)
    right, left = pair, pair
    for step in range(1, half):
        right, left = shifted(right, n_z, 1), shifted(left, n_z, -1)
        full = placed(full, right, -step)
        full = placed(full, left, step)
    right, left = shifted(right[:, :1], n_z, 1), shifted(left[:, 1:], n_z, -1)
    return placed(full, jnp.concatenate([right, left], axis=1), half)


def empty_kernel(out_ref):
    pass


def unset(shape, dtype):
    return pl.pallas_call(
        empty_kernel,
        out_shape=jax.ShapeDtypeStruct(shape, dtype),
        out_specs=ANYWHERE,
        name="unset",
    )()


def norm_kernel(x_ref, normed_ref, inverse_ref):
    x = x_ref[0, 0].astype(F32)
    inverse = lax.rsqrt(jnp.mean(x * x, axis=-1, keepdims=True) + EPS)
    normed_ref[0] = (x * inverse).astype(BF16)
    inverse_ref[0] = jnp.broadcast_to(inverse, inverse_ref.shape[1:])


def norms(saved_inputs):
    ticks, _, rows, width = saved_inputs.shape
    return pl.pallas_call(
        norm_kernel,
        grid=(ticks,),
        out_shape=[
            jax.ShapeDtypeStruct((ticks, rows, width), BF16),
            jax.ShapeDtypeStruct((ticks, rows, 128), F32),
        ],
        in_specs=[pl.BlockSpec((1, 1, rows, width), lambda i: (i, 0, 0, 0))],
        out_specs=[
            pl.BlockSpec((1, rows, width), lambda i: (i, 0, 0)),
            pl.BlockSpec((1, rows, 128), lambda i: (i, 0, 0)),
        ],
        compiler_params=LIMIT,
        cost_estimate=COST,
        name="norms",
    )(saved_inputs)


def forward_values(normed, down):
    latent = jnp.dot(normed, down, preferred_element_type=F32)
    gate = jax.nn.sigmoid(latent)
    active = (latent * gate).astype(BF16)
    return latent, gate * (1.0 + latent * (1.0 - gate)), active


def forward_kernel(levels_ref, normed_ref, maps_ref, dep_ref, latent_ref, slope_ref, active_ref):
    rank = latent_ref.shape[2]
    latent_ref[0], slope_ref[0], active_ref[0] = forward_values(
        normed_ref[0], maps_ref[0, :, :rank]
    )


def forward_rest(levels, normed, maps, dep):
    ticks, rows, width = normed.shape
    rank = maps.shape[2] // 2
    rest = ticks - 1

    def made(dtype):
        return jax.ShapeDtypeStruct((rest, rows, rank), dtype)

    return pl.pallas_call(
        forward_kernel,
        grid_spec=pltpu.PrefetchScalarGridSpec(
            num_scalar_prefetch=1,
            grid=(rest,),
            in_specs=[
                pl.BlockSpec((1, rows, width), lambda i, levels: (i + 1, 0, 0)),
                pl.BlockSpec((1, width, 2 * rank), lambda i, levels: (levels[i + 1], 0, 0)),
                ANYWHERE,
            ],
            out_specs=[pl.BlockSpec((1, rows, rank), lambda i, levels: (i, 0, 0))] * 3,
        ),
        out_shape=[made(F32), made(F32), made(BF16)],
        compiler_params=LIMIT,
        cost_estimate=COST,
        name="forward_rest",
    )(levels, normed, maps, dep)


def tick_kernel(tick, part, levels_ref, incoming_ref, normed_ref, inverse_ref, maps_ref, *refs):
    _, rows, width = normed_ref.shape
    rank = maps_ref.shape[2] // 2
    if tick == 0:
        stack_ref, sent_ref, grad_latent_ref, active_ref, sem = refs[1:]
    else:
        latent_ref, slope_ref = refs[:2]
        stack_ref, sent_ref, grad_latent_ref, sem = refs[3:]
    keep = pltpu.make_async_copy(
        incoming_ref, stack_ref.at[tick, pl.ds(part * rows, rows)], sem
    )
    keep.start()
    if tick == 0:
        latent, slope, active_ref[...] = forward_values(normed_ref[0], maps_ref[0, :, :rank])
    else:
        latent, slope = latent_ref[0], slope_ref[0]
    grad_act = jnp.dot(incoming_ref[...], maps_ref[0, :, rank:], preferred_element_type=F32)
    grad_latent = (grad_act * slope).astype(BF16)
    grad_latent_ref[...] = grad_latent
    inner = jnp.sum(grad_latent.astype(F32) * latent, axis=-1, keepdims=True) / width
    inverse = inverse_ref[0][:, :1]
    scale = inverse * inner
    run = width // 4
    for start in range(0, width, run):
        at = pl.ds(start, run)
        grad_normed = lax.dot_general(
            grad_latent, maps_ref[0, at, :rank], (((1,), (1,)), ((), ())), preferred_element_type=F32
        )
        sent = incoming_ref[:, at].astype(F32) + (
            inverse * grad_normed - normed_ref[0, :, at].astype(F32) * scale
        )
        sent_ref[:, at] = sent.astype(BF16)
    keep.wait()


def tick_layer(tick, part, levels, incoming, normed, inverse, maps, forward, stack):
    _, rows, width = normed.shape
    rows //= 2
    rank = maps.shape[2] // 2
    first = tick == 0
    narrow = jax.ShapeDtypeStruct((rows, rank), BF16)
    incoming_spec = (
        pl.BlockSpec((rows, width), lambda i, levels: (part, 0)) if first else IN_VMEM
    )
    forward_spec = pl.BlockSpec((1, rows, rank), lambda i, levels: (tick - 1, part, 0))
    return pl.pallas_call(
        functools.partial(tick_kernel, tick, part),
        grid_spec=pltpu.PrefetchScalarGridSpec(
            num_scalar_prefetch=1,
            grid=(1,),
            in_specs=[
                incoming_spec,
                pl.BlockSpec((1, rows, width), lambda i, levels: (tick, part, 0)),
                pl.BlockSpec((1, rows, 128), lambda i, levels: (tick, part, 0)),
                pl.BlockSpec((1, width, 2 * rank), lambda i, levels: (levels[tick], 0, 0)),
            ]
            + [forward_spec] * len(forward)
            + [ANYWHERE],
            out_specs=[ANYWHERE, IN_VMEM, IN_VMEM] + [IN_VMEM] * first,
            scratch_shapes=[pltpu.SemaphoreType.DMA],
        ),
        out_shape=[
            jax.ShapeDtypeStruct(stack.shape, stack.dtype),
            jax.ShapeDtypeStruct((rows, width), BF16),
            narrow,
        ]
        + [narrow] * first,
        input_output_aliases={5 + len(forward): 0},
        compiler_params=LIMIT,
        cost_estimate=COST,
        name="tick_layer",
    )(levels, incoming, normed, inverse, maps, *forward, stack)


def beside_kernel(left_ref, right_ref, out_ref):
    lanes = left_ref.shape[1]
    out_ref[:, :lanes] = left_ref[...]
    out_ref[:, lanes:] = right_ref[...]


def beside(left, right):
    rows, lanes = left.shape
    run = rows // 4
    block = pl.BlockSpec((run, lanes), lambda i: (i, 0))
    return pl.pallas_call(
        beside_kernel,
        grid=(rows // run,),
        out_shape=jax.ShapeDtypeStruct((rows, 2 * lanes), left.dtype),
        in_specs=[block, block],
        out_specs=pl.BlockSpec((run, 2 * lanes), lambda i: (i, 0)),
        compiler_params=LIMIT,
        name="side_by_side",
    )(left, right)


def sum_kernel(moved_ref, out_ref):
    total = jnp.sum(moved_ref[...].astype(F32), axis=0)
    if total.shape == out_ref.shape:
        out_ref[...] = total
    else:
        rank = total.shape[1] // 2
        zeros = jnp.zeros((total.shape[0], rank), F32)
        out_ref[...] = jnp.concatenate([total[:, :rank], zeros, total[:, rank:], zeros], axis=1)


def summed(moved, lanes):
    return pl.pallas_call(
        sum_kernel,
        out_shape=jax.ShapeDtypeStruct((moved.shape[1], lanes), F32),
        in_specs=[IN_VMEM],
        out_specs=IN_VMEM,
        compiler_params=LIMIT,
        name="sum_partials",
    )(moved)


def finish_kernel(total_ref, low_ref, high_ref, grad_ref, down_ref, up_ref):
    rows, rank = low_ref.shape[0], down_ref.shape[3]
    grad_ref[0, :rows] = low_ref[...]
    grad_ref[0, rows:] = high_ref[...]
    for i, out in enumerate((down_ref, up_ref)):
        for j, level in enumerate((1, 0)):
            at = (2 * i + j) * rank
            out[level, 0] = total_ref[:, at : at + rank]


def finish(total, low, high, share, rank):
    rows, width = low.shape
    made = jax.ShapeDtypeStruct((2, 1, share, rank), F32)
    return pl.pallas_call(
        finish_kernel,
        out_shape=[jax.ShapeDtypeStruct((1, 2 * rows, width), low.dtype), made, made],
        in_specs=[IN_VMEM] * 3,
        out_specs=[IN_VMEM] * 3,
        compiler_params=LIMIT,
        name="finish",
    )(total, low, high)


def on_device(saved_inputs, grad_in, adapter_down, adapter_up):
    n_sec = lax.axis_size("section")
    n_dp = lax.axis_size("dp")
    n_z = n_dp // 2
    position = lax.axis_index("section")
    ticks = saved_inputs.shape[0]
    rank, share = adapter_down.shape[2], adapter_down.shape[3]
    width = saved_inputs.shape[3]
    two_layers = position + ticks - 1 >= n_sec
    levels = [1 - (position + tick) // n_sec for tick in range(ticks)]

    def shard_of(down, up, level):
        return jnp.concatenate([down[level].T, up[level].T], axis=1)

    def gather_two(down, up, x):
        shards = jnp.stack([shard_of(down, up, level) for level in range(2)])
        full = ring_gather(shards, n_z)
        return full.reshape(2, width, 2 * rank), *norms(x)

    def gather_one(down, up, x):
        shard = shard_of(down, up, 1)
        copies = jnp.broadcast_to(shard[None], (n_dp,) + shard.shape)
        full = lax.all_to_all(copies, "dp", 0, 0, tiled=True)
        both = unset((2, width, 2 * rank), full.dtype)
        both = lax.dynamic_update_index_in_dim(both, full.reshape(width, 2 * rank), 1, 0)
        return both, *norms(x)

    maps, normed, inverse = lax.cond(
        two_layers, gather_two, gather_one, adapter_down[:, 0], adapter_up[:, 0], saved_inputs
    )

    down_one = [(s, (s - 1) % n_sec) for s in range(n_sec)]
    level_stack = jnp.stack(levels).astype(jnp.int32)
    stack = unset(normed.shape, grad_in.dtype)
    grad_latents, first_actives, moving = [], [], []
    for part in range(2):
        stack, sent, grad_latent, active = tick_layer(
            0, part, level_stack, grad_in[0], normed, inverse, maps, [], stack
        )
        grad_latents.append(grad_latent)
        first_actives.append(active)
        moving.append(lax.ppermute(sent, "section", down_one))
    latents, slopes, actives = forward_rest(level_stack, normed, maps, grad_latent)
    for tick in range(1, ticks):
        arrived, moving = moving, []
        for part in range(2):
            stack, sent, grad_latent = tick_layer(
                tick, part, level_stack, arrived[part], normed, inverse, maps, [latents, slopes], stack
            )
            grad_latents.append(grad_latent)
            moving.append(lax.ppermute(sent, "section", down_one))

    normed_all = normed.reshape(-1, width)
    grads_all = stack.reshape(-1, width)
    actives = jnp.concatenate([jnp.concatenate(first_actives)[None], actives], axis=0)

    def products(lats, acts):
        contract = (((0,), (0,)), ((), ()))
        down = lax.dot_general(normed_all, lats, contract, preferred_element_type=F32)
        up = lax.dot_general(grads_all, acts, contract, preferred_element_type=F32)
        both = beside(down.astype(BF16), up.astype(BF16))
        moved = lax.all_to_all(both.reshape(n_dp, share, -1), "dp", 0, 0, tiled=True)
        return summed(moved, 4 * rank)

    def reduce_one(lats, acts):
        return products(lats.reshape(-1, rank), acts.reshape(-1, rank))

    def reduce_two(lats, acts):
        level = level_stack[:, None, None]
        zero = jnp.zeros((), BF16)

        def split(value):
            both = [jnp.where(level == 1, value, zero), jnp.where(level == 0, value, zero)]
            return jnp.concatenate(both, axis=2).reshape(-1, 2 * rank)

        return products(split(lats), split(acts))

    total = lax.cond(two_layers, reduce_two, reduce_one, jnp.concatenate(grad_latents).reshape(actives.shape), actives)
    grad_out, down_grad, up_grad = finish(total, *moving, share, rank)
    return grad_out, jnp.swapaxes(down_grad, 2, 3), jnp.swapaxes(up_grad, 2, 3)


def solution(mesh):
    in_specs = (
        P(None, "section", "dp", None),
        P("section", "dp", None),
        P(None, "section", None, "dp"),
        P(None, "section", None, "dp"),
    )
    out_specs = (
        P("section", "dp", None),
        P(None, "section", None, "dp"),
        P(None, "section", None, "dp"),
    )
    return jax.shard_map(
        on_device, mesh=mesh, in_specs=in_specs, out_specs=out_specs, check_vma=False
    )
```

```python
import functools

import jax
import jax.numpy as jnp
from jax import lax
from jax.experimental import pallas as pl
from jax.experimental.pallas import tpu as pltpu
from jax.sharding import PartitionSpec as P

EPS = 1e-06
F32 = jnp.float32
BF16 = jnp.bfloat16
LIMIT = pltpu.CompilerParams(vmem_limit_bytes=24 * 1024 * 1024)
IN_VMEM = pl.BlockSpec(memory_space=pltpu.VMEM)
ANYWHERE = pl.BlockSpec(memory_space=pl.ANY)
COST = pl.CostEstimate(flops=2**32, bytes_accessed=2**23, transcendentals=0)
SCALAR = pl.BlockSpec(memory_space=pltpu.SMEM)


def dp_pairs(n_z, step, flip):
    return [
        (2 * z + h, 2 * ((z + step) % n_z) + (h ^ flip)) for z in range(n_z) for h in range(2)
    ]


def shifted(value, n_z, step):
    return lax.ppermute(value, "dp", dp_pairs(n_z, step, 0))


def swapped(value, n_z):
    return lax.ppermute(value, "dp", dp_pairs(n_z, 0, 1))


def ring_gather(shard, n_z, beside):
    index = lax.axis_index("dp")
    z, h = index // 2, index % 2
    other, *beside = lax.optimization_barrier((swapped(shard, n_z), *beside))
    pair = jnp.stack([jnp.where(h == 0, shard, other), jnp.where(h == 0, other, shard)], axis=1)
    half = n_z // 2
    full = unset((2, n_z) + pair.shape[1:], pair.dtype)

    def placed(full, piece, offset):
        return lax.dynamic_update_slice(full, piece[:, None], (0, (z + offset) % n_z, 0, 0, 0))

    full = placed(full, pair, 0)
    right, left = pair, pair
    for step in range(1, half):
        right, left = shifted(right, n_z, 1), shifted(left, n_z, -1)
        full = placed(full, right, -step)
        full = placed(full, left, step)
    right, left = shifted(right[:, :1], n_z, 1), shifted(left[:, 1:], n_z, -1)
    return placed(full, jnp.concatenate([right, left], axis=1), half), beside


def empty_kernel(out_ref):
    pass


def unset(shape, dtype):
    return pl.pallas_call(
        empty_kernel,
        out_shape=jax.ShapeDtypeStruct(shape, dtype),
        out_specs=ANYWHERE,
        name="unset",
    )()


def norm_kernel(x_ref, normed_ref, inverse_ref):
    x = x_ref[0, 0].astype(F32)
    inverse = lax.rsqrt(jnp.mean(x * x, axis=-1, keepdims=True) + EPS)
    normed_ref[0] = (x * inverse).astype(BF16)
    inverse_ref[0] = jnp.broadcast_to(inverse, inverse_ref.shape[1:])


def norms(saved_inputs):
    ticks, _, rows, width = saved_inputs.shape
    return pl.pallas_call(
        norm_kernel,
        grid=(ticks,),
        out_shape=[
            jax.ShapeDtypeStruct((ticks, rows, width), BF16),
            jax.ShapeDtypeStruct((ticks, rows, 128), F32),
        ],
        in_specs=[pl.BlockSpec((1, 1, rows, width), lambda i: (i, 0, 0, 0))],
        out_specs=[
            pl.BlockSpec((1, rows, width), lambda i: (i, 0, 0)),
            pl.BlockSpec((1, rows, 128), lambda i: (i, 0, 0)),
        ],
        compiler_params=LIMIT,
        cost_estimate=COST,
        name="norms",
    )(saved_inputs)


def forward_values(normed, down):
    latent = jnp.dot(normed, down, preferred_element_type=F32)
    gate = jax.nn.sigmoid(latent)
    active = (latent * gate).astype(BF16)
    return latent, gate * (1.0 + latent * (1.0 - gate)), active


def forward_kernel(levels_ref, normed_ref, maps_ref, dep_ref, latent_ref, slope_ref, active_ref):
    rank = latent_ref.shape[2]
    latent_ref[0], slope_ref[0], active_ref[0] = forward_values(
        normed_ref[0], maps_ref[0, :, :rank]
    )


def forward_rest(levels, normed, maps, dep):
    ticks, rows, width = normed.shape
    rank = maps.shape[2] // 2
    rest = ticks - 1

    def made(dtype):
        return jax.ShapeDtypeStruct((rest, rows, rank), dtype)

    return pl.pallas_call(
        forward_kernel,
        grid_spec=pltpu.PrefetchScalarGridSpec(
            num_scalar_prefetch=1,
            grid=(rest,),
            in_specs=[
                pl.BlockSpec((1, rows, width), lambda i, levels: (i + 1, 0, 0)),
                pl.BlockSpec((1, width, 2 * rank), lambda i, levels: (levels[i + 1], 0, 0)),
                ANYWHERE,
            ],
            out_specs=[pl.BlockSpec((1, rows, rank), lambda i, levels: (i, 0, 0))] * 3,
        ),
        out_shape=[made(F32), made(F32), made(BF16)],
        compiler_params=LIMIT,
        cost_estimate=COST,
        name="forward_rest",
    )(levels, normed, maps, dep)


def tick_kernel(tick, part, levels_ref, incoming_ref, normed_ref, inverse_ref, maps_ref, *refs):
    _, rows, width = normed_ref.shape
    rank = maps_ref.shape[2] // 2
    if tick == 0:
        stack_ref, sent_ref, grad_latent_ref, active_ref, sem = refs[1:]
    else:
        latent_ref, slope_ref = refs[:2]
        stack_ref, sent_ref, grad_latent_ref, sem = refs[3:]
    keep = pltpu.make_async_copy(
        incoming_ref, stack_ref.at[tick, pl.ds(part * rows, rows)], sem
    )
    keep.start()
    if tick == 0:
        latent, slope, active_ref[...] = forward_values(normed_ref[0], maps_ref[0, :, :rank])
    else:
        latent, slope = latent_ref[0], slope_ref[0]
    grad_act = jnp.dot(incoming_ref[...], maps_ref[0, :, rank:], preferred_element_type=F32)
    grad_latent = (grad_act * slope).astype(BF16)
    grad_latent_ref[...] = grad_latent
    inner = jnp.sum(grad_latent.astype(F32) * latent, axis=-1, keepdims=True) / width
    inverse = inverse_ref[0][:, :1]
    scale = inverse * inner
    run = width // 4
    for start in range(0, width, run):
        at = pl.ds(start, run)
        grad_normed = lax.dot_general(
            grad_latent, maps_ref[0, at, :rank], (((1,), (1,)), ((), ())), preferred_element_type=F32
        )
        sent = incoming_ref[:, at].astype(F32) + (
            inverse * grad_normed - normed_ref[0, :, at].astype(F32) * scale
        )
        sent_ref[:, at] = sent.astype(BF16)
    keep.wait()


def tick_layer(tick, part, levels, incoming, normed, inverse, maps, forward, stack):
    _, rows, width = normed.shape
    rows //= 2
    rank = maps.shape[2] // 2
    first = tick == 0
    narrow = jax.ShapeDtypeStruct((rows, rank), BF16)
    incoming_spec = (
        pl.BlockSpec((rows, width), lambda i, levels: (part, 0)) if first else IN_VMEM
    )
    forward_spec = pl.BlockSpec((1, rows, rank), lambda i, levels: (tick - 1, part, 0))
    return pl.pallas_call(
        functools.partial(tick_kernel, tick, part),
        grid_spec=pltpu.PrefetchScalarGridSpec(
            num_scalar_prefetch=1,
            grid=(1,),
            in_specs=[
                incoming_spec,
                pl.BlockSpec((1, rows, width), lambda i, levels: (tick, part, 0)),
                pl.BlockSpec((1, rows, 128), lambda i, levels: (tick, part, 0)),
                pl.BlockSpec((1, width, 2 * rank), lambda i, levels: (levels[tick], 0, 0)),
            ]
            + [forward_spec] * len(forward)
            + [ANYWHERE],
            out_specs=[ANYWHERE, IN_VMEM, IN_VMEM] + [IN_VMEM] * first,
            scratch_shapes=[pltpu.SemaphoreType.DMA],
        ),
        out_shape=[
            jax.ShapeDtypeStruct(stack.shape, stack.dtype),
            jax.ShapeDtypeStruct((rows, width), BF16),
            narrow,
        ]
        + [narrow] * first,
        input_output_aliases={5 + len(forward): 0},
        compiler_params=LIMIT,
        cost_estimate=COST,
        name="tick_layer",
    )(levels, incoming, normed, inverse, maps, *forward, stack)


def join_kernel(helps_ref, *refs):
    down_ref, up_ref = refs[:2]
    out_ref = refs[-1]
    lanes = down_ref.shape[1]
    out_ref[:, :lanes] = down_ref[...]
    out_ref[:, lanes:] = up_ref[...]
    if len(refs) == 4:
        rank = lanes // 2
        guest_ref = refs[2]

        @pl.when(helps_ref[0] == 1)
        def _():
            out_ref[:, rank:lanes] = guest_ref[:, :rank]
            out_ref[:, lanes + rank :] = guest_ref[:, rank:]


def joined(helps, *parts):
    rows, lanes = parts[0].shape
    run = rows // 4
    return pl.pallas_call(
        join_kernel,
        grid=(rows // run,),
        out_shape=jax.ShapeDtypeStruct((rows, 2 * lanes), parts[0].dtype),
        in_specs=[SCALAR] + [pl.BlockSpec((run, v.shape[1]), lambda i: (i, 0)) for v in parts],
        out_specs=pl.BlockSpec((run, 2 * lanes), lambda i: (i, 0)),
        compiler_params=LIMIT,
        name="join_parts",
    )(helps, *parts)


def sum_kernel(moved_ref, out_ref):
    total = jnp.sum(moved_ref[...].astype(F32), axis=0)
    if total.shape == out_ref.shape:
        out_ref[...] = total
    else:
        rank = total.shape[1] // 2
        zeros = jnp.zeros((total.shape[0], rank), F32)
        out_ref[...] = jnp.concatenate([total[:, :rank], zeros, total[:, rank:], zeros], axis=1)


def summed(moved, lanes):
    return pl.pallas_call(
        sum_kernel,
        out_shape=jax.ShapeDtypeStruct((moved.shape[1], lanes), F32),
        in_specs=[IN_VMEM],
        out_specs=IN_VMEM,
        compiler_params=LIMIT,
        name="sum_partials",
    )(moved)


def finish_kernel(flags_ref, total_ref, guest_ref, low_ref, high_ref, grad_ref, down_ref, up_ref):
    rows, rank = low_ref.shape[0], down_ref.shape[3]
    grad_ref[0, :rows] = low_ref[...]
    grad_ref[0, rows:] = high_ref[...]
    level = flags_ref[0]
    for i, out in enumerate((down_ref, up_ref)):
        at = 2 * i * rank
        out[level, 0] = total_ref[:, at : at + rank]
        own = total_ref[:, at + rank : at + 2 * rank]
        own = jnp.where(flags_ref[1] == 1, jnp.zeros_like(own), own)
        out[1 - level, 0] = own + guest_ref[:, i * rank : (i + 1) * rank]


def finish(flags, total, guest, low, high, share, rank):
    rows, width = low.shape
    made = jax.ShapeDtypeStruct((2, 1, share, rank), F32)
    return pl.pallas_call(
        finish_kernel,
        out_shape=[jax.ShapeDtypeStruct((1, 2 * rows, width), low.dtype), made, made],
        in_specs=[SCALAR] + [IN_VMEM] * 4,
        out_specs=[IN_VMEM] * 3,
        compiler_params=LIMIT,
        name="finish",
    )(flags, total, guest, low, high)


def on_device(saved_inputs, grad_in, adapter_down, adapter_up):
    n_sec = lax.axis_size("section")
    n_dp = lax.axis_size("dp")
    n_z = n_dp // 2
    position = lax.axis_index("section")
    ticks = saved_inputs.shape[0]
    rank, share = adapter_down.shape[2], adapter_down.shape[3]
    width = saved_inputs.shape[3]
    two_layers = position + ticks - 1 >= n_sec
    levels = [1 - (position + tick) // n_sec for tick in range(ticks)]

    def shard_of(down, up, level):
        return jnp.concatenate([down[level].T, up[level].T], axis=1)

    def gather_two(down, up, x):
        shards = jnp.stack([shard_of(down, up, level) for level in range(2)])
        full, made = ring_gather(shards, n_z, norms(x))
        return full.reshape(2, width, 2 * rank), *made

    def gather_one(down, up, x):
        shard = shard_of(down, up, 1)
        copies = jnp.broadcast_to(shard[None], (n_dp,) + shard.shape)
        full = lax.all_to_all(copies, "dp", 0, 0, tiled=True)
        both = unset((2, width, 2 * rank), full.dtype)
        both = lax.dynamic_update_index_in_dim(both, full.reshape(width, 2 * rank), 1, 0)
        return both, *norms(x)

    maps, normed, inverse = lax.cond(
        two_layers, gather_two, gather_one, adapter_down[:, 0], adapter_up[:, 0], saved_inputs
    )

    down_one = [(s, (s - 1) % n_sec) for s in range(n_sec)]
    level_stack = jnp.stack(levels).astype(jnp.int32)
    stack = unset(normed.shape, grad_in.dtype)
    grad_latents, first_actives, moving = [], [], []
    for part in range(2):
        stack, sent, grad_latent, active = tick_layer(
            0, part, level_stack, grad_in[0], normed, inverse, maps, [], stack
        )
        grad_latents.append(grad_latent)
        first_actives.append(active)
        moving.append(lax.ppermute(sent, "section", down_one))
    latents, slopes, actives = forward_rest(level_stack, normed, maps, grad_latent)
    first_active = jnp.concatenate(first_actives)

    def product(wide, narrow):
        contract = (((0,), (0,)), ((), ()))
        return lax.dot_general(wide, narrow, contract, preferred_element_type=F32).astype(BF16)

    guest, helper = n_sec - 1, n_sec - 1 - n_sec // 4
    is_guest, is_helper = position == guest, position == helper
    helps = is_helper.astype(jnp.int32)[None]
    first_latent = jnp.concatenate(grad_latents)

    def guest_parts(lats, acts):
        return joined(helps, product(normed[0], lats), product(grad_in[0], acts))

    def no_parts(lats, acts):
        return unset((width, 2 * rank), BF16)

    parts = lax.cond(is_guest, guest_parts, no_parts, first_latent, first_active)
    guest_in = lax.ppermute(parts, "section", [(guest, helper)])
    for tick in range(1, ticks):
        arrived, moving = moving, []
        for part in range(2):
            stack, sent, grad_latent = tick_layer(
                tick, part, level_stack, arrived[part], normed, inverse, maps, [latents, slopes], stack
            )
            grad_latents.append(grad_latent)
            moving.append(lax.ppermute(sent, "section", down_one))

    normed_all = normed.reshape(-1, width)
    grads_all = stack.reshape(-1, width)
    actives = jnp.concatenate([first_active[None], actives], axis=0)
    grad_latents = jnp.concatenate(grad_latents).reshape(actives.shape)

    same = (level_stack == level_stack[-1])[:, None, None]
    zero = jnp.zeros((), BF16)

    def summed_parts(parts):
        moved = lax.all_to_all(parts.reshape(n_dp, share, -1), "dp", 0, 0, tiled=True)
        return summed(moved, 4 * rank)

    def reduce_one(lats, acts, guest_in):
        def kept(value):
            return jnp.where(same, value, zero).reshape(-1, rank)

        return summed_parts(
            joined(helps, product(normed_all, kept(lats)), product(grads_all, kept(acts)))
        )

    def reduce_two(lats, acts, guest_in):
        def split(value):
            both = [jnp.where(same, value, zero), jnp.where(same, zero, value)]
            return jnp.concatenate(both, axis=2).reshape(-1, 2 * rank)

        return summed_parts(
            joined(
                helps, product(normed_all, split(lats)), product(grads_all, split(acts)), guest_in
            )
        )

    twice = (two_layers & ~is_guest) | is_helper
    total = lax.cond(twice, reduce_two, reduce_one, grad_latents, actives, guest_in)
    extra = jnp.concatenate([total[:, rank : 2 * rank], total[:, 3 * rank :]], axis=1)
    back = lax.ppermute(extra, "section", [(helper, guest)])
    flags = jnp.stack([level_stack[-1], helps[0]])
    grad_out, down_grad, up_grad = finish(flags, total, back, *moving, share, rank)
    return grad_out, jnp.swapaxes(down_grad, 2, 3), jnp.swapaxes(up_grad, 2, 3)


def solution(mesh):
    in_specs = (
        P(None, "section", "dp", None),
        P("section", "dp", None),
        P(None, "section", None, "dp"),
        P(None, "section", None, "dp"),
    )
    out_specs = (
        P("section", "dp", None),
        P(None, "section", None, "dp"),
        P(None, "section", None, "dp"),
    )
    return jax.shard_map(
        on_device, mesh=mesh, in_specs=in_specs, out_specs=out_specs, check_vma=False
    )
```

```python
import functools

import jax
import jax.numpy as jnp
from jax import lax
from jax.experimental import pallas as pl
from jax.experimental.pallas import tpu as pltpu
from jax.sharding import PartitionSpec as P

EPS = 1e-06
F32 = jnp.float32
BF16 = jnp.bfloat16
LIMIT = pltpu.CompilerParams(vmem_limit_bytes=24 * 1024 * 1024)
IN_VMEM = pl.BlockSpec(memory_space=pltpu.VMEM)
ANYWHERE = pl.BlockSpec(memory_space=pl.ANY)
COST = pl.CostEstimate(flops=2**32, bytes_accessed=2**23, transcendentals=0)
SCALAR = pl.BlockSpec(memory_space=pltpu.SMEM)


def dp_pairs(n_z, step, flip):
    return [
        (2 * z + h, 2 * ((z + step) % n_z) + (h ^ flip)) for z in range(n_z) for h in range(2)
    ]


def shifted(value, n_z, step):
    return lax.ppermute(value, "dp", dp_pairs(n_z, step, 0))


def swapped(value, n_z):
    return lax.ppermute(value, "dp", dp_pairs(n_z, 0, 1))


def ring_gather(shard, n_z):
    index = lax.axis_index("dp")
    z, h = index // 2, index % 2
    half = n_z // 2
    full = unset((2, n_z, 2) + shard.shape[1:], shard.dtype)

    def placed(full, piece, offset, side):
        at = (0, (z + offset) % n_z, side, 0, 0)
        return lax.dynamic_update_slice(full, piece[:, None, None], at)

    other = swapped(shard, n_z)
    far = shifted(shard, n_z, half)
    right, left = shifted(shard, n_z, 1), shifted(shard, n_z, -1)
    full = placed(full, shard, 0, h)
    full = placed(full, right, -1, h)
    full = placed(full, left, 1, h)
    full = placed(full, other, 0, 1 - h)
    full = placed(full, far, half, h)
    right, left = jnp.stack([right, other]), jnp.stack([left, other])
    for step in range(2, half):
        right, left = shifted(right, n_z, 1), shifted(left, n_z, -1)
        if step == 2:
            far = swapped(far, n_z)
        for value, sign in ((right, -1), (left, 1)):
            full = placed(full, value[0], sign * step, h)
            full = placed(full, value[1], sign * (step - 1), 1 - h)
    full = placed(full, far, half, 1 - h)
    right, left = shifted(right[1], n_z, 1), shifted(left[1], n_z, -1)
    full = placed(full, right, 1 - half, 1 - h)
    return placed(full, left, half - 1, 1 - h)


def empty_kernel(out_ref):
    pass


def unset(shape, dtype):
    return pl.pallas_call(
        empty_kernel,
        out_shape=jax.ShapeDtypeStruct(shape, dtype),
        out_specs=ANYWHERE,
        name="unset",
    )()


def norm_kernel(x_ref, normed_ref, inverse_ref):
    x = x_ref[0, 0].astype(F32)
    inverse = lax.rsqrt(jnp.mean(x * x, axis=-1, keepdims=True) + EPS)
    normed_ref[0] = (x * inverse).astype(BF16)
    inverse_ref[0] = jnp.broadcast_to(inverse, inverse_ref.shape[1:])


def norms(saved_inputs):
    ticks, _, rows, width = saved_inputs.shape
    return pl.pallas_call(
        norm_kernel,
        grid=(ticks,),
        out_shape=[
            jax.ShapeDtypeStruct((ticks, rows, width), BF16),
            jax.ShapeDtypeStruct((ticks, rows, 128), F32),
        ],
        in_specs=[pl.BlockSpec((1, 1, rows, width), lambda i: (i, 0, 0, 0))],
        out_specs=[
            pl.BlockSpec((1, rows, width), lambda i: (i, 0, 0)),
            pl.BlockSpec((1, rows, 128), lambda i: (i, 0, 0)),
        ],
        compiler_params=LIMIT,
        cost_estimate=COST,
        name="norms",
    )(saved_inputs)


def forward_values(normed, down):
    latent = jnp.dot(normed, down, preferred_element_type=F32)
    gate = jax.nn.sigmoid(latent)
    active = (latent * gate).astype(BF16)
    return latent, gate * (1.0 + latent * (1.0 - gate)), active


def forward_kernel(levels_ref, normed_ref, maps_ref, dep_ref, latent_ref, slope_ref, active_ref):
    rank = latent_ref.shape[2]
    latent_ref[0], slope_ref[0], active_ref[0] = forward_values(
        normed_ref[0], maps_ref[0, :, :rank]
    )


def forward_rest(levels, normed, maps, dep):
    ticks, rows, width = normed.shape
    rank = maps.shape[2] // 2
    rest = ticks - 1

    def made(dtype):
        return jax.ShapeDtypeStruct((rest, rows, rank), dtype)

    return pl.pallas_call(
        forward_kernel,
        grid_spec=pltpu.PrefetchScalarGridSpec(
            num_scalar_prefetch=1,
            grid=(rest,),
            in_specs=[
                pl.BlockSpec((1, rows, width), lambda i, levels: (i + 1, 0, 0)),
                pl.BlockSpec((1, width, 2 * rank), lambda i, levels: (levels[i + 1], 0, 0)),
                ANYWHERE,
            ],
            out_specs=[pl.BlockSpec((1, rows, rank), lambda i, levels: (i, 0, 0))] * 3,
        ),
        out_shape=[made(F32), made(F32), made(BF16)],
        compiler_params=LIMIT,
        cost_estimate=COST,
        name="forward_rest",
    )(levels, normed, maps, dep)


def tick_kernel(tick, part, levels_ref, incoming_ref, normed_ref, inverse_ref, maps_ref, *refs):
    _, rows, width = normed_ref.shape
    rank = maps_ref.shape[2] // 2
    if tick == 0:
        stack_ref, sent_ref, grad_latent_ref, active_ref, sem = refs[1:]
    else:
        latent_ref, slope_ref = refs[:2]
        stack_ref, sent_ref, grad_latent_ref, sem = refs[3:]
    keep = pltpu.make_async_copy(
        incoming_ref, stack_ref.at[tick, pl.ds(part * rows, rows)], sem
    )
    keep.start()
    if tick == 0:
        latent, slope, active_ref[...] = forward_values(normed_ref[0], maps_ref[0, :, :rank])
    else:
        latent, slope = latent_ref[0], slope_ref[0]
    grad_act = jnp.dot(incoming_ref[...], maps_ref[0, :, rank:], preferred_element_type=F32)
    grad_latent = (grad_act * slope).astype(BF16)
    grad_latent_ref[...] = grad_latent
    inner = jnp.sum(grad_latent.astype(F32) * latent, axis=-1, keepdims=True) / width
    inverse = inverse_ref[0][:, :1]
    scale = inverse * inner
    run = width // 4
    for start in range(0, width, run):
        at = pl.ds(start, run)
        grad_normed = lax.dot_general(
            grad_latent, maps_ref[0, at, :rank], (((1,), (1,)), ((), ())), preferred_element_type=F32
        )
        sent = incoming_ref[:, at].astype(F32) + (
            inverse * grad_normed - normed_ref[0, :, at].astype(F32) * scale
        )
        sent_ref[:, at] = sent.astype(BF16)
    keep.wait()


def tick_layer(tick, part, levels, incoming, normed, inverse, maps, forward, stack):
    _, rows, width = normed.shape
    rows //= 2
    rank = maps.shape[2] // 2
    first = tick == 0
    narrow = jax.ShapeDtypeStruct((rows, rank), BF16)
    incoming_spec = (
        pl.BlockSpec((rows, width), lambda i, levels: (part, 0)) if first else IN_VMEM
    )
    forward_spec = pl.BlockSpec((1, rows, rank), lambda i, levels: (tick - 1, part, 0))
    return pl.pallas_call(
        functools.partial(tick_kernel, tick, part),
        grid_spec=pltpu.PrefetchScalarGridSpec(
            num_scalar_prefetch=1,
            grid=(1,),
            in_specs=[
                incoming_spec,
                pl.BlockSpec((1, rows, width), lambda i, levels: (tick, part, 0)),
                pl.BlockSpec((1, rows, 128), lambda i, levels: (tick, part, 0)),
                pl.BlockSpec((1, width, 2 * rank), lambda i, levels: (levels[tick], 0, 0)),
            ]
            + [forward_spec] * len(forward)
            + [ANYWHERE],
            out_specs=[ANYWHERE, IN_VMEM, IN_VMEM] + [IN_VMEM] * first,
            scratch_shapes=[pltpu.SemaphoreType.DMA],
        ),
        out_shape=[
            jax.ShapeDtypeStruct(stack.shape, stack.dtype),
            jax.ShapeDtypeStruct((rows, width), BF16),
            narrow,
        ]
        + [narrow] * first,
        input_output_aliases={5 + len(forward): 0},
        compiler_params=LIMIT,
        cost_estimate=COST,
        name="tick_layer",
    )(levels, incoming, normed, inverse, maps, *forward, stack)


def beside_kernel(left_ref, right_ref, out_ref):
    lanes = left_ref.shape[1]
    out_ref[:, :lanes] = left_ref[...]
    out_ref[:, lanes:] = right_ref[...]


def beside(left, right):
    rows, lanes = left.shape
    run = rows // 4
    block = pl.BlockSpec((run, lanes), lambda i: (i, 0))
    return pl.pallas_call(
        beside_kernel,
        grid=(rows // run,),
        out_shape=jax.ShapeDtypeStruct((rows, 2 * lanes), left.dtype),
        in_specs=[block, block],
        out_specs=pl.BlockSpec((run, 2 * lanes), lambda i: (i, 0)),
        compiler_params=LIMIT,
        name="side_by_side",
    )(left, right)


def sum_kernel(moved_ref, out_ref):
    total = jnp.sum(moved_ref[...].astype(F32), axis=0)
    if total.shape == out_ref.shape:
        out_ref[...] = total
    else:
        rank = total.shape[1] // 2
        zeros = jnp.zeros((total.shape[0], rank), F32)
        out_ref[...] = jnp.concatenate([total[:, :rank], zeros, total[:, rank:], zeros], axis=1)


def summed(moved, lanes):
    return pl.pallas_call(
        sum_kernel,
        out_shape=jax.ShapeDtypeStruct((moved.shape[1], lanes), F32),
        in_specs=[IN_VMEM],
        out_specs=IN_VMEM,
        compiler_params=LIMIT,
        name="sum_partials",
    )(moved)


def finish_kernel(total_ref, low_ref, high_ref, grad_ref, down_ref, up_ref):
    rows, rank = low_ref.shape[0], down_ref.shape[3]
    grad_ref[0, :rows] = low_ref[...]
    grad_ref[0, rows:] = high_ref[...]
    for i, out in enumerate((down_ref, up_ref)):
        for j, level in enumerate((1, 0)):
            at = (2 * i + j) * rank
            out[level, 0] = total_ref[:, at : at + rank]


def finish(total, low, high, share, rank):
    rows, width = low.shape
    made = jax.ShapeDtypeStruct((2, 1, share, rank), F32)
    return pl.pallas_call(
        finish_kernel,
        out_shape=[jax.ShapeDtypeStruct((1, 2 * rows, width), low.dtype), made, made],
        in_specs=[IN_VMEM] * 3,
        out_specs=[IN_VMEM] * 3,
        compiler_params=LIMIT,
        name="finish",
    )(total, low, high)


def on_device(saved_inputs, grad_in, adapter_down, adapter_up):
    n_sec = lax.axis_size("section")
    n_dp = lax.axis_size("dp")
    n_z = n_dp // 2
    position = lax.axis_index("section")
    ticks = saved_inputs.shape[0]
    rank, share = adapter_down.shape[2], adapter_down.shape[3]
    width = saved_inputs.shape[3]
    two_layers = position + ticks - 1 >= n_sec
    levels = [1 - (position + tick) // n_sec for tick in range(ticks)]

    def shard_of(down, up, level):
        return jnp.concatenate([down[level].T, up[level].T], axis=1)

    def gather_two(down, up, x):
        shards = jnp.stack([shard_of(down, up, level) for level in range(2)])
        full = ring_gather(shards, n_z)
        return full.reshape(2, width, 2 * rank), *norms(x)

    def gather_one(down, up, x):
        shard = shard_of(down, up, 1)
        copies = jnp.broadcast_to(shard[None], (n_dp,) + shard.shape)
        full = lax.all_to_all(copies, "dp", 0, 0, tiled=True)
        both = unset((2, width, 2 * rank), full.dtype)
        both = lax.dynamic_update_index_in_dim(both, full.reshape(width, 2 * rank), 1, 0)
        return both, *norms(x)

    maps, normed, inverse = lax.cond(
        two_layers, gather_two, gather_one, adapter_down[:, 0], adapter_up[:, 0], saved_inputs
    )

    down_one = [(s, (s - 1) % n_sec) for s in range(n_sec)]
    level_stack = jnp.stack(levels).astype(jnp.int32)
    stack = unset(normed.shape, grad_in.dtype)
    grad_latents, first_actives, moving = [], [], []
    for part in range(2):
        stack, sent, grad_latent, active = tick_layer(
            0, part, level_stack, grad_in[0], normed, inverse, maps, [], stack
        )
        grad_latents.append(grad_latent)
        first_actives.append(active)
        moving.append(lax.ppermute(sent, "section", down_one))
    latents, slopes, actives = forward_rest(level_stack, normed, maps, grad_latent)
    for tick in range(1, ticks):
        arrived, moving = moving, []
        for part in range(2):
            stack, sent, grad_latent = tick_layer(
                tick, part, level_stack, arrived[part], normed, inverse, maps, [latents, slopes], stack
            )
            grad_latents.append(grad_latent)
            moving.append(lax.ppermute(sent, "section", down_one))

    normed_all = normed.reshape(-1, width)
    grads_all = stack.reshape(-1, width)
    actives = jnp.concatenate([jnp.concatenate(first_actives)[None], actives], axis=0)

    def products(lats, acts):
        contract = (((0,), (0,)), ((), ()))
        down = lax.dot_general(normed_all, lats, contract, preferred_element_type=F32)
        up = lax.dot_general(grads_all, acts, contract, preferred_element_type=F32)
        both = beside(down.astype(BF16), up.astype(BF16))
        moved = lax.all_to_all(both.reshape(n_dp, share, -1), "dp", 0, 0, tiled=True)
        return summed(moved, 4 * rank)

    def reduce_one(lats, acts):
        return products(lats.reshape(-1, rank), acts.reshape(-1, rank))

    def reduce_two(lats, acts):
        level = level_stack[:, None, None]
        zero = jnp.zeros((), BF16)

        def split(value):
            both = [jnp.where(level == 1, value, zero), jnp.where(level == 0, value, zero)]
            return jnp.concatenate(both, axis=2).reshape(-1, 2 * rank)

        return products(split(lats), split(acts))

    total = lax.cond(two_layers, reduce_two, reduce_one, jnp.concatenate(grad_latents).reshape(actives.shape), actives)
    grad_out, down_grad, up_grad = finish(total, *moving, share, rank)
    return grad_out, jnp.swapaxes(down_grad, 2, 3), jnp.swapaxes(up_grad, 2, 3)


def solution(mesh):
    in_specs = (
        P(None, "section", "dp", None),
        P("section", "dp", None),
        P(None, "section", None, "dp"),
        P(None, "section", None, "dp"),
    )
    out_specs = (
        P("section", "dp", None),
        P(None, "section", None, "dp"),
        P(None, "section", None, "dp"),
    )
    return jax.shard_map(
        on_device, mesh=mesh, in_specs=in_specs, out_specs=out_specs, check_vma=False
    )
```

```python
import functools

import jax
import jax.numpy as jnp
from jax import lax
from jax.experimental import pallas as pl
from jax.experimental.pallas import tpu as pltpu
from jax.sharding import PartitionSpec as P

EPS = 1e-06
F32 = jnp.float32
BF16 = jnp.bfloat16
LIMIT = pltpu.CompilerParams(vmem_limit_bytes=24 * 1024 * 1024)
IN_VMEM = pl.BlockSpec(memory_space=pltpu.VMEM)
ANYWHERE = pl.BlockSpec(memory_space=pl.ANY)
COST = pl.CostEstimate(flops=2**32, bytes_accessed=2**23, transcendentals=0)
SCALAR = pl.BlockSpec(memory_space=pltpu.SMEM)


def dp_pairs(n_z, step, flip):
    return [
        (2 * z + h, 2 * ((z + step) % n_z) + (h ^ flip)) for z in range(n_z) for h in range(2)
    ]


def shifted(value, n_z, step):
    return lax.ppermute(value, "dp", dp_pairs(n_z, step, 0))


def swapped(value, n_z):
    return lax.ppermute(value, "dp", dp_pairs(n_z, 0, 1))


def ring_gather(shard, n_z):
    index = lax.axis_index("dp")
    z, h = index // 2, index % 2
    other = swapped(shard, n_z)
    pair = jnp.stack([jnp.where(h == 0, shard, other), jnp.where(h == 0, other, shard)], axis=1)
    half = n_z // 2
    full = unset((2, n_z) + pair.shape[1:], pair.dtype)

    def placed(full, piece, offset):
        return lax.dynamic_update_slice(full, piece[:, None], (0, (z + offset) % n_z, 0, 0, 0))

    full = placed(full, pair, 0)
    right, left = pair, pair
    for step in range(1, half):
        right, left = shifted(right, n_z, 1), shifted(left, n_z, -1)
        full = placed(full, right, -step)
        full = placed(full, left, step)
    right, left = shifted(right[:, :1], n_z, 1), shifted(left[:, 1:], n_z, -1)
    return placed(full, jnp.concatenate([right, left], axis=1), half)


def empty_kernel(out_ref):
    pass


def unset(shape, dtype):
    return pl.pallas_call(
        empty_kernel,
        out_shape=jax.ShapeDtypeStruct(shape, dtype),
        out_specs=ANYWHERE,
        name="unset",
    )()


def norm_kernel(x_ref, normed_ref, inverse_ref):
    x = x_ref[0, 0].astype(F32)
    inverse = lax.rsqrt(jnp.mean(x * x, axis=-1, keepdims=True) + EPS)
    normed_ref[0] = (x * inverse).astype(BF16)
    inverse_ref[0] = jnp.broadcast_to(inverse, inverse_ref.shape[1:])


def norms(saved_inputs):
    ticks, _, rows, width = saved_inputs.shape
    return pl.pallas_call(
        norm_kernel,
        grid=(ticks,),
        out_shape=[
            jax.ShapeDtypeStruct((ticks, rows, width), BF16),
            jax.ShapeDtypeStruct((ticks, rows, 128), F32),
        ],
        in_specs=[pl.BlockSpec((1, 1, rows, width), lambda i: (i, 0, 0, 0))],
        out_specs=[
            pl.BlockSpec((1, rows, width), lambda i: (i, 0, 0)),
            pl.BlockSpec((1, rows, 128), lambda i: (i, 0, 0)),
        ],
        compiler_params=LIMIT,
        cost_estimate=COST,
        name="norms",
    )(saved_inputs)


def forward_values(normed, down):
    latent = jnp.dot(normed, down, preferred_element_type=F32)
    gate = jax.nn.sigmoid(latent)
    active = (latent * gate).astype(BF16)
    return latent, gate * (1.0 + latent * (1.0 - gate)), active


def forward_kernel(levels_ref, normed_ref, maps_ref, dep_ref, latent_ref, slope_ref, active_ref):
    rank = latent_ref.shape[2]
    latent_ref[0], slope_ref[0], active_ref[0] = forward_values(
        normed_ref[0], maps_ref[0, :, :rank]
    )


def forward_rest(levels, normed, maps, dep):
    ticks, rows, width = normed.shape
    rank = maps.shape[2] // 2
    rest = ticks - 1

    def made(dtype):
        return jax.ShapeDtypeStruct((rest, rows, rank), dtype)

    return pl.pallas_call(
        forward_kernel,
        grid_spec=pltpu.PrefetchScalarGridSpec(
            num_scalar_prefetch=1,
            grid=(rest,),
            in_specs=[
                pl.BlockSpec((1, rows, width), lambda i, levels: (i + 1, 0, 0)),
                pl.BlockSpec((1, width, 2 * rank), lambda i, levels: (levels[i + 1], 0, 0)),
                ANYWHERE,
            ],
            out_specs=[pl.BlockSpec((1, rows, rank), lambda i, levels: (i, 0, 0))] * 3,
        ),
        out_shape=[made(F32), made(F32), made(BF16)],
        compiler_params=LIMIT,
        cost_estimate=COST,
        name="forward_rest",
    )(levels, normed, maps, dep)


def tick_kernel(tick, part, levels_ref, incoming_ref, normed_ref, inverse_ref, maps_ref, *refs):
    _, rows, width = normed_ref.shape
    rank = maps_ref.shape[2] // 2
    if tick == 0:
        stack_ref, sent_ref, grad_latent_ref, active_ref, sem = refs[1:]
    else:
        latent_ref, slope_ref = refs[:2]
        stack_ref, sent_ref, grad_latent_ref, sem = refs[-4:]
    base = sent_ref.shape[0] - rows
    if base:
        sent_ref[:base] = refs[2][...]
    keep = pltpu.make_async_copy(
        incoming_ref, stack_ref.at[tick, pl.ds(part * rows, rows)], sem
    )
    keep.start()
    if tick == 0:
        latent, slope, active_ref[...] = forward_values(normed_ref[0], maps_ref[0, :, :rank])
    else:
        latent, slope = latent_ref[0], slope_ref[0]
    grad_act = jnp.dot(incoming_ref[...], maps_ref[0, :, rank:], preferred_element_type=F32)
    grad_latent = (grad_act * slope).astype(BF16)
    grad_latent_ref[...] = grad_latent
    inner = jnp.sum(grad_latent.astype(F32) * latent, axis=-1, keepdims=True) / width
    inverse = inverse_ref[0][:, :1]
    scale = inverse * inner
    run = width // 4
    for start in range(0, width, run):
        at = pl.ds(start, run)
        grad_normed = lax.dot_general(
            grad_latent, maps_ref[0, at, :rank], (((1,), (1,)), ((), ())), preferred_element_type=F32
        )
        sent = incoming_ref[:, at].astype(F32) + (
            inverse * grad_normed - normed_ref[0, :, at].astype(F32) * scale
        )
        sent_ref[base:, at] = sent.astype(BF16)
    keep.wait()


def tick_layer(tick, part, levels, incoming, normed, inverse, maps, forward, stack, before=()):
    _, rows, width = normed.shape
    rows //= 2
    rank = maps.shape[2] // 2
    first = tick == 0
    narrow = jax.ShapeDtypeStruct((rows, rank), BF16)
    incoming_spec = (
        pl.BlockSpec((rows, width), lambda i, levels: (part, 0)) if first else IN_VMEM
    )
    forward_spec = pl.BlockSpec((1, rows, rank), lambda i, levels: (tick - 1, part, 0))
    return pl.pallas_call(
        functools.partial(tick_kernel, tick, part),
        grid_spec=pltpu.PrefetchScalarGridSpec(
            num_scalar_prefetch=1,
            grid=(1,),
            in_specs=[
                incoming_spec,
                pl.BlockSpec((1, rows, width), lambda i, levels: (tick, part, 0)),
                pl.BlockSpec((1, rows, 128), lambda i, levels: (tick, part, 0)),
                pl.BlockSpec((1, width, 2 * rank), lambda i, levels: (levels[tick], 0, 0)),
            ]
            + [forward_spec] * len(forward)
            + [IN_VMEM] * len(before)
            + [ANYWHERE],
            out_specs=[ANYWHERE, IN_VMEM, IN_VMEM] + [IN_VMEM] * first,
            scratch_shapes=[pltpu.SemaphoreType.DMA],
        ),
        out_shape=[
            jax.ShapeDtypeStruct(stack.shape, stack.dtype),
            jax.ShapeDtypeStruct((rows * (1 + len(before)), width), BF16),
            narrow,
        ]
        + [narrow] * first,
        input_output_aliases={5 + len(forward) + len(before): 0},
        compiler_params=LIMIT,
        cost_estimate=COST,
        name="tick_layer",
    )(levels, incoming, normed, inverse, maps, *forward, *before, stack)


def products_kernel(normed_ref, grads_ref, lats_ref, acts_ref, out_ref):
    lanes = lats_ref.shape[1]
    contract = (((0,), (0,)), ((), ()))
    for i, (wide_ref, narrow_ref) in enumerate(((normed_ref, lats_ref), (grads_ref, acts_ref))):
        wide = wide_ref[...].reshape(-1, wide_ref.shape[2])
        part = lax.dot_general(wide, narrow_ref[...], contract, preferred_element_type=F32)
        out_ref[:, i * lanes : (i + 1) * lanes] = part.astype(BF16)


def kernel_products(normed, grads, lats, acts):
    ticks, rows, width = normed.shape
    lanes = lats.shape[1]
    run = width // 4
    by_run = pl.BlockSpec((ticks, rows, run), lambda i: (0, 0, i))
    whole = pl.BlockSpec((ticks * rows, lanes), lambda i: (0, 0))
    return pl.pallas_call(
        products_kernel,
        grid=(width // run,),
        out_shape=jax.ShapeDtypeStruct((width, 2 * lanes), BF16),
        in_specs=[by_run, by_run, whole, whole],
        out_specs=pl.BlockSpec((run, 2 * lanes), lambda i: (i, 0)),
        compiler_params=LIMIT,
        cost_estimate=COST,
        name="weight_products",
    )(normed, grads, lats, acts)


def beside_kernel(left_ref, right_ref, out_ref):
    lanes = left_ref.shape[1]
    out_ref[:, :lanes] = left_ref[...]
    out_ref[:, lanes:] = right_ref[...]


def beside(left, right):
    rows, lanes = left.shape
    run = rows // 4
    block = pl.BlockSpec((run, lanes), lambda i: (i, 0))
    return pl.pallas_call(
        beside_kernel,
        grid=(rows // run,),
        out_shape=jax.ShapeDtypeStruct((rows, 2 * lanes), left.dtype),
        in_specs=[block, block],
        out_specs=pl.BlockSpec((run, 2 * lanes), lambda i: (i, 0)),
        compiler_params=LIMIT,
        name="side_by_side",
    )(left, right)


def sum_kernel(moved_ref, out_ref):
    total = jnp.sum(moved_ref[...].astype(F32), axis=0)
    if total.shape == out_ref.shape:
        out_ref[...] = total
    else:
        rank = total.shape[1] // 2
        zeros = jnp.zeros((total.shape[0], rank), F32)
        out_ref[...] = jnp.concatenate([total[:, :rank], zeros, total[:, rank:], zeros], axis=1)


def summed(moved, lanes):
    return pl.pallas_call(
        sum_kernel,
        out_shape=jax.ShapeDtypeStruct((moved.shape[1], lanes), F32),
        in_specs=[IN_VMEM],
        out_specs=IN_VMEM,
        compiler_params=LIMIT,
        name="sum_partials",
    )(moved)


def finish_kernel(total_ref, down_ref, up_ref):
    rank = down_ref.shape[3]
    for i, out in enumerate((down_ref, up_ref)):
        for j, level in enumerate((1, 0)):
            at = (2 * i + j) * rank
            out[level, 0] = total_ref[:, at : at + rank]


def finish(total, share, rank):
    made = jax.ShapeDtypeStruct((2, 1, share, rank), F32)
    return pl.pallas_call(
        finish_kernel,
        out_shape=[made, made],
        in_specs=[IN_VMEM],
        out_specs=[IN_VMEM] * 2,
        compiler_params=LIMIT,
        name="finish",
    )(total)


def on_device(saved_inputs, grad_in, adapter_down, adapter_up):
    n_sec = lax.axis_size("section")
    n_dp = lax.axis_size("dp")
    n_z = n_dp // 2
    position = lax.axis_index("section")
    ticks = saved_inputs.shape[0]
    rank, share = adapter_down.shape[2], adapter_down.shape[3]
    width = saved_inputs.shape[3]
    two_layers = position + ticks - 1 >= n_sec
    levels = [1 - (position + tick) // n_sec for tick in range(ticks)]

    def shard_of(down, up, level):
        return jnp.concatenate([down[level].T, up[level].T], axis=1)

    def gather_two(down, up, x):
        shards = jnp.stack([shard_of(down, up, level) for level in range(2)])
        full = ring_gather(shards, n_z)
        return full.reshape(2, width, 2 * rank), *norms(x)

    def gather_one(down, up, x):
        shard = shard_of(down, up, 1)
        copies = jnp.broadcast_to(shard[None], (n_dp,) + shard.shape)
        full = lax.all_to_all(copies, "dp", 0, 0, tiled=True)
        both = unset((2, width, 2 * rank), full.dtype)
        both = lax.dynamic_update_index_in_dim(both, full.reshape(width, 2 * rank), 1, 0)
        return both, *norms(x)

    maps, normed, inverse = lax.cond(
        two_layers, gather_two, gather_one, adapter_down[:, 0], adapter_up[:, 0], saved_inputs
    )

    down_one = [(s, (s - 1) % n_sec) for s in range(n_sec)]
    level_stack = jnp.stack(levels).astype(jnp.int32)
    stack = unset(normed.shape, grad_in.dtype)
    grad_latents, first_actives, moving = [], [], []
    for part in range(2):
        stack, sent, grad_latent, active = tick_layer(
            0, part, level_stack, grad_in[0], normed, inverse, maps, [], stack
        )
        grad_latents.append(grad_latent)
        first_actives.append(active)
        moving.append(lax.ppermute(sent, "section", down_one))
    latents, slopes, actives = forward_rest(level_stack, normed, maps, grad_latent)
    for tick in range(1, ticks):
        arrived, moving = moving, []
        before = []
        for part in range(2):
            stack, sent, grad_latent = tick_layer(
                tick,
                part,
                level_stack,
                arrived[part],
                normed,
                inverse,
                maps,
                [latents, slopes],
                stack,
                before,
            )
            grad_latents.append(grad_latent)
            if tick == ticks - 1 and part == 0:
                before = [sent]
            else:
                moving.append(lax.ppermute(sent, "section", down_one))

    normed_all = normed.reshape(-1, width)
    grads_all = stack.reshape(-1, width)
    actives = jnp.concatenate([jnp.concatenate(first_actives)[None], actives], axis=0)

    def summed_parts(parts):
        moved = lax.all_to_all(parts.reshape(n_dp, share, -1), "dp", 0, 0, tiled=True)
        return summed(moved, 4 * rank)

    def products(lats, acts):
        contract = (((0,), (0,)), ((), ()))
        down = lax.dot_general(normed_all, lats, contract, preferred_element_type=F32)
        up = lax.dot_general(grads_all, acts, contract, preferred_element_type=F32)
        return beside(down.astype(BF16), up.astype(BF16))

    def reduce_one(lats, acts):
        return summed_parts(products(lats.reshape(-1, rank), acts.reshape(-1, rank)))

    def reduce_two(lats, acts):
        level = level_stack[:, None, None]
        zero = jnp.zeros((), BF16)

        def split(value):
            both = [jnp.where(level == 1, value, zero), jnp.where(level == 0, value, zero)]
            return jnp.concatenate(both, axis=2).reshape(-1, 2 * rank)

        return summed_parts(kernel_products(normed, stack, split(lats), split(acts)))

    total = lax.cond(two_layers, reduce_two, reduce_one, jnp.concatenate(grad_latents).reshape(actives.shape), actives)
    down_grad, up_grad = finish(total, share, rank)
    return moving[0][None], jnp.swapaxes(down_grad, 2, 3), jnp.swapaxes(up_grad, 2, 3)


def solution(mesh):
    in_specs = (
        P(None, "section", "dp", None),
        P("section", "dp", None),
        P(None, "section", None, "dp"),
        P(None, "section", None, "dp"),
    )
    out_specs = (
        P("section", "dp", None),
        P(None, "section", None, "dp"),
        P(None, "section", None, "dp"),
    )
    return jax.shard_map(
        on_device, mesh=mesh, in_specs=in_specs, out_specs=out_specs, check_vma=False
    )
```

```python
import functools

import jax
import jax.numpy as jnp
from jax import lax
from jax.experimental import pallas as pl
from jax.experimental.pallas import tpu as pltpu
from jax.sharding import PartitionSpec as P

EPS = 1e-06
F32 = jnp.float32
BF16 = jnp.bfloat16
LIMIT = pltpu.CompilerParams(vmem_limit_bytes=24 * 1024 * 1024)
IN_VMEM = pl.BlockSpec(memory_space=pltpu.VMEM)
ANYWHERE = pl.BlockSpec(memory_space=pl.ANY)
COST = pl.CostEstimate(flops=2**32, bytes_accessed=2**23, transcendentals=0)
SCALAR = pl.BlockSpec(memory_space=pltpu.SMEM)


def dp_pairs(n_z, step, flip):
    return [
        (2 * z + h, 2 * ((z + step) % n_z) + (h ^ flip)) for z in range(n_z) for h in range(2)
    ]


def shifted(value, n_z, step):
    return lax.ppermute(value, "dp", dp_pairs(n_z, step, 0))


def swapped(value, n_z):
    return lax.ppermute(value, "dp", dp_pairs(n_z, 0, 1))


def ring_gather(shard, n_z):
    index = lax.axis_index("dp")
    z, h = index // 2, index % 2
    other = swapped(shard, n_z)
    pair = jnp.stack([jnp.where(h == 0, shard, other), jnp.where(h == 0, other, shard)], axis=1)
    half = n_z // 2
    full = unset((2, n_z) + pair.shape[1:], pair.dtype)

    def placed(full, piece, offset):
        return lax.dynamic_update_slice(full, piece[:, None], (0, (z + offset) % n_z, 0, 0, 0))

    full = placed(full, pair, 0)
    right, left = pair, pair
    for step in range(1, half):
        right, left = shifted(right, n_z, 1), shifted(left, n_z, -1)
        full = placed(full, right, -step)
        if step < half - 1:
            full = placed(full, left, step)
    full = placed(full, shifted(right, n_z, 1), -half)
    return placed(full, left, half - 1)


def empty_kernel(out_ref):
    pass


def unset(shape, dtype):
    return pl.pallas_call(
        empty_kernel,
        out_shape=jax.ShapeDtypeStruct(shape, dtype),
        out_specs=ANYWHERE,
        name="unset",
    )()


def norm_kernel(x_ref, normed_ref, inverse_ref):
    x = x_ref[0, 0].astype(F32)
    inverse = lax.rsqrt(jnp.mean(x * x, axis=-1, keepdims=True) + EPS)
    normed_ref[0] = (x * inverse).astype(BF16)
    inverse_ref[0] = jnp.broadcast_to(inverse, inverse_ref.shape[1:])


def norms(saved_inputs):
    ticks, _, rows, width = saved_inputs.shape
    return pl.pallas_call(
        norm_kernel,
        grid=(ticks,),
        out_shape=[
            jax.ShapeDtypeStruct((ticks, rows, width), BF16),
            jax.ShapeDtypeStruct((ticks, rows, 128), F32),
        ],
        in_specs=[pl.BlockSpec((1, 1, rows, width), lambda i: (i, 0, 0, 0))],
        out_specs=[
            pl.BlockSpec((1, rows, width), lambda i: (i, 0, 0)),
            pl.BlockSpec((1, rows, 128), lambda i: (i, 0, 0)),
        ],
        compiler_params=LIMIT,
        cost_estimate=COST,
        name="norms",
    )(saved_inputs)


def forward_values(normed, down):
    latent = jnp.dot(normed, down, preferred_element_type=F32)
    gate = jax.nn.sigmoid(latent)
    active = (latent * gate).astype(BF16)
    return latent, gate * (1.0 + latent * (1.0 - gate)), active


def forward_kernel(levels_ref, normed_ref, maps_ref, dep_ref, latent_ref, slope_ref, active_ref):
    rank = latent_ref.shape[2]
    latent_ref[0], slope_ref[0], active_ref[0] = forward_values(
        normed_ref[0], maps_ref[0, :, :rank]
    )


def forward_rest(levels, normed, maps, dep):
    ticks, rows, width = normed.shape
    rank = maps.shape[2] // 2
    rest = ticks - 1

    def made(dtype):
        return jax.ShapeDtypeStruct((rest, rows, rank), dtype)

    return pl.pallas_call(
        forward_kernel,
        grid_spec=pltpu.PrefetchScalarGridSpec(
            num_scalar_prefetch=1,
            grid=(rest,),
            in_specs=[
                pl.BlockSpec((1, rows, width), lambda i, levels: (i + 1, 0, 0)),
                pl.BlockSpec((1, width, 2 * rank), lambda i, levels: (levels[i + 1], 0, 0)),
                ANYWHERE,
            ],
            out_specs=[pl.BlockSpec((1, rows, rank), lambda i, levels: (i, 0, 0))] * 3,
        ),
        out_shape=[made(F32), made(F32), made(BF16)],
        compiler_params=LIMIT,
        cost_estimate=COST,
        name="forward_rest",
    )(levels, normed, maps, dep)


def tick_kernel(tick, part, levels_ref, incoming_ref, normed_ref, inverse_ref, maps_ref, *refs):
    _, rows, width = normed_ref.shape
    rank = maps_ref.shape[2] // 2
    if tick == 0:
        stack_ref, sent_ref, grad_latent_ref, active_ref, sem = refs[1:]
    else:
        latent_ref, slope_ref = refs[:2]
        stack_ref, sent_ref, grad_latent_ref, sem = refs[3:]
    keep = pltpu.make_async_copy(
        incoming_ref, stack_ref.at[tick, pl.ds(part * rows, rows)], sem
    )
    keep.start()
    if tick == 0:
        latent, slope, active_ref[...] = forward_values(normed_ref[0], maps_ref[0, :, :rank])
    else:
        latent, slope = latent_ref[0], slope_ref[0]
    grad_act = jnp.dot(incoming_ref[...], maps_ref[0, :, rank:], preferred_element_type=F32)
    grad_latent = (grad_act * slope).astype(BF16)
    grad_latent_ref[...] = grad_latent
    inner = jnp.sum(grad_latent.astype(F32) * latent, axis=-1, keepdims=True) / width
    inverse = inverse_ref[0][:, :1]
    scale = inverse * inner
    run = width // 4
    for start in range(0, width, run):
        at = pl.ds(start, run)
        grad_normed = lax.dot_general(
            grad_latent, maps_ref[0, at, :rank], (((1,), (1,)), ((), ())), preferred_element_type=F32
        )
        sent = incoming_ref[:, at].astype(F32) + (
            inverse * grad_normed - normed_ref[0, :, at].astype(F32) * scale
        )
        sent_ref[:, at] = sent.astype(BF16)
    keep.wait()


def tick_layer(tick, part, levels, incoming, normed, inverse, maps, forward, stack):
    _, rows, width = normed.shape
    rows //= 2
    rank = maps.shape[2] // 2
    first = tick == 0
    narrow = jax.ShapeDtypeStruct((rows, rank), BF16)
    incoming_spec = (
        pl.BlockSpec((rows, width), lambda i, levels: (part, 0)) if first else IN_VMEM
    )
    forward_spec = pl.BlockSpec((1, rows, rank), lambda i, levels: (tick - 1, part, 0))
    return pl.pallas_call(
        functools.partial(tick_kernel, tick, part),
        grid_spec=pltpu.PrefetchScalarGridSpec(
            num_scalar_prefetch=1,
            grid=(1,),
            in_specs=[
                incoming_spec,
                pl.BlockSpec((1, rows, width), lambda i, levels: (tick, part, 0)),
                pl.BlockSpec((1, rows, 128), lambda i, levels: (tick, part, 0)),
                pl.BlockSpec((1, width, 2 * rank), lambda i, levels: (levels[tick], 0, 0)),
            ]
            + [forward_spec] * len(forward)
            + [ANYWHERE],
            out_specs=[ANYWHERE, IN_VMEM, IN_VMEM] + [IN_VMEM] * first,
            scratch_shapes=[pltpu.SemaphoreType.DMA],
        ),
        out_shape=[
            jax.ShapeDtypeStruct(stack.shape, stack.dtype),
            jax.ShapeDtypeStruct((rows, width), BF16),
            narrow,
        ]
        + [narrow] * first,
        input_output_aliases={5 + len(forward): 0},
        compiler_params=LIMIT,
        cost_estimate=COST,
        name="tick_layer",
    )(levels, incoming, normed, inverse, maps, *forward, stack)


def products_kernel(normed_ref, grads_ref, lats_ref, acts_ref, out_ref):
    lanes = lats_ref.shape[1]
    contract = (((0,), (0,)), ((), ()))
    for i, (wide_ref, narrow_ref) in enumerate(((normed_ref, lats_ref), (grads_ref, acts_ref))):
        wide = wide_ref[...].reshape(-1, wide_ref.shape[2])
        part = lax.dot_general(wide, narrow_ref[...], contract, preferred_element_type=F32)
        out_ref[:, i * lanes : (i + 1) * lanes] = part.astype(BF16)


def kernel_products(normed, grads, lats, acts):
    ticks, rows, width = normed.shape
    lanes = lats.shape[1]
    run = width // 4
    by_run = pl.BlockSpec((ticks, rows, run), lambda i: (0, 0, i))
    whole = pl.BlockSpec((ticks * rows, lanes), lambda i: (0, 0))
    return pl.pallas_call(
        products_kernel,
        grid=(width // run,),
        out_shape=jax.ShapeDtypeStruct((width, 2 * lanes), BF16),
        in_specs=[by_run, by_run, whole, whole],
        out_specs=pl.BlockSpec((run, 2 * lanes), lambda i: (i, 0)),
        compiler_params=LIMIT,
        cost_estimate=COST,
        name="weight_products",
    )(normed, grads, lats, acts)


def beside_kernel(left_ref, right_ref, out_ref):
    lanes = left_ref.shape[1]
    out_ref[:, :lanes] = left_ref[...]
    out_ref[:, lanes:] = right_ref[...]


def beside(left, right):
    rows, lanes = left.shape
    run = rows // 4
    block = pl.BlockSpec((run, lanes), lambda i: (i, 0))
    return pl.pallas_call(
        beside_kernel,
        grid=(rows // run,),
        out_shape=jax.ShapeDtypeStruct((rows, 2 * lanes), left.dtype),
        in_specs=[block, block],
        out_specs=pl.BlockSpec((run, 2 * lanes), lambda i: (i, 0)),
        compiler_params=LIMIT,
        name="side_by_side",
    )(left, right)


def sum_kernel(moved_ref, out_ref):
    total = jnp.sum(moved_ref[...].astype(F32), axis=0)
    if total.shape == out_ref.shape:
        out_ref[...] = total
    else:
        rank = total.shape[1] // 2
        zeros = jnp.zeros((total.shape[0], rank), F32)
        out_ref[...] = jnp.concatenate([total[:, :rank], zeros, total[:, rank:], zeros], axis=1)


def summed(moved, lanes):
    return pl.pallas_call(
        sum_kernel,
        out_shape=jax.ShapeDtypeStruct((moved.shape[1], lanes), F32),
        in_specs=[IN_VMEM],
        out_specs=IN_VMEM,
        compiler_params=LIMIT,
        name="sum_partials",
    )(moved)


def finish_kernel(total_ref, low_ref, high_ref, grad_ref, down_ref, up_ref):
    rows, rank = low_ref.shape[0], down_ref.shape[3]
    grad_ref[0, :rows] = low_ref[...]
    grad_ref[0, rows:] = high_ref[...]
    for i, out in enumerate((down_ref, up_ref)):
        for j, level in enumerate((1, 0)):
            at = (2 * i + j) * rank
            out[level, 0] = total_ref[:, at : at + rank]


def finish(total, low, high, share, rank):
    rows, width = low.shape
    made = jax.ShapeDtypeStruct((2, 1, share, rank), F32)
    return pl.pallas_call(
        finish_kernel,
        out_shape=[jax.ShapeDtypeStruct((1, 2 * rows, width), low.dtype), made, made],
        in_specs=[IN_VMEM] * 3,
        out_specs=[IN_VMEM] * 3,
        compiler_params=LIMIT,
        name="finish",
    )(total, low, high)


def on_device(saved_inputs, grad_in, adapter_down, adapter_up):
    n_sec = lax.axis_size("section")
    n_dp = lax.axis_size("dp")
    n_z = n_dp // 2
    position = lax.axis_index("section")
    ticks = saved_inputs.shape[0]
    rank, share = adapter_down.shape[2], adapter_down.shape[3]
    width = saved_inputs.shape[3]
    two_layers = position + ticks - 1 >= n_sec
    levels = [1 - (position + tick) // n_sec for tick in range(ticks)]

    def shard_of(down, up, level):
        return jnp.concatenate([down[level].T, up[level].T], axis=1)

    def gather_two(down, up, x):
        shards = jnp.stack([shard_of(down, up, level) for level in range(2)])
        full = ring_gather(shards, n_z)
        return full.reshape(2, width, 2 * rank), *norms(x)

    def gather_one(down, up, x):
        shard = shard_of(down, up, 1)
        copies = jnp.broadcast_to(shard[None], (n_dp,) + shard.shape)
        full = lax.all_to_all(copies, "dp", 0, 0, tiled=True)
        both = unset((2, width, 2 * rank), full.dtype)
        both = lax.dynamic_update_index_in_dim(both, full.reshape(width, 2 * rank), 1, 0)
        return both, *norms(x)

    maps, normed, inverse = lax.cond(
        two_layers, gather_two, gather_one, adapter_down[:, 0], adapter_up[:, 0], saved_inputs
    )

    down_one = [(s, (s - 1) % n_sec) for s in range(n_sec)]
    level_stack = jnp.stack(levels).astype(jnp.int32)
    stack = unset(normed.shape, grad_in.dtype)
    grad_latents, first_actives, moving = [], [], []
    for part in range(2):
        stack, sent, grad_latent, active = tick_layer(
            0, part, level_stack, grad_in[0], normed, inverse, maps, [], stack
        )
        grad_latents.append(grad_latent)
        first_actives.append(active)
        moving.append(lax.ppermute(sent, "section", down_one))
    latents, slopes, actives = forward_rest(level_stack, normed, maps, grad_latent)
    for tick in range(1, ticks):
        arrived, moving = moving, []
        for part in range(2):
            stack, sent, grad_latent = tick_layer(
                tick, part, level_stack, arrived[part], normed, inverse, maps, [latents, slopes], stack
            )
            grad_latents.append(grad_latent)
            moving.append(lax.ppermute(sent, "section", down_one))

    normed_all = normed.reshape(-1, width)
    grads_all = stack.reshape(-1, width)
    actives = jnp.concatenate([jnp.concatenate(first_actives)[None], actives], axis=0)

    def summed_parts(parts):
        moved = lax.all_to_all(parts.reshape(n_dp, share, -1), "dp", 0, 0, tiled=True)
        return summed(moved, 4 * rank)

    def products(lats, acts):
        contract = (((0,), (0,)), ((), ()))
        down = lax.dot_general(normed_all, lats, contract, preferred_element_type=F32)
        up = lax.dot_general(grads_all, acts, contract, preferred_element_type=F32)
        return beside(down.astype(BF16), up.astype(BF16))

    def reduce_one(lats, acts):
        return summed_parts(products(lats.reshape(-1, rank), acts.reshape(-1, rank)))

    def reduce_two(lats, acts):
        level = level_stack[:, None, None]
        zero = jnp.zeros((), BF16)

        def split(value):
            both = [jnp.where(level == 1, value, zero), jnp.where(level == 0, value, zero)]
            return jnp.concatenate(both, axis=2).reshape(-1, 2 * rank)

        return summed_parts(kernel_products(normed, stack, split(lats), split(acts)))

    total = lax.cond(two_layers, reduce_two, reduce_one, jnp.concatenate(grad_latents).reshape(actives.shape), actives)
    grad_out, down_grad, up_grad = finish(total, *moving, share, rank)
    return grad_out, jnp.swapaxes(down_grad, 2, 3), jnp.swapaxes(up_grad, 2, 3)


def solution(mesh):
    in_specs = (
        P(None, "section", "dp", None),
        P("section", "dp", None),
        P(None, "section", None, "dp"),
        P(None, "section", None, "dp"),
    )
    out_specs = (
        P("section", "dp", None),
        P(None, "section", None, "dp"),
        P(None, "section", None, "dp"),
    )
    return jax.shard_map(
        on_device, mesh=mesh, in_specs=in_specs, out_specs=out_specs, check_vma=False
    )
```

```python
import functools

import jax
import jax.numpy as jnp
from jax import lax
from jax.experimental import pallas as pl
from jax.experimental.pallas import tpu as pltpu
from jax.sharding import PartitionSpec as P

EPS = 1e-06
F32 = jnp.float32
BF16 = jnp.bfloat16
LIMIT = pltpu.CompilerParams(vmem_limit_bytes=24 * 1024 * 1024)
IN_VMEM = pl.BlockSpec(memory_space=pltpu.VMEM)
ANYWHERE = pl.BlockSpec(memory_space=pl.ANY)
COST = pl.CostEstimate(flops=2**32, bytes_accessed=2**23, transcendentals=0)
SCALAR = pl.BlockSpec(memory_space=pltpu.SMEM)


def dp_pairs(n_z, step, flip):
    return [
        (2 * z + h, 2 * ((z + step) % n_z) + (h ^ flip)) for z in range(n_z) for h in range(2)
    ]


def shifted(value, n_z, step):
    return lax.ppermute(value, "dp", dp_pairs(n_z, step, 0))


def swapped(value, n_z):
    return lax.ppermute(value, "dp", dp_pairs(n_z, 0, 1))


def ring_gather(shard, n_z, made):
    index = lax.axis_index("dp")
    z, h = index // 2, index % 2
    other, *made = lax.optimization_barrier((swapped(shard, n_z), *made))
    pair = jnp.stack([jnp.where(h == 0, shard, other), jnp.where(h == 0, other, shard)], axis=1)
    half = n_z // 2
    full = unset((2, n_z) + pair.shape[1:], pair.dtype)

    def placed(full, piece, offset):
        return lax.dynamic_update_slice(full, piece[:, None], (0, (z + offset) % n_z, 0, 0, 0))

    full = placed(full, pair, 0)
    right, left = pair, pair
    for step in range(1, half):
        right, left = shifted(right, n_z, 1), shifted(left, n_z, -1)
        full = placed(full, right, -step)
        if step < half - 1:
            full = placed(full, left, step)
    full = placed(full, shifted(right, n_z, 1), -half)
    return placed(full, left, half - 1), made


def empty_kernel(out_ref):
    pass


def unset(shape, dtype):
    return pl.pallas_call(
        empty_kernel,
        out_shape=jax.ShapeDtypeStruct(shape, dtype),
        out_specs=ANYWHERE,
        name="unset",
    )()


def norm_kernel(x_ref, normed_ref, inverse_ref):
    x = x_ref[0, 0].astype(F32)
    inverse = lax.rsqrt(jnp.mean(x * x, axis=-1, keepdims=True) + EPS)
    normed_ref[0] = (x * inverse).astype(BF16)
    inverse_ref[0] = jnp.broadcast_to(inverse, inverse_ref.shape[1:])


def norms(saved_inputs):
    ticks, _, rows, width = saved_inputs.shape
    return pl.pallas_call(
        norm_kernel,
        grid=(ticks,),
        out_shape=[
            jax.ShapeDtypeStruct((ticks, rows, width), BF16),
            jax.ShapeDtypeStruct((ticks, rows, 128), F32),
        ],
        in_specs=[pl.BlockSpec((1, 1, rows, width), lambda i: (i, 0, 0, 0))],
        out_specs=[
            pl.BlockSpec((1, rows, width), lambda i: (i, 0, 0)),
            pl.BlockSpec((1, rows, 128), lambda i: (i, 0, 0)),
        ],
        compiler_params=LIMIT,
        cost_estimate=COST,
        name="norms",
    )(saved_inputs)


def forward_values(normed, down):
    latent = jnp.dot(normed, down, preferred_element_type=F32)
    gate = jax.nn.sigmoid(latent)
    active = (latent * gate).astype(BF16)
    return latent, gate * (1.0 + latent * (1.0 - gate)), active


def forward_kernel(levels_ref, normed_ref, maps_ref, dep_ref, latent_ref, slope_ref, active_ref):
    rank = latent_ref.shape[2]
    latent_ref[0], slope_ref[0], active_ref[0] = forward_values(
        normed_ref[0], maps_ref[0, :, :rank]
    )


def forward_rest(levels, normed, maps, dep):
    ticks, rows, width = normed.shape
    rank = maps.shape[2] // 2
    rest = ticks - 1

    def made(dtype):
        return jax.ShapeDtypeStruct((rest, rows, rank), dtype)

    return pl.pallas_call(
        forward_kernel,
        grid_spec=pltpu.PrefetchScalarGridSpec(
            num_scalar_prefetch=1,
            grid=(rest,),
            in_specs=[
                pl.BlockSpec((1, rows, width), lambda i, levels: (i + 1, 0, 0)),
                pl.BlockSpec((1, width, 2 * rank), lambda i, levels: (levels[i + 1], 0, 0)),
                ANYWHERE,
            ],
            out_specs=[pl.BlockSpec((1, rows, rank), lambda i, levels: (i, 0, 0))] * 3,
        ),
        out_shape=[made(F32), made(F32), made(BF16)],
        compiler_params=LIMIT,
        cost_estimate=COST,
        name="forward_rest",
    )(levels, normed, maps, dep)


def tick_kernel(tick, part, levels_ref, incoming_ref, normed_ref, inverse_ref, maps_ref, *refs):
    _, rows, width = normed_ref.shape
    rank = maps_ref.shape[2] // 2
    if tick == 0:
        stack_ref, sent_ref, grad_latent_ref, active_ref, sem = refs[1:]
    else:
        latent_ref, slope_ref = refs[:2]
        stack_ref, sent_ref, grad_latent_ref, sem = refs[3:]
    keep = pltpu.make_async_copy(
        incoming_ref, stack_ref.at[tick, pl.ds(part * rows, rows)], sem
    )
    keep.start()
    if tick == 0:
        latent, slope, active_ref[...] = forward_values(normed_ref[0], maps_ref[0, :, :rank])
    else:
        latent, slope = latent_ref[0], slope_ref[0]
    grad_act = jnp.dot(incoming_ref[...], maps_ref[0, :, rank:], preferred_element_type=F32)
    grad_latent = (grad_act * slope).astype(BF16)
    grad_latent_ref[...] = grad_latent
    inner = jnp.sum(grad_latent.astype(F32) * latent, axis=-1, keepdims=True) / width
    inverse = inverse_ref[0][:, :1]
    scale = inverse * inner
    run = width // 4
    for start in range(0, width, run):
        at = pl.ds(start, run)
        grad_normed = lax.dot_general(
            grad_latent, maps_ref[0, at, :rank], (((1,), (1,)), ((), ())), preferred_element_type=F32
        )
        sent = incoming_ref[:, at].astype(F32) + (
            inverse * grad_normed - normed_ref[0, :, at].astype(F32) * scale
        )
        sent_ref[:, at] = sent.astype(BF16)
    keep.wait()


def tick_layer(tick, part, levels, incoming, normed, inverse, maps, forward, stack):
    _, rows, width = normed.shape
    rows //= 2
    rank = maps.shape[2] // 2
    first = tick == 0
    narrow = jax.ShapeDtypeStruct((rows, rank), BF16)
    incoming_spec = (
        pl.BlockSpec((rows, width), lambda i, levels: (part, 0)) if first else IN_VMEM
    )
    forward_spec = pl.BlockSpec((1, rows, rank), lambda i, levels: (tick - 1, part, 0))
    return pl.pallas_call(
        functools.partial(tick_kernel, tick, part),
        grid_spec=pltpu.PrefetchScalarGridSpec(
            num_scalar_prefetch=1,
            grid=(1,),
            in_specs=[
                incoming_spec,
                pl.BlockSpec((1, rows, width), lambda i, levels: (tick, part, 0)),
                pl.BlockSpec((1, rows, 128), lambda i, levels: (tick, part, 0)),
                pl.BlockSpec((1, width, 2 * rank), lambda i, levels: (levels[tick], 0, 0)),
            ]
            + [forward_spec] * len(forward)
            + [ANYWHERE],
            out_specs=[ANYWHERE, IN_VMEM, IN_VMEM] + [IN_VMEM] * first,
            scratch_shapes=[pltpu.SemaphoreType.DMA],
        ),
        out_shape=[
            jax.ShapeDtypeStruct(stack.shape, stack.dtype),
            jax.ShapeDtypeStruct((rows, width), BF16),
            narrow,
        ]
        + [narrow] * first,
        input_output_aliases={5 + len(forward): 0},
        compiler_params=LIMIT,
        cost_estimate=COST,
        name="tick_layer",
    )(levels, incoming, normed, inverse, maps, *forward, stack)


def products_kernel(normed_ref, grads_ref, lats_ref, acts_ref, out_ref):
    lanes = lats_ref.shape[1]
    contract = (((0,), (0,)), ((), ()))
    for i, (wide_ref, narrow_ref) in enumerate(((normed_ref, lats_ref), (grads_ref, acts_ref))):
        wide = wide_ref[...].reshape(-1, wide_ref.shape[2])
        part = lax.dot_general(wide, narrow_ref[...], contract, preferred_element_type=F32)
        out_ref[:, i * lanes : (i + 1) * lanes] = part.astype(BF16)


def kernel_products(normed, grads, lats, acts):
    ticks, rows, width = normed.shape
    lanes = lats.shape[1]
    run = width // 4
    by_run = pl.BlockSpec((ticks, rows, run), lambda i: (0, 0, i))
    whole = pl.BlockSpec((ticks * rows, lanes), lambda i: (0, 0))
    return pl.pallas_call(
        products_kernel,
        grid=(width // run,),
        out_shape=jax.ShapeDtypeStruct((width, 2 * lanes), BF16),
        in_specs=[by_run, by_run, whole, whole],
        out_specs=pl.BlockSpec((run, 2 * lanes), lambda i: (i, 0)),
        compiler_params=LIMIT,
        cost_estimate=COST,
        name="weight_products",
    )(normed, grads, lats, acts)


def beside_kernel(left_ref, right_ref, out_ref):
    lanes = left_ref.shape[1]
    out_ref[:, :lanes] = left_ref[...]
    out_ref[:, lanes:] = right_ref[...]


def beside(left, right):
    rows, lanes = left.shape
    run = rows // 4
    block = pl.BlockSpec((run, lanes), lambda i: (i, 0))
    return pl.pallas_call(
        beside_kernel,
        grid=(rows // run,),
        out_shape=jax.ShapeDtypeStruct((rows, 2 * lanes), left.dtype),
        in_specs=[block, block],
        out_specs=pl.BlockSpec((run, 2 * lanes), lambda i: (i, 0)),
        compiler_params=LIMIT,
        name="side_by_side",
    )(left, right)


def sum_kernel(moved_ref, out_ref):
    total = jnp.sum(moved_ref[...].astype(F32), axis=0)
    if total.shape == out_ref.shape:
        out_ref[...] = total
    else:
        rank = total.shape[1] // 2
        zeros = jnp.zeros((total.shape[0], rank), F32)
        out_ref[...] = jnp.concatenate([total[:, :rank], zeros, total[:, rank:], zeros], axis=1)


def summed(moved, lanes):
    return pl.pallas_call(
        sum_kernel,
        out_shape=jax.ShapeDtypeStruct((moved.shape[1], lanes), F32),
        in_specs=[IN_VMEM],
        out_specs=IN_VMEM,
        compiler_params=LIMIT,
        name="sum_partials",
    )(moved)


def finish_kernel(total_ref, low_ref, high_ref, grad_ref, down_ref, up_ref):
    rows, rank = low_ref.shape[0], down_ref.shape[3]
    grad_ref[0, :rows] = low_ref[...]
    grad_ref[0, rows:] = high_ref[...]
    for i, out in enumerate((down_ref, up_ref)):
        for j, level in enumerate((1, 0)):
            at = (2 * i + j) * rank
            out[level, 0] = total_ref[:, at : at + rank]


def finish(total, low, high, share, rank):
    rows, width = low.shape
    made = jax.ShapeDtypeStruct((2, 1, share, rank), F32)
    return pl.pallas_call(
        finish_kernel,
        out_shape=[jax.ShapeDtypeStruct((1, 2 * rows, width), low.dtype), made, made],
        in_specs=[IN_VMEM] * 3,
        out_specs=[IN_VMEM] * 3,
        compiler_params=LIMIT,
        name="finish",
    )(total, low, high)


def on_device(saved_inputs, grad_in, adapter_down, adapter_up):
    n_sec = lax.axis_size("section")
    n_dp = lax.axis_size("dp")
    n_z = n_dp // 2
    position = lax.axis_index("section")
    ticks = saved_inputs.shape[0]
    rank, share = adapter_down.shape[2], adapter_down.shape[3]
    width = saved_inputs.shape[3]
    two_layers = position + ticks - 1 >= n_sec
    levels = [1 - (position + tick) // n_sec for tick in range(ticks)]

    def shard_of(down, up, level):
        return jnp.concatenate([down[level].T, up[level].T], axis=1)

    def gather_two(down, up, x):
        shards = jnp.stack([shard_of(down, up, level) for level in range(2)])
        full, made = ring_gather(shards, n_z, norms(x))
        return full.reshape(2, width, 2 * rank), *made

    def gather_one(down, up, x):
        shard = shard_of(down, up, 1)
        copies = jnp.broadcast_to(shard[None], (n_dp,) + shard.shape)
        full = lax.all_to_all(copies, "dp", 0, 0, tiled=True)
        both = unset((2, width, 2 * rank), full.dtype)
        both = lax.dynamic_update_index_in_dim(both, full.reshape(width, 2 * rank), 1, 0)
        return both, *norms(x)

    maps, normed, inverse = lax.cond(
        two_layers, gather_two, gather_one, adapter_down[:, 0], adapter_up[:, 0], saved_inputs
    )

    down_one = [(s, (s - 1) % n_sec) for s in range(n_sec)]
    level_stack = jnp.stack(levels).astype(jnp.int32)
    stack = unset(normed.shape, grad_in.dtype)
    grad_latents, first_actives, moving = [], [], []
    for part in range(2):
        stack, sent, grad_latent, active = tick_layer(
            0, part, level_stack, grad_in[0], normed, inverse, maps, [], stack
        )
        grad_latents.append(grad_latent)
        first_actives.append(active)
        moving.append(lax.ppermute(sent, "section", down_one))
    latents, slopes, actives = forward_rest(level_stack, normed, maps, grad_latent)
    for tick in range(1, ticks):
        arrived, moving = moving, []
        for part in range(2):
            stack, sent, grad_latent = tick_layer(
                tick, part, level_stack, arrived[part], normed, inverse, maps, [latents, slopes], stack
            )
            grad_latents.append(grad_latent)
            moving.append(lax.ppermute(sent, "section", down_one))

    normed_all = normed.reshape(-1, width)
    grads_all = stack.reshape(-1, width)
    actives = jnp.concatenate([jnp.concatenate(first_actives)[None], actives], axis=0)

    def summed_parts(parts):
        moved = lax.all_to_all(parts.reshape(n_dp, share, -1), "dp", 0, 0, tiled=True)
        return summed(moved, 4 * rank)

    def products(lats, acts):
        contract = (((0,), (0,)), ((), ()))
        down = lax.dot_general(normed_all, lats, contract, preferred_element_type=F32)
        up = lax.dot_general(grads_all, acts, contract, preferred_element_type=F32)
        return beside(down.astype(BF16), up.astype(BF16))

    def reduce_one(lats, acts):
        return summed_parts(products(lats.reshape(-1, rank), acts.reshape(-1, rank)))

    def reduce_two(lats, acts):
        level = level_stack[:, None, None]
        zero = jnp.zeros((), BF16)

        def split(value):
            both = [jnp.where(level == 1, value, zero), jnp.where(level == 0, value, zero)]
            return jnp.concatenate(both, axis=2).reshape(-1, 2 * rank)

        return summed_parts(kernel_products(normed, stack, split(lats), split(acts)))

    total = lax.cond(two_layers, reduce_two, reduce_one, jnp.concatenate(grad_latents).reshape(actives.shape), actives)
    grad_out, down_grad, up_grad = finish(total, *moving, share, rank)
    return grad_out, jnp.swapaxes(down_grad, 2, 3), jnp.swapaxes(up_grad, 2, 3)


def solution(mesh):
    in_specs = (
        P(None, "section", "dp", None),
        P("section", "dp", None),
        P(None, "section", None, "dp"),
        P(None, "section", None, "dp"),
    )
    out_specs = (
        P("section", "dp", None),
        P(None, "section", None, "dp"),
        P(None, "section", None, "dp"),
    )
    return jax.shard_map(
        on_device, mesh=mesh, in_specs=in_specs, out_specs=out_specs, check_vma=False
    )
```

```python
import functools

import jax
import jax.numpy as jnp
from jax import lax
from jax.experimental import pallas as pl
from jax.experimental.pallas import tpu as pltpu
from jax.sharding import PartitionSpec as P

EPS = 1e-06
F32 = jnp.float32
BF16 = jnp.bfloat16
LIMIT = pltpu.CompilerParams(vmem_limit_bytes=24 * 1024 * 1024)
IN_VMEM = pl.BlockSpec(memory_space=pltpu.VMEM)
ANYWHERE = pl.BlockSpec(memory_space=pl.ANY)
COST = pl.CostEstimate(flops=2**32, bytes_accessed=2**23, transcendentals=0)
SCALAR = pl.BlockSpec(memory_space=pltpu.SMEM)


def dp_pairs(n_z, step, flip):
    return [
        (2 * z + h, 2 * ((z + step) % n_z) + (h ^ flip)) for z in range(n_z) for h in range(2)
    ]


def shifted(value, n_z, step):
    return lax.ppermute(value, "dp", dp_pairs(n_z, step, 0))


def swapped(value, n_z):
    return lax.ppermute(value, "dp", dp_pairs(n_z, 0, 1))


def ring_gather(shard, n_z):
    index = lax.axis_index("dp")
    z, h = index // 2, index % 2
    other = swapped(shard, n_z)
    pair = jnp.stack([jnp.where(h == 0, shard, other), jnp.where(h == 0, other, shard)], axis=1)
    half = n_z // 2
    full = unset((2, n_z) + pair.shape[1:], pair.dtype)

    def placed(full, piece, offset):
        return lax.dynamic_update_slice(full, piece[:, None], (0, (z + offset) % n_z, 0, 0, 0))

    full = placed(full, pair, 0)
    right, left = pair, pair
    for step in range(1, half):
        right, left = shifted(right, n_z, 1), shifted(left, n_z, -1)
        full = placed(full, right, -step)
        if step < half - 1:
            full = placed(full, left, step)
    full = placed(full, shifted(right, n_z, 1), -half)
    return placed(full, left, half - 1)


def empty_kernel(out_ref):
    pass


def unset(shape, dtype):
    return pl.pallas_call(
        empty_kernel,
        out_shape=jax.ShapeDtypeStruct(shape, dtype),
        out_specs=ANYWHERE,
        name="unset",
    )()


def norm_kernel(x_ref, normed_ref, inverse_ref):
    x = x_ref[0, 0].astype(F32)
    inverse = lax.rsqrt(jnp.mean(x * x, axis=-1, keepdims=True) + EPS)
    normed_ref[0] = (x * inverse).astype(BF16)
    inverse_ref[0] = jnp.broadcast_to(inverse, inverse_ref.shape[1:])


def norms(saved_inputs):
    ticks, _, rows, width = saved_inputs.shape
    return pl.pallas_call(
        norm_kernel,
        grid=(ticks,),
        out_shape=[
            jax.ShapeDtypeStruct((ticks, rows, width), BF16),
            jax.ShapeDtypeStruct((ticks, rows, 128), F32),
        ],
        in_specs=[pl.BlockSpec((1, 1, rows, width), lambda i: (i, 0, 0, 0))],
        out_specs=[
            pl.BlockSpec((1, rows, width), lambda i: (i, 0, 0)),
            pl.BlockSpec((1, rows, 128), lambda i: (i, 0, 0)),
        ],
        compiler_params=LIMIT,
        cost_estimate=COST,
        name="norms",
    )(saved_inputs)


def forward_values(normed, down):
    latent = jnp.dot(normed, down, preferred_element_type=F32)
    gate = jax.nn.sigmoid(latent)
    active = (latent * gate).astype(BF16)
    return latent, gate * (1.0 + latent * (1.0 - gate)), active


def forward_kernel(levels_ref, normed_ref, maps_ref, dep_ref, latent_ref, slope_ref, active_ref):
    rank = latent_ref.shape[2]
    latent_ref[0], slope_ref[0], active_ref[0] = forward_values(
        normed_ref[0], maps_ref[0, :, :rank]
    )


def forward_rest(levels, normed, maps, dep):
    ticks, rows, width = normed.shape
    rank = maps.shape[2] // 2
    rest = ticks - 1

    def made(dtype):
        return jax.ShapeDtypeStruct((rest, rows, rank), dtype)

    return pl.pallas_call(
        forward_kernel,
        grid_spec=pltpu.PrefetchScalarGridSpec(
            num_scalar_prefetch=1,
            grid=(rest,),
            in_specs=[
                pl.BlockSpec((1, rows, width), lambda i, levels: (i + 1, 0, 0)),
                pl.BlockSpec((1, width, 2 * rank), lambda i, levels: (levels[i + 1], 0, 0)),
                ANYWHERE,
            ],
            out_specs=[pl.BlockSpec((1, rows, rank), lambda i, levels: (i, 0, 0))] * 3,
        ),
        out_shape=[made(F32), made(F32), made(BF16)],
        compiler_params=LIMIT,
        cost_estimate=COST,
        name="forward_rest",
    )(levels, normed, maps, dep)


def tick_kernel(tick, part, levels_ref, incoming_ref, normed_ref, inverse_ref, maps_ref, *refs):
    _, rows, width = normed_ref.shape
    rank = maps_ref.shape[2] // 2
    if tick == 0:
        stack_ref, sent_ref, grad_latent_ref, active_ref, sem, arrived, get_sem = refs[1:]
        get = pltpu.make_async_copy(incoming_ref.at[pl.ds(part * rows, rows)], arrived, get_sem)
        get.start()
        latent, slope, active_ref[...] = forward_values(normed_ref[0], maps_ref[0, :, :rank])
        get.wait()
        incoming_ref = arrived
    else:
        latent_ref, slope_ref = refs[:2]
        stack_ref, sent_ref, grad_latent_ref, sem = refs[3:]
    keep = pltpu.make_async_copy(
        incoming_ref, stack_ref.at[tick, pl.ds(part * rows, rows)], sem
    )
    keep.start()
    if tick:
        latent, slope = latent_ref[0], slope_ref[0]
    grad_act = jnp.dot(incoming_ref[...], maps_ref[0, :, rank:], preferred_element_type=F32)
    grad_latent = (grad_act * slope).astype(BF16)
    grad_latent_ref[...] = grad_latent
    inner = jnp.sum(grad_latent.astype(F32) * latent, axis=-1, keepdims=True) / width
    inverse = inverse_ref[0][:, :1]
    scale = inverse * inner
    run = width // 4
    for start in range(0, width, run):
        at = pl.ds(start, run)
        grad_normed = lax.dot_general(
            grad_latent, maps_ref[0, at, :rank], (((1,), (1,)), ((), ())), preferred_element_type=F32
        )
        sent = incoming_ref[:, at].astype(F32) + (
            inverse * grad_normed - normed_ref[0, :, at].astype(F32) * scale
        )
        sent_ref[:, at] = sent.astype(BF16)
    keep.wait()


def tick_layer(tick, part, levels, incoming, normed, inverse, maps, forward, stack):
    _, rows, width = normed.shape
    rows //= 2
    rank = maps.shape[2] // 2
    first = tick == 0
    narrow = jax.ShapeDtypeStruct((rows, rank), BF16)
    incoming_spec = pl.BlockSpec(memory_space=pltpu.HBM) if first else IN_VMEM
    scratch = [pltpu.VMEM((rows, width), BF16), pltpu.SemaphoreType.DMA] if first else []
    forward_spec = pl.BlockSpec((1, rows, rank), lambda i, levels: (tick - 1, part, 0))
    return pl.pallas_call(
        functools.partial(tick_kernel, tick, part),
        grid_spec=pltpu.PrefetchScalarGridSpec(
            num_scalar_prefetch=1,
            grid=(1,),
            in_specs=[
                incoming_spec,
                pl.BlockSpec((1, rows, width), lambda i, levels: (tick, part, 0)),
                pl.BlockSpec((1, rows, 128), lambda i, levels: (tick, part, 0)),
                pl.BlockSpec((1, width, 2 * rank), lambda i, levels: (levels[tick], 0, 0)),
            ]
            + [forward_spec] * len(forward)
            + [ANYWHERE],
            out_specs=[ANYWHERE, IN_VMEM, IN_VMEM] + [IN_VMEM] * first,
            scratch_shapes=[pltpu.SemaphoreType.DMA] + scratch,
        ),
        out_shape=[
            jax.ShapeDtypeStruct(stack.shape, stack.dtype),
            jax.ShapeDtypeStruct((rows, width), BF16),
            narrow,
        ]
        + [narrow] * first,
        input_output_aliases={5 + len(forward): 0},
        compiler_params=LIMIT,
        cost_estimate=COST,
        name="tick_layer",
    )(levels, incoming, normed, inverse, maps, *forward, stack)


def products_kernel(normed_ref, grads_ref, lats_ref, acts_ref, out_ref):
    lanes = lats_ref.shape[1]
    contract = (((0,), (0,)), ((), ()))
    for i, (wide_ref, narrow_ref) in enumerate(((normed_ref, lats_ref), (grads_ref, acts_ref))):
        wide = wide_ref[...].reshape(-1, wide_ref.shape[2])
        part = lax.dot_general(wide, narrow_ref[...], contract, preferred_element_type=F32)
        out_ref[:, i * lanes : (i + 1) * lanes] = part.astype(BF16)


def kernel_products(normed, grads, lats, acts):
    ticks, rows, width = normed.shape
    lanes = lats.shape[1]
    run = width // 4
    by_run = pl.BlockSpec((ticks, rows, run), lambda i: (0, 0, i))
    whole = pl.BlockSpec((ticks * rows, lanes), lambda i: (0, 0))
    return pl.pallas_call(
        products_kernel,
        grid=(width // run,),
        out_shape=jax.ShapeDtypeStruct((width, 2 * lanes), BF16),
        in_specs=[by_run, by_run, whole, whole],
        out_specs=pl.BlockSpec((run, 2 * lanes), lambda i: (i, 0)),
        compiler_params=LIMIT,
        cost_estimate=COST,
        name="weight_products",
    )(normed, grads, lats, acts)


def beside_kernel(left_ref, right_ref, out_ref):
    lanes = left_ref.shape[1]
    out_ref[:, :lanes] = left_ref[...]
    out_ref[:, lanes:] = right_ref[...]


def beside(left, right):
    rows, lanes = left.shape
    run = rows // 4
    block = pl.BlockSpec((run, lanes), lambda i: (i, 0))
    return pl.pallas_call(
        beside_kernel,
        grid=(rows // run,),
        out_shape=jax.ShapeDtypeStruct((rows, 2 * lanes), left.dtype),
        in_specs=[block, block],
        out_specs=pl.BlockSpec((run, 2 * lanes), lambda i: (i, 0)),
        compiler_params=LIMIT,
        name="side_by_side",
    )(left, right)


def sum_kernel(moved_ref, out_ref):
    total = jnp.sum(moved_ref[...].astype(F32), axis=0)
    if total.shape == out_ref.shape:
        out_ref[...] = total
    else:
        rank = total.shape[1] // 2
        zeros = jnp.zeros((total.shape[0], rank), F32)
        out_ref[...] = jnp.concatenate([total[:, :rank], zeros, total[:, rank:], zeros], axis=1)


def summed(moved, lanes):
    return pl.pallas_call(
        sum_kernel,
        out_shape=jax.ShapeDtypeStruct((moved.shape[1], lanes), F32),
        in_specs=[IN_VMEM],
        out_specs=IN_VMEM,
        compiler_params=LIMIT,
        name="sum_partials",
    )(moved)


def finish_kernel(total_ref, low_ref, high_ref, grad_ref, down_ref, up_ref):
    rows, rank = low_ref.shape[0], down_ref.shape[3]
    grad_ref[0, :rows] = low_ref[...]
    grad_ref[0, rows:] = high_ref[...]
    for i, out in enumerate((down_ref, up_ref)):
        for j, level in enumerate((1, 0)):
            at = (2 * i + j) * rank
            out[level, 0] = total_ref[:, at : at + rank]


def finish(total, low, high, share, rank):
    rows, width = low.shape
    made = jax.ShapeDtypeStruct((2, 1, share, rank), F32)
    return pl.pallas_call(
        finish_kernel,
        out_shape=[jax.ShapeDtypeStruct((1, 2 * rows, width), low.dtype), made, made],
        in_specs=[IN_VMEM] * 3,
        out_specs=[IN_VMEM] * 3,
        compiler_params=LIMIT,
        name="finish",
    )(total, low, high)


def on_device(saved_inputs, grad_in, adapter_down, adapter_up):
    n_sec = lax.axis_size("section")
    n_dp = lax.axis_size("dp")
    n_z = n_dp // 2
    position = lax.axis_index("section")
    ticks = saved_inputs.shape[0]
    rank, share = adapter_down.shape[2], adapter_down.shape[3]
    width = saved_inputs.shape[3]
    two_layers = position + ticks - 1 >= n_sec
    levels = [1 - (position + tick) // n_sec for tick in range(ticks)]

    def shard_of(down, up, level):
        return jnp.concatenate([down[level].T, up[level].T], axis=1)

    def gather_two(down, up, x):
        shards = jnp.stack([shard_of(down, up, level) for level in range(2)])
        full = ring_gather(shards, n_z)
        return full.reshape(2, width, 2 * rank), *norms(x)

    def gather_one(down, up, x):
        shard = shard_of(down, up, 1)
        copies = jnp.broadcast_to(shard[None], (n_dp,) + shard.shape)
        full = lax.all_to_all(copies, "dp", 0, 0, tiled=True)
        both = unset((2, width, 2 * rank), full.dtype)
        both = lax.dynamic_update_index_in_dim(both, full.reshape(width, 2 * rank), 1, 0)
        return both, *norms(x)

    maps, normed, inverse = lax.cond(
        two_layers, gather_two, gather_one, adapter_down[:, 0], adapter_up[:, 0], saved_inputs
    )

    down_one = [(s, (s - 1) % n_sec) for s in range(n_sec)]
    level_stack = jnp.stack(levels).astype(jnp.int32)
    stack = unset(normed.shape, grad_in.dtype)
    grad_latents, first_actives, moving = [], [], []
    for part in range(2):
        stack, sent, grad_latent, active = tick_layer(
            0, part, level_stack, grad_in[0], normed, inverse, maps, [], stack
        )
        grad_latents.append(grad_latent)
        first_actives.append(active)
        moving.append(lax.ppermute(sent, "section", down_one))
    latents, slopes, actives = forward_rest(level_stack, normed, maps, grad_latent)
    for tick in range(1, ticks):
        arrived, moving = moving, []
        for part in range(2):
            stack, sent, grad_latent = tick_layer(
                tick, part, level_stack, arrived[part], normed, inverse, maps, [latents, slopes], stack
            )
            grad_latents.append(grad_latent)
            moving.append(lax.ppermute(sent, "section", down_one))

    normed_all = normed.reshape(-1, width)
    grads_all = stack.reshape(-1, width)
    actives = jnp.concatenate([jnp.concatenate(first_actives)[None], actives], axis=0)

    def summed_parts(parts):
        moved = lax.all_to_all(parts.reshape(n_dp, share, -1), "dp", 0, 0, tiled=True)
        return summed(moved, 4 * rank)

    def products(lats, acts):
        contract = (((0,), (0,)), ((), ()))
        down = lax.dot_general(normed_all, lats, contract, preferred_element_type=F32)
        up = lax.dot_general(grads_all, acts, contract, preferred_element_type=F32)
        return beside(down.astype(BF16), up.astype(BF16))

    def reduce_one(lats, acts):
        return summed_parts(products(lats.reshape(-1, rank), acts.reshape(-1, rank)))

    def reduce_two(lats, acts):
        level = level_stack[:, None, None]
        zero = jnp.zeros((), BF16)

        def split(value):
            both = [jnp.where(level == 1, value, zero), jnp.where(level == 0, value, zero)]
            return jnp.concatenate(both, axis=2).reshape(-1, 2 * rank)

        return summed_parts(kernel_products(normed, stack, split(lats), split(acts)))

    total = lax.cond(two_layers, reduce_two, reduce_one, jnp.concatenate(grad_latents).reshape(actives.shape), actives)
    grad_out, down_grad, up_grad = finish(total, *moving, share, rank)
    return grad_out, jnp.swapaxes(down_grad, 2, 3), jnp.swapaxes(up_grad, 2, 3)


def solution(mesh):
    in_specs = (
        P(None, "section", "dp", None),
        P("section", "dp", None),
        P(None, "section", None, "dp"),
        P(None, "section", None, "dp"),
    )
    out_specs = (
        P("section", "dp", None),
        P(None, "section", None, "dp"),
        P(None, "section", None, "dp"),
    )
    return jax.shard_map(
        on_device, mesh=mesh, in_specs=in_specs, out_specs=out_specs, check_vma=False
    )
```

```python
import functools

import jax
import jax.numpy as jnp
from jax import lax
from jax.experimental import pallas as pl
from jax.experimental.pallas import tpu as pltpu
from jax.sharding import PartitionSpec as P

EPS = 1e-06
F32 = jnp.float32
BF16 = jnp.bfloat16
LIMIT = pltpu.CompilerParams(vmem_limit_bytes=24 * 1024 * 1024)
IN_VMEM = pl.BlockSpec(memory_space=pltpu.VMEM)
ANYWHERE = pl.BlockSpec(memory_space=pl.ANY)
COST = pl.CostEstimate(flops=2**32, bytes_accessed=2**23, transcendentals=0)
SCALAR = pl.BlockSpec(memory_space=pltpu.SMEM)


def dp_pairs(n_z, step, flip):
    return [
        (2 * z + h, 2 * ((z + step) % n_z) + (h ^ flip)) for z in range(n_z) for h in range(2)
    ]


def shifted(value, n_z, step):
    return lax.ppermute(value, "dp", dp_pairs(n_z, step, 0))


def swapped(value, n_z):
    return lax.ppermute(value, "dp", dp_pairs(n_z, 0, 1))


def ring_gather(shard, n_z):
    index = lax.axis_index("dp")
    z, h = index // 2, index % 2
    other = swapped(shard, n_z)
    pair = jnp.stack([jnp.where(h == 0, shard, other), jnp.where(h == 0, other, shard)], axis=1)
    half = n_z // 2
    full = unset((2, n_z) + pair.shape[1:], pair.dtype)

    def placed(full, piece, offset):
        return lax.dynamic_update_slice(full, piece[:, None], (0, (z + offset) % n_z, 0, 0, 0))

    full = placed(full, pair, 0)
    right, left = pair, pair
    for step in range(1, half):
        right, left = shifted(right, n_z, 1), shifted(left, n_z, -1)
        full = placed(full, right, -step)
        if step < half - 1:
            full = placed(full, left, step)
    full = placed(full, shifted(right, n_z, 1), -half)
    return placed(full, left, half - 1)


def empty_kernel(out_ref):
    pass


def unset(shape, dtype):
    return pl.pallas_call(
        empty_kernel,
        out_shape=jax.ShapeDtypeStruct(shape, dtype),
        out_specs=ANYWHERE,
        name="unset",
    )()


def norm_kernel(x_ref, normed_ref, inverse_ref):
    x = x_ref[0, 0].astype(F32)
    inverse = lax.rsqrt(jnp.mean(x * x, axis=-1, keepdims=True) + EPS)
    normed_ref[0] = (x * inverse).astype(BF16)
    inverse_ref[0] = jnp.broadcast_to(inverse, inverse_ref.shape[1:])


def norms(saved_inputs):
    ticks, _, rows, width = saved_inputs.shape
    return pl.pallas_call(
        norm_kernel,
        grid=(ticks,),
        out_shape=[
            jax.ShapeDtypeStruct((ticks, rows, width), BF16),
            jax.ShapeDtypeStruct((ticks, rows, 128), F32),
        ],
        in_specs=[pl.BlockSpec((1, 1, rows, width), lambda i: (i, 0, 0, 0))],
        out_specs=[
            pl.BlockSpec((1, rows, width), lambda i: (i, 0, 0)),
            pl.BlockSpec((1, rows, 128), lambda i: (i, 0, 0)),
        ],
        compiler_params=LIMIT,
        cost_estimate=COST,
        name="norms",
    )(saved_inputs)


def forward_values(normed, down):
    latent = jnp.dot(normed, down, preferred_element_type=F32)
    gate = jax.nn.sigmoid(latent)
    active = (latent * gate).astype(BF16)
    return latent, gate * (1.0 + latent * (1.0 - gate)), active


def forward_kernel(levels_ref, normed_ref, maps_ref, dep_ref, latent_ref, slope_ref, active_ref):
    rank = latent_ref.shape[2]
    latent_ref[0], slope_ref[0], active_ref[0] = forward_values(
        normed_ref[0], maps_ref[0, :, :rank]
    )


def forward_rest(levels, normed, maps, dep):
    ticks, rows, width = normed.shape
    rank = maps.shape[2] // 2
    rest = ticks - 1

    def made(dtype):
        return jax.ShapeDtypeStruct((rest, rows, rank), dtype)

    return pl.pallas_call(
        forward_kernel,
        grid_spec=pltpu.PrefetchScalarGridSpec(
            num_scalar_prefetch=1,
            grid=(rest,),
            in_specs=[
                pl.BlockSpec((1, rows, width), lambda i, levels: (i + 1, 0, 0)),
                pl.BlockSpec((1, width, 2 * rank), lambda i, levels: (levels[i + 1], 0, 0)),
                ANYWHERE,
            ],
            out_specs=[pl.BlockSpec((1, rows, rank), lambda i, levels: (i, 0, 0))] * 3,
        ),
        out_shape=[made(F32), made(F32), made(BF16)],
        compiler_params=LIMIT,
        cost_estimate=COST,
        name="forward_rest",
    )(levels, normed, maps, dep)


def tick_kernel(tick, part, levels_ref, incoming_ref, normed_ref, inverse_ref, maps_ref, *refs):
    _, rows, _ = inverse_ref.shape
    width = maps_ref.shape[1]
    rank = maps_ref.shape[2] // 2
    if tick == 0:
        stack_ref, sent_ref, grad_latent_ref, active_ref, sem, arrived, own, get_sems = refs[1:]
        at = pl.ds(part * rows, rows)
        get_own = pltpu.make_async_copy(normed_ref.at[pl.ds(0, 1), at], own, get_sems.at[0])
        get_arrived = pltpu.make_async_copy(incoming_ref.at[at], arrived, get_sems.at[1])
        get_own.start()
        get_arrived.start()
        get_own.wait()
        latent, slope, active_ref[...] = forward_values(own[0], maps_ref[0, :, :rank])
        get_arrived.wait()
        incoming_ref, normed_ref = arrived, own
    else:
        latent_ref, slope_ref = refs[:2]
        stack_ref, sent_ref, grad_latent_ref, sem = refs[3:]
    keep = pltpu.make_async_copy(
        incoming_ref, stack_ref.at[tick, pl.ds(part * rows, rows)], sem
    )
    keep.start()
    if tick:
        latent, slope = latent_ref[0], slope_ref[0]
    grad_act = jnp.dot(incoming_ref[...], maps_ref[0, :, rank:], preferred_element_type=F32)
    grad_latent = (grad_act * slope).astype(BF16)
    grad_latent_ref[...] = grad_latent
    inner = jnp.sum(grad_latent.astype(F32) * latent, axis=-1, keepdims=True) / width
    inverse = inverse_ref[0][:, :1]
    scale = inverse * inner
    run = width // 4
    for start in range(0, width, run):
        at = pl.ds(start, run)
        grad_normed = lax.dot_general(
            grad_latent, maps_ref[0, at, :rank], (((1,), (1,)), ((), ())), preferred_element_type=F32
        )
        sent = incoming_ref[:, at].astype(F32) + (
            inverse * grad_normed - normed_ref[0, :, at].astype(F32) * scale
        )
        sent_ref[:, at] = sent.astype(BF16)
    keep.wait()


def tick_layer(tick, part, levels, incoming, normed, inverse, maps, forward, stack):
    _, rows, width = normed.shape
    rows //= 2
    rank = maps.shape[2] // 2
    first = tick == 0
    narrow = jax.ShapeDtypeStruct((rows, rank), BF16)
    incoming_spec = pl.BlockSpec(memory_space=pltpu.HBM) if first else IN_VMEM
    normed_spec = pl.BlockSpec((1, rows, width), lambda i, levels: (tick, part, 0))
    scratch = []
    if first:
        normed_spec = pl.BlockSpec(memory_space=pltpu.HBM)
        scratch = [
            pltpu.VMEM((rows, width), BF16),
            pltpu.VMEM((1, rows, width), BF16),
            pltpu.SemaphoreType.DMA((2,)),
        ]
    forward_spec = pl.BlockSpec((1, rows, rank), lambda i, levels: (tick - 1, part, 0))
    return pl.pallas_call(
        functools.partial(tick_kernel, tick, part),
        grid_spec=pltpu.PrefetchScalarGridSpec(
            num_scalar_prefetch=1,
            grid=(1,),
            in_specs=[
                incoming_spec,
                normed_spec,
                pl.BlockSpec((1, rows, 128), lambda i, levels: (tick, part, 0)),
                pl.BlockSpec((1, width, 2 * rank), lambda i, levels: (levels[tick], 0, 0)),
            ]
            + [forward_spec] * len(forward)
            + [ANYWHERE],
            out_specs=[ANYWHERE, IN_VMEM, IN_VMEM] + [IN_VMEM] * first,
            scratch_shapes=[pltpu.SemaphoreType.DMA] + scratch,
        ),
        out_shape=[
            jax.ShapeDtypeStruct(stack.shape, stack.dtype),
            jax.ShapeDtypeStruct((rows, width), BF16),
            narrow,
        ]
        + [narrow] * first,
        input_output_aliases={5 + len(forward): 0},
        compiler_params=LIMIT,
        cost_estimate=COST,
        name="tick_layer",
    )(levels, incoming, normed, inverse, maps, *forward, stack)


def products_kernel(normed_ref, grads_ref, lats_ref, acts_ref, out_ref):
    lanes = lats_ref.shape[1]
    contract = (((0,), (0,)), ((), ()))
    for i, (wide_ref, narrow_ref) in enumerate(((normed_ref, lats_ref), (grads_ref, acts_ref))):
        wide = wide_ref[...].reshape(-1, wide_ref.shape[2])
        part = lax.dot_general(wide, narrow_ref[...], contract, preferred_element_type=F32)
        out_ref[:, i * lanes : (i + 1) * lanes] = part.astype(BF16)


def kernel_products(normed, grads, lats, acts):
    ticks, rows, width = normed.shape
    lanes = lats.shape[1]
    run = width // 4
    by_run = pl.BlockSpec((ticks, rows, run), lambda i: (0, 0, i))
    whole = pl.BlockSpec((ticks * rows, lanes), lambda i: (0, 0))
    return pl.pallas_call(
        products_kernel,
        grid=(width // run,),
        out_shape=jax.ShapeDtypeStruct((width, 2 * lanes), BF16),
        in_specs=[by_run, by_run, whole, whole],
        out_specs=pl.BlockSpec((run, 2 * lanes), lambda i: (i, 0)),
        compiler_params=LIMIT,
        cost_estimate=COST,
        name="weight_products",
    )(normed, grads, lats, acts)


def beside_kernel(left_ref, right_ref, out_ref):
    lanes = left_ref.shape[1]
    out_ref[:, :lanes] = left_ref[...]
    out_ref[:, lanes:] = right_ref[...]


def beside(left, right):
    rows, lanes = left.shape
    run = rows // 4
    block = pl.BlockSpec((run, lanes), lambda i: (i, 0))
    return pl.pallas_call(
        beside_kernel,
        grid=(rows // run,),
        out_shape=jax.ShapeDtypeStruct((rows, 2 * lanes), left.dtype),
        in_specs=[block, block],
        out_specs=pl.BlockSpec((run, 2 * lanes), lambda i: (i, 0)),
        compiler_params=LIMIT,
        name="side_by_side",
    )(left, right)


def sum_kernel(moved_ref, out_ref):
    total = jnp.sum(moved_ref[...].astype(F32), axis=0)
    if total.shape == out_ref.shape:
        out_ref[...] = total
    else:
        rank = total.shape[1] // 2
        zeros = jnp.zeros((total.shape[0], rank), F32)
        out_ref[...] = jnp.concatenate([total[:, :rank], zeros, total[:, rank:], zeros], axis=1)


def summed(moved, lanes):
    return pl.pallas_call(
        sum_kernel,
        out_shape=jax.ShapeDtypeStruct((moved.shape[1], lanes), F32),
        in_specs=[IN_VMEM],
        out_specs=IN_VMEM,
        compiler_params=LIMIT,
        name="sum_partials",
    )(moved)


def finish_kernel(total_ref, low_ref, high_ref, grad_ref, down_ref, up_ref):
    rows, rank = low_ref.shape[0], down_ref.shape[3]
    grad_ref[0, :rows] = low_ref[...]
    grad_ref[0, rows:] = high_ref[...]
    for i, out in enumerate((down_ref, up_ref)):
        for j, level in enumerate((1, 0)):
            at = (2 * i + j) * rank
            out[level, 0] = total_ref[:, at : at + rank]


def finish(total, low, high, share, rank):
    rows, width = low.shape
    made = jax.ShapeDtypeStruct((2, 1, share, rank), F32)
    return pl.pallas_call(
        finish_kernel,
        out_shape=[jax.ShapeDtypeStruct((1, 2 * rows, width), low.dtype), made, made],
        in_specs=[IN_VMEM] * 3,
        out_specs=[IN_VMEM] * 3,
        compiler_params=LIMIT,
        name="finish",
    )(total, low, high)


def on_device(saved_inputs, grad_in, adapter_down, adapter_up):
    n_sec = lax.axis_size("section")
    n_dp = lax.axis_size("dp")
    n_z = n_dp // 2
    position = lax.axis_index("section")
    ticks = saved_inputs.shape[0]
    rank, share = adapter_down.shape[2], adapter_down.shape[3]
    width = saved_inputs.shape[3]
    two_layers = position + ticks - 1 >= n_sec
    levels = [1 - (position + tick) // n_sec for tick in range(ticks)]

    def shard_of(down, up, level):
        return jnp.concatenate([down[level].T, up[level].T], axis=1)

    def gather_two(down, up, x):
        shards = jnp.stack([shard_of(down, up, level) for level in range(2)])
        full = ring_gather(shards, n_z)
        return full.reshape(2, width, 2 * rank), *norms(x)

    def gather_one(down, up, x):
        shard = shard_of(down, up, 1)
        copies = jnp.broadcast_to(shard[None], (n_dp,) + shard.shape)
        full = lax.all_to_all(copies, "dp", 0, 0, tiled=True)
        both = unset((2, width, 2 * rank), full.dtype)
        both = lax.dynamic_update_index_in_dim(both, full.reshape(width, 2 * rank), 1, 0)
        return both, *norms(x)

    maps, normed, inverse = lax.cond(
        two_layers, gather_two, gather_one, adapter_down[:, 0], adapter_up[:, 0], saved_inputs
    )

    down_one = [(s, (s - 1) % n_sec) for s in range(n_sec)]
    level_stack = jnp.stack(levels).astype(jnp.int32)
    stack = unset(normed.shape, grad_in.dtype)
    grad_latents, first_actives, moving = [], [], []
    for part in range(2):
        stack, sent, grad_latent, active = tick_layer(
            0, part, level_stack, grad_in[0], normed, inverse, maps, [], stack
        )
        grad_latents.append(grad_latent)
        first_actives.append(active)
        moving.append(lax.ppermute(sent, "section", down_one))
    latents, slopes, actives = forward_rest(level_stack, normed, maps, grad_latent)
    for tick in range(1, ticks):
        arrived, moving = moving, []
        for part in range(2):
            stack, sent, grad_latent = tick_layer(
                tick, part, level_stack, arrived[part], normed, inverse, maps, [latents, slopes], stack
            )
            grad_latents.append(grad_latent)
            moving.append(lax.ppermute(sent, "section", down_one))

    normed_all = normed.reshape(-1, width)
    grads_all = stack.reshape(-1, width)
    actives = jnp.concatenate([jnp.concatenate(first_actives)[None], actives], axis=0)

    def summed_parts(parts):
        moved = lax.all_to_all(parts.reshape(n_dp, share, -1), "dp", 0, 0, tiled=True)
        return summed(moved, 4 * rank)

    def products(lats, acts):
        contract = (((0,), (0,)), ((), ()))
        down = lax.dot_general(normed_all, lats, contract, preferred_element_type=F32)
        up = lax.dot_general(grads_all, acts, contract, preferred_element_type=F32)
        return beside(down.astype(BF16), up.astype(BF16))

    def reduce_one(lats, acts):
        return summed_parts(products(lats.reshape(-1, rank), acts.reshape(-1, rank)))

    def reduce_two(lats, acts):
        level = level_stack[:, None, None]
        zero = jnp.zeros((), BF16)

        def split(value):
            both = [jnp.where(level == 1, value, zero), jnp.where(level == 0, value, zero)]
            return jnp.concatenate(both, axis=2).reshape(-1, 2 * rank)

        return summed_parts(kernel_products(normed, stack, split(lats), split(acts)))

    total = lax.cond(two_layers, reduce_two, reduce_one, jnp.concatenate(grad_latents).reshape(actives.shape), actives)
    grad_out, down_grad, up_grad = finish(total, *moving, share, rank)
    return grad_out, jnp.swapaxes(down_grad, 2, 3), jnp.swapaxes(up_grad, 2, 3)


def solution(mesh):
    in_specs = (
        P(None, "section", "dp", None),
        P("section", "dp", None),
        P(None, "section", None, "dp"),
        P(None, "section", None, "dp"),
    )
    out_specs = (
        P("section", "dp", None),
        P(None, "section", None, "dp"),
        P(None, "section", None, "dp"),
    )
    return jax.shard_map(
        on_device, mesh=mesh, in_specs=in_specs, out_specs=out_specs, check_vma=False
    )
```

```python
import functools

import jax
import jax.numpy as jnp
from jax import lax
from jax.experimental import pallas as pl
from jax.experimental.pallas import tpu as pltpu
from jax.sharding import PartitionSpec as P

EPS = 1e-06
F32 = jnp.float32
BF16 = jnp.bfloat16
LIMIT = pltpu.CompilerParams(vmem_limit_bytes=24 * 1024 * 1024)
IN_VMEM = pl.BlockSpec(memory_space=pltpu.VMEM)
ANYWHERE = pl.BlockSpec(memory_space=pl.ANY)
COST = pl.CostEstimate(flops=2**32, bytes_accessed=2**23, transcendentals=0)
SCALAR = pl.BlockSpec(memory_space=pltpu.SMEM)


def dp_pairs(n_z, step, flip):
    return [
        (2 * z + h, 2 * ((z + step) % n_z) + (h ^ flip)) for z in range(n_z) for h in range(2)
    ]


def shifted(value, n_z, step):
    return lax.ppermute(value, "dp", dp_pairs(n_z, step, 0))


def swapped(value, n_z):
    return lax.ppermute(value, "dp", dp_pairs(n_z, 0, 1))


def ring_gather(shard, n_z):
    index = lax.axis_index("dp")
    z, h = index // 2, index % 2
    other = swapped(shard, n_z)
    pair = jnp.stack([jnp.where(h == 0, shard, other), jnp.where(h == 0, other, shard)], axis=1)
    half = n_z // 2
    full = unset((2, n_z) + pair.shape[1:], pair.dtype)

    def placed(full, piece, offset):
        return lax.dynamic_update_slice(full, piece[:, None], (0, (z + offset) % n_z, 0, 0, 0))

    full = placed(full, pair, 0)
    right, left = pair, pair
    for step in range(1, half):
        right, left = shifted(right, n_z, 1), shifted(left, n_z, -1)
        full = placed(full, right, -step)
        if step < half - 1:
            full = placed(full, left, step)
    full = placed(full, shifted(right, n_z, 1), -half)
    return placed(full, left, half - 1)


def empty_kernel(out_ref):
    pass


def unset(shape, dtype):
    return pl.pallas_call(
        empty_kernel,
        out_shape=jax.ShapeDtypeStruct(shape, dtype),
        out_specs=ANYWHERE,
        name="unset",
    )()


def norm_kernel(x_ref, normed_ref, inverse_ref):
    x = x_ref[0, 0].astype(F32)
    inverse = lax.rsqrt(jnp.mean(x * x, axis=-1, keepdims=True) + EPS)
    normed_ref[0] = (x * inverse).astype(BF16)
    inverse_ref[0] = jnp.broadcast_to(inverse, inverse_ref.shape[1:])


def norms(saved_inputs):
    ticks, _, rows, width = saved_inputs.shape
    return pl.pallas_call(
        norm_kernel,
        grid=(ticks,),
        out_shape=[
            jax.ShapeDtypeStruct((ticks, rows, width), BF16),
            jax.ShapeDtypeStruct((ticks, rows, 128), F32),
        ],
        in_specs=[pl.BlockSpec((1, 1, rows, width), lambda i: (i, 0, 0, 0))],
        out_specs=[
            pl.BlockSpec((1, rows, width), lambda i: (i, 0, 0)),
            pl.BlockSpec((1, rows, 128), lambda i: (i, 0, 0)),
        ],
        compiler_params=LIMIT,
        cost_estimate=COST,
        name="norms",
    )(saved_inputs)


def forward_values(normed, down):
    latent = jnp.dot(normed, down, preferred_element_type=F32)
    gate = jax.nn.sigmoid(latent)
    active = (latent * gate).astype(BF16)
    return latent, gate * (1.0 + latent * (1.0 - gate)), active


def forward_kernel(levels_ref, normed_ref, maps_ref, dep_ref, latent_ref, slope_ref, active_ref):
    rank = latent_ref.shape[2]
    latent_ref[0], slope_ref[0], active_ref[0] = forward_values(
        normed_ref[0], maps_ref[0, :, :rank]
    )


def forward_rest(levels, normed, maps, dep):
    ticks, rows, width = normed.shape
    rank = maps.shape[2] // 2
    rest = ticks - 1

    def made(dtype):
        return jax.ShapeDtypeStruct((rest, rows, rank), dtype)

    return pl.pallas_call(
        forward_kernel,
        grid_spec=pltpu.PrefetchScalarGridSpec(
            num_scalar_prefetch=1,
            grid=(rest,),
            in_specs=[
                pl.BlockSpec((1, rows, width), lambda i, levels: (i + 1, 0, 0)),
                pl.BlockSpec((1, width, 2 * rank), lambda i, levels: (levels[i + 1], 0, 0)),
                ANYWHERE,
            ],
            out_specs=[pl.BlockSpec((1, rows, rank), lambda i, levels: (i, 0, 0))] * 3,
        ),
        out_shape=[made(F32), made(F32), made(BF16)],
        compiler_params=LIMIT,
        cost_estimate=COST,
        name="forward_rest",
    )(levels, normed, maps, dep)


def tick_kernel(tick, part, levels_ref, incoming_ref, normed_ref, inverse_ref, maps_ref, *refs):
    _, rows, width = normed_ref.shape
    rank = maps_ref.shape[2] // 2
    if tick == 0:
        stack_ref, sent_ref, grad_latent_ref, active_ref, sem = refs[1:]
    else:
        latent_ref, slope_ref = refs[:2]
        stack_ref, sent_ref, grad_latent_ref, sem = refs[3:]
    keep = pltpu.make_async_copy(
        incoming_ref, stack_ref.at[tick, pl.ds(part * rows, rows)], sem
    )
    keep.start()
    if tick == 0:
        latent, slope, active_ref[...] = forward_values(normed_ref[0], maps_ref[0, :, :rank])
    else:
        latent, slope = latent_ref[0], slope_ref[0]
    grad_act = jnp.dot(incoming_ref[...], maps_ref[0, :, rank:], preferred_element_type=F32)
    grad_latent = (grad_act * slope).astype(BF16)
    grad_latent_ref[...] = grad_latent
    inner = jnp.sum(grad_latent.astype(F32) * latent, axis=-1, keepdims=True) / width
    inverse = inverse_ref[0][:, :1]
    scale = inverse * inner
    run = width // 4
    for start in range(0, width, run):
        at = pl.ds(start, run)
        grad_normed = lax.dot_general(
            grad_latent, maps_ref[0, at, :rank], (((1,), (1,)), ((), ())), preferred_element_type=F32
        )
        sent = incoming_ref[:, at].astype(F32) + (
            inverse * grad_normed - normed_ref[0, :, at].astype(F32) * scale
        )
        sent_ref[:, at] = sent.astype(BF16)
    keep.wait()


def tick_layer(tick, part, levels, incoming, normed, inverse, maps, forward, stack):
    _, rows, width = normed.shape
    rows //= 2
    rank = maps.shape[2] // 2
    first = tick == 0
    narrow = jax.ShapeDtypeStruct((rows, rank), BF16)
    incoming_spec = (
        pl.BlockSpec((rows, width), lambda i, levels: (part, 0)) if first else IN_VMEM
    )
    forward_spec = pl.BlockSpec((1, rows, rank), lambda i, levels: (tick - 1, part, 0))
    return pl.pallas_call(
        functools.partial(tick_kernel, tick, part),
        grid_spec=pltpu.PrefetchScalarGridSpec(
            num_scalar_prefetch=1,
            grid=(1,),
            in_specs=[
                incoming_spec,
                pl.BlockSpec((1, rows, width), lambda i, levels: (tick, part, 0)),
                pl.BlockSpec((1, rows, 128), lambda i, levels: (tick, part, 0)),
                pl.BlockSpec((1, width, 2 * rank), lambda i, levels: (levels[tick], 0, 0)),
            ]
            + [forward_spec] * len(forward)
            + [ANYWHERE],
            out_specs=[ANYWHERE, IN_VMEM, IN_VMEM] + [IN_VMEM] * first,
            scratch_shapes=[pltpu.SemaphoreType.DMA],
        ),
        out_shape=[
            jax.ShapeDtypeStruct(stack.shape, stack.dtype),
            jax.ShapeDtypeStruct((rows, width), BF16),
            narrow,
        ]
        + [narrow] * first,
        input_output_aliases={5 + len(forward): 0},
        compiler_params=LIMIT,
        cost_estimate=COST,
        name="tick_layer",
    )(levels, incoming, normed, inverse, maps, *forward, stack)


def products_kernel(normed_ref, grads_ref, lats_ref, acts_ref, out_ref):
    lanes = lats_ref.shape[1]
    contract = (((0,), (0,)), ((), ()))
    for i, (wide_ref, narrow_ref) in enumerate(((normed_ref, lats_ref), (grads_ref, acts_ref))):
        wide = wide_ref[...].reshape(-1, wide_ref.shape[2])
        part = lax.dot_general(wide, narrow_ref[...], contract, preferred_element_type=F32)
        out_ref[:, i * lanes : (i + 1) * lanes] = part.astype(BF16)


def kernel_products(normed, grads, lats, acts):
    ticks, rows, width = normed.shape
    lanes = lats.shape[1]
    run = width // 4
    by_run = pl.BlockSpec((ticks, rows, run), lambda i: (0, 0, i))
    whole = pl.BlockSpec((ticks * rows, lanes), lambda i: (0, 0))
    return pl.pallas_call(
        products_kernel,
        grid=(width // run,),
        out_shape=jax.ShapeDtypeStruct((width, 2 * lanes), BF16),
        in_specs=[by_run, by_run, whole, whole],
        out_specs=pl.BlockSpec((run, 2 * lanes), lambda i: (i, 0)),
        compiler_params=LIMIT,
        cost_estimate=COST,
        name="weight_products",
    )(normed, grads, lats, acts)


def beside_kernel(left_ref, right_ref, out_ref):
    lanes = left_ref.shape[1]
    out_ref[:, :lanes] = left_ref[...]
    out_ref[:, lanes:] = right_ref[...]


def beside(left, right):
    rows, lanes = left.shape
    run = rows // 4
    block = pl.BlockSpec((run, lanes), lambda i: (i, 0))
    return pl.pallas_call(
        beside_kernel,
        grid=(rows // run,),
        out_shape=jax.ShapeDtypeStruct((rows, 2 * lanes), left.dtype),
        in_specs=[block, block],
        out_specs=pl.BlockSpec((run, 2 * lanes), lambda i: (i, 0)),
        compiler_params=LIMIT,
        name="side_by_side",
    )(left, right)


def sum_kernel(moved_ref, out_ref):
    total = jnp.sum(moved_ref[...].astype(F32), axis=0)
    if total.shape == out_ref.shape:
        out_ref[...] = total
    else:
        rank = total.shape[1] // 2
        zeros = jnp.zeros((total.shape[0], rank), F32)
        out_ref[...] = jnp.concatenate([total[:, :rank], zeros, total[:, rank:], zeros], axis=1)


def summed(moved, lanes):
    return pl.pallas_call(
        sum_kernel,
        out_shape=jax.ShapeDtypeStruct((moved.shape[1], lanes), F32),
        in_specs=[IN_VMEM],
        out_specs=IN_VMEM,
        compiler_params=LIMIT,
        name="sum_partials",
    )(moved)


def finish_kernel(total_ref, relayed_ref, grad_ref, down_ref, up_ref):
    rank = down_ref.shape[3]
    grad_ref[0] = relayed_ref[...]
    for i, out in enumerate((down_ref, up_ref)):
        for j, level in enumerate((1, 0)):
            at = (2 * i + j) * rank
            out[level, 0] = total_ref[:, at : at + rank]


def finish(total, relayed, share, rank):
    made = jax.ShapeDtypeStruct((2, 1, share, rank), F32)
    return pl.pallas_call(
        finish_kernel,
        out_shape=[jax.ShapeDtypeStruct((1,) + relayed.shape, relayed.dtype), made, made],
        in_specs=[IN_VMEM] * 2,
        out_specs=[IN_VMEM] * 3,
        compiler_params=LIMIT,
        name="finish",
    )(total, relayed)


def on_device(saved_inputs, grad_in, adapter_down, adapter_up):
    n_sec = lax.axis_size("section")
    n_dp = lax.axis_size("dp")
    n_z = n_dp // 2
    position = lax.axis_index("section")
    ticks = saved_inputs.shape[0]
    rank, share = adapter_down.shape[2], adapter_down.shape[3]
    width = saved_inputs.shape[3]
    two_layers = position + ticks - 1 >= n_sec
    levels = [1 - (position + tick) // n_sec for tick in range(ticks)]

    def shard_of(down, up, level):
        return jnp.concatenate([down[level].T, up[level].T], axis=1)

    def gather_two(down, up, x):
        shards = jnp.stack([shard_of(down, up, level) for level in range(2)])
        full = ring_gather(shards, n_z)
        return full.reshape(2, width, 2 * rank), *norms(x)

    def gather_one(down, up, x):
        shard = shard_of(down, up, 1)
        copies = jnp.broadcast_to(shard[None], (n_dp,) + shard.shape)
        full = lax.all_to_all(copies, "dp", 0, 0, tiled=True)
        both = unset((2, width, 2 * rank), full.dtype)
        both = lax.dynamic_update_index_in_dim(both, full.reshape(width, 2 * rank), 1, 0)
        return both, *norms(x)

    maps, normed, inverse = lax.cond(
        two_layers, gather_two, gather_one, adapter_down[:, 0], adapter_up[:, 0], saved_inputs
    )

    down_one = [(s, (s - 1) % n_sec) for s in range(n_sec)]
    level_stack = jnp.stack(levels).astype(jnp.int32)
    stack = unset(normed.shape, grad_in.dtype)
    grad_latents, first_actives, moving = [], [], []
    for part in range(2):
        stack, sent, grad_latent, active = tick_layer(
            0, part, level_stack, grad_in[0], normed, inverse, maps, [], stack
        )
        grad_latents.append(grad_latent)
        first_actives.append(active)
        moving.append(lax.ppermute(sent, "section", down_one))
    latents, slopes, actives = forward_rest(level_stack, normed, maps, grad_latent)
    for tick in range(1, ticks):
        arrived, moving = moving, []
        for part in range(2):
            stack, sent, grad_latent = tick_layer(
                tick, part, level_stack, arrived[part], normed, inverse, maps, [latents, slopes], stack
            )
            grad_latents.append(grad_latent)
            moving.append(sent if tick == ticks - 1 else lax.ppermute(sent, "section", down_one))
    relayed = lax.ppermute(jnp.concatenate(moving), "section", down_one)

    normed_all = normed.reshape(-1, width)
    grads_all = stack.reshape(-1, width)
    actives = jnp.concatenate([jnp.concatenate(first_actives)[None], actives], axis=0)

    def summed_parts(parts):
        moved = lax.all_to_all(parts.reshape(n_dp, share, -1), "dp", 0, 0, tiled=True)
        return summed(moved, 4 * rank)

    def products(lats, acts):
        contract = (((0,), (0,)), ((), ()))
        down = lax.dot_general(normed_all, lats, contract, preferred_element_type=F32)
        up = lax.dot_general(grads_all, acts, contract, preferred_element_type=F32)
        return beside(down.astype(BF16), up.astype(BF16))

    def reduce_one(lats, acts):
        return summed_parts(products(lats.reshape(-1, rank), acts.reshape(-1, rank)))

    def reduce_two(lats, acts):
        level = level_stack[:, None, None]
        zero = jnp.zeros((), BF16)

        def split(value):
            both = [jnp.where(level == 1, value, zero), jnp.where(level == 0, value, zero)]
            return jnp.concatenate(both, axis=2).reshape(-1, 2 * rank)

        return summed_parts(kernel_products(normed, stack, split(lats), split(acts)))

    total = lax.cond(two_layers, reduce_two, reduce_one, jnp.concatenate(grad_latents).reshape(actives.shape), actives)
    grad_out, down_grad, up_grad = finish(total, relayed, share, rank)
    return grad_out, jnp.swapaxes(down_grad, 2, 3), jnp.swapaxes(up_grad, 2, 3)


def solution(mesh):
    in_specs = (
        P(None, "section", "dp", None),
        P("section", "dp", None),
        P(None, "section", None, "dp"),
        P(None, "section", None, "dp"),
    )
    out_specs = (
        P("section", "dp", None),
        P(None, "section", None, "dp"),
        P(None, "section", None, "dp"),
    )
    return jax.shard_map(
        on_device, mesh=mesh, in_specs=in_specs, out_specs=out_specs, check_vma=False
    )
```
